32 devices in a mesh: ens: 2 (over x), gx: 16 (over z, y, core).
Axes of the slice: x: 2, y: 2, z: 4, core: 2. Of those that a mesh axis runs over, the one named last changes fastest.
Arguments:
- fraction: float32 [128, 128, 256], P(('ens', 'gx')), parts along dimension 0, may hold values from 0 to 1
- first_velocity: float32 [128, 128, 256], P(('ens', 'gx')), parts along dimension 0, may hold values from -12 to 12
- second_velocity: float32 [128, 128, 256], P(('ens', 'gx')), parts along dimension 0, may hold values from -12 to 12
- third_velocity: float32 [128, 128, 256], P(('ens', 'gx')), parts along dimension 0, may hold values from -12 to 12
- wall_class: int32 [64, 128], replicated, may hold values from 0 to 3
- seed_mask: int32 [128, 128, 256], P(('ens', 'gx')), parts along dimension 0, may hold values 0 or 1
Outputs:
- liquid: float32 [128, 128, 256], P(('ens', 'gx')), parts along dimension 0
The draws below stay inside these ranges and needn't reach their ends.
There are 2 independent parts, one for each index of `ens`. The reference program is written for one: setup_inputs(seed, part) draws one part's arguments, and reference() takes and returns one part's arrays. A program takes and returns all parts, laid end to end along the dimension named above; an argument that names none is the same for every part. Nothing has to cross between parts.
All inputs are finite; a program needn't handle non-finite values. Where the reference program divides by a largest or mean magnitude, that divisor is 1e-20 or more. No bound on the sum of `seed_mask` on one device may be relied on, other than what follows from the above.
Results may differ from the reference program's by a relative error of at most 0.0003.
Values sent between devices are 32-bit elements; how exact they have to be, the bound alone decides.
No kernel may reach another device: no remote copies, remote signals or barrier semaphores. Data moves between devices by JAX's collectives and lax.ppermute only.
A program may use at most 64 MiB of HBM per device.

```python
import jax
import jax.numpy as jnp

NY = 128
NZ = 256
STEPS = 2
NEWTON = 4
WALL_CLASSES = 4
NX = 64


def rough_scale(key):
    return jnp.exp(jnp.log(0.3) + jnp.log(10.0) * jax.random.uniform(key, (NX, NY, NZ), jnp.float32))


def draw_first_velocity(key, part):
    key = jax.random.fold_in(key, 11)
    key_values, key_scale = jax.random.split(key, 2)
    values = jnp.clip(jax.random.normal(key_values, (NX, NY, NZ), jnp.float32), -4.0, 4.0)
    return values * rough_scale(key_scale)


def draw_second_velocity(key, part):
    key = jax.random.fold_in(key, 12)
    key_values, key_scale = jax.random.split(key, 2)
    values = jnp.clip(jax.random.normal(key_values, (NX, NY, NZ), jnp.float32), -4.0, 4.0)
    return values * rough_scale(key_scale)


def draw_third_velocity(key, part):
    key = jax.random.fold_in(key, 13)
    key_values, key_scale = jax.random.split(key, 2)
    values = jnp.clip(jax.random.normal(key_values, (NX, NY, NZ), jnp.float32), -4.0, 4.0)
    return values * rough_scale(key_scale)


def place_ends(values, rng, least, top_value):
    place = [jax.random.randint(jax.random.fold_in(rng, axis), (), 0, length) for axis, length in enumerate(values.shape)]
    longest = values.shape.index(max(values.shape))
    neighbour = place[:longest] + [(place[longest] + 1) % values.shape[longest]] + place[longest + 1:]
    return values.at[tuple(place)].set(least).at[tuple(neighbour)].set(top_value)


def block_levels(own_key, shape, cuts, least, largest):
    def one(dim, shards_of):
        draws = jax.random.uniform(jax.random.fold_in(jax.random.fold_in(own_key, 6), dim), (shards_of,), jnp.float32, least / len(cuts), largest / len(cuts))
        return jnp.repeat(jnp.exp(draws), shape[dim] // shards_of).reshape((-1,) + (1,) * (len(shape) - dim - 1))

    gain = one(*cuts[0])
    for cut in cuts[1:]:
        gain = gain * one(*cut)
    return gain


def setup_inputs(seed: int = 0, part: int = 0) -> dict:
    key_list = jax.random.split(jax.random.key(seed), 7)
    own_keys = jax.random.split(jax.random.fold_in(key_list[6], part), 7)
    return {
        "fraction": jnp.clip(1.0 * jax.random.uniform(own_keys[0], (NX, NY, NZ), jnp.float32) ** block_levels(own_keys[0], (NX, NY, NZ), ((0, 16),), -0.2, 0.2), 0.0, 1.0),
        "first_velocity": draw_first_velocity(jax.random.fold_in(jax.random.fold_in(key_list[6], part), 71), part),
        "second_velocity": draw_second_velocity(jax.random.fold_in(jax.random.fold_in(key_list[6], part), 71), part),
        "third_velocity": draw_third_velocity(jax.random.fold_in(jax.random.fold_in(key_list[6], part), 71), part),
        "wall_class": place_ends(jax.random.randint(key_list[4], (NX, NY), 0, WALL_CLASSES), jax.random.fold_in(key_list[4], 1), 0, WALL_CLASSES - 1).astype(jnp.int32),
        "seed_mask": place_ends((jax.random.randint(own_keys[5], (NX, NY, NZ), 0, 16) < 1).astype(jnp.int32), jax.random.fold_in(own_keys[5], 1), 0, 1),
    }


CFL_NUMBER = 0.45
NEWTON_DAMPING = 0.5


def cube_part(values):
    positive = jnp.maximum(values, 0.0)
    return positive * positive * positive


def square_part(values):
    positive = jnp.maximum(values, 0.0)
    return positive * positive


def corner_terms(plane_at, slope_a, slope_b, slope_c, power_map):
    paired = slope_b + slope_c
    summed = power_map(plane_at) - power_map(plane_at - slope_b) - power_map(plane_at - slope_c) + power_map(plane_at - paired)
    shifted = plane_at - slope_a
    summed = summed - power_map(shifted) + power_map(shifted - slope_b) + power_map(shifted - slope_c) - power_map(shifted - paired)
    return summed


def plane_level(target, slope_a, slope_b, slope_c, inverse):
    plane_at = jnp.full_like(target, 0.5)
    for newton_turn in range(NEWTON):
        volume = corner_terms(plane_at, slope_a, slope_b, slope_c, cube_part) * inverse
        growth = corner_terms(plane_at, slope_a, slope_b, slope_c, square_part) * (3.0 * inverse)
        plane_at = plane_at - NEWTON_DAMPING * (volume - target) / growth
    return plane_at


def flux_volume(donor, normal_along, normal_other, normal_third, velocity, step_size):
    courant = jnp.abs(velocity) * step_size
    heading = jnp.where(velocity > 0.0, 1.0, -1.0)
    weight_sum = jnp.abs(normal_along) + jnp.abs(normal_other) + jnp.abs(normal_third) + 0.3
    slope_along = (jnp.abs(normal_along) + 0.1) / weight_sum
    slope_other = (jnp.abs(normal_other) + 0.1) / weight_sum
    slope_third = (jnp.abs(normal_third) + 0.1) / weight_sum
    inverse = 1.0 / (6.0 * slope_along * slope_other * slope_third)
    lighter = donor <= 0.5
    target = jnp.clip(jnp.minimum(donor, 1.0 - donor), 0.0, 0.5)
    plane_at = plane_level(target, slope_along, slope_other, slope_third, inverse)

    def box_volume(slab_span):
        return corner_terms(plane_at, slab_span * slope_along, slope_other, slope_third, cube_part) * inverse

    high_side = box_volume(1.0) - box_volume(1.0 - courant)
    low_side = box_volume(courant)
    facing = jnp.where(lighter, normal_along, -normal_along)
    weight = jnp.clip(0.5 + 2.0 * facing * heading / weight_sum, 0.0, 1.0)
    phase_part = weight * high_side + (1.0 - weight) * low_side
    phase_moved = jnp.where(lighter, phase_part, courant - phase_part)
    return heading * phase_moved


def normal_field(padded, wall_cosine):
    centre_cells = padded[1:-1]
    normal_x = 0.5 * (padded[:-2] - padded[2:])
    normal_y = 0.5 * (jnp.roll(centre_cells, 1, 1) - jnp.roll(centre_cells, -1, 1))
    from_below = jnp.concatenate([centre_cells[:, :, :1], centre_cells[:, :, :-1]], 2)
    from_above = jnp.concatenate([centre_cells[:, :, 1:], centre_cells[:, :, -1:]], 2)
    normal_z = 0.5 * (from_below - from_above)
    bottom_layer = jnp.arange(centre_cells.shape[2]) == 0
    contact = wall_cosine[:, :, None] * (jnp.abs(normal_x) + jnp.abs(normal_y))
    normal_z = jnp.where(bottom_layer[None, None, :], contact, normal_z)
    return centre_cells, normal_x, normal_y, normal_z


def advect_first_axis(padded, face_speed, wall_cosine, step_size):
    centre_cells, normal_x, normal_y, normal_z = normal_field(padded, wall_cosine)
    forward = face_speed > 0.0

    def choose_donor(values):
        return jnp.where(forward, values[:-1], values[1:])

    moved_volume = flux_volume(choose_donor(centre_cells), choose_donor(normal_x), choose_donor(normal_y), choose_donor(normal_z), face_speed, step_size)
    return jnp.clip(centre_cells[1:-1] - moved_volume[1:] + moved_volume[:-1], 0.0, 1.0)


def advect_second_axis(padded, face_speed, wall_cosine, step_size):
    centre_cells, normal_x, normal_y, normal_z = normal_field(padded, wall_cosine)
    forward = face_speed > 0.0

    def choose_donor(values):
        return jnp.where(forward, values, jnp.roll(values, -1, 1))

    moved_volume = flux_volume(choose_donor(centre_cells), choose_donor(normal_y), choose_donor(normal_x), choose_donor(normal_z), face_speed, step_size)
    return jnp.clip(centre_cells - moved_volume + jnp.roll(moved_volume, 1, 1), 0.0, 1.0)


def advect_third_axis(padded, face_speed, wall_cosine, step_size):
    centre_cells, normal_x, normal_y, normal_z = normal_field(padded, wall_cosine)
    top_face = jnp.arange(centre_cells.shape[2]) == centre_cells.shape[2] - 1
    face_speed = jnp.where(top_face[None, None, :], 0.0, face_speed)
    forward = face_speed > 0.0

    def choose_donor(values):
        return jnp.where(forward, values, jnp.concatenate([values[:, :, 1:], values[:, :, -1:]], 2))

    moved_volume = flux_volume(choose_donor(centre_cells), choose_donor(normal_z), choose_donor(normal_x), choose_donor(normal_y), face_speed, step_size)
    inflow = jnp.concatenate([jnp.zeros_like(moved_volume[:, :, :1]), moved_volume[:, :, :-1]], 2)
    return jnp.clip(centre_cells - moved_volume + inflow, 0.0, 1.0)


def wrap_margin(values, margin):
    return jnp.concatenate([values[-margin:], values, values[:margin]], 0)


def reference(fraction, first_velocity, second_velocity, third_velocity, wall_class, seed_mask):
    wall_cosine = jnp.cos(jnp.pi * (wall_class.astype(jnp.float32) + 1.0) / (WALL_CLASSES + 1))
    liquid = jnp.where(seed_mask == 1, jnp.ones_like(fraction), fraction)
    speed_peak = jnp.maximum(jnp.maximum(jnp.max(jnp.abs(first_velocity)), jnp.max(jnp.abs(second_velocity))), jnp.max(jnp.abs(third_velocity)))
    step_size = CFL_NUMBER / (speed_peak + 1e-6)
    first_faces = jnp.concatenate([first_velocity[-1:], first_velocity], 0)
    first_cosine = jnp.concatenate([wall_cosine[-1:], wall_cosine, wall_cosine[:1]], 0)
    for step_turn in range(STEPS):
        liquid = advect_first_axis(wrap_margin(liquid, 2), first_faces, first_cosine, step_size)
        liquid = advect_second_axis(wrap_margin(liquid, 1), second_velocity, wall_cosine, step_size)
        liquid = advect_third_axis(wrap_margin(liquid, 1), third_velocity, wall_cosine, step_size)
    return liquid
```

```python
import functools

import jax
import jax.numpy as jnp
from jax import lax
from jax.experimental import pallas as pl
from jax.experimental.pallas import tpu as pltpu
from jax.sharding import PartitionSpec as P

STEPS = 2
NEWTON = 4
WALL_CLASSES = 4
CFL_NUMBER = 0.45

LANES = 128
PAD = 8
ROWS = 32
HALVES = (0, 1)
OUTER = 3
INNER = 2
VMEM_LIMIT = 24 * 1024 * 1024


def cube(t):
    t = jnp.maximum(t, 0.0)
    return t * t * t


def square(t):
    t = jnp.maximum(t, 0.0)
    return t * t


def rcp(x):
    return pl.reciprocal(x, approx=True)


def plane(donor, span, soft_a, soft_b):
    low = jnp.minimum(soft_a, soft_b)
    high = jnp.maximum(soft_a, soft_b)
    pair = soft_a + soft_b
    half = 0.5 * (span + pair)
    top = jnp.maximum(span, high)
    mid = jnp.minimum(span, high)
    over = half - top
    last = half - jnp.abs(over)
    sign = jnp.where(over > 0.0, -1.0, 1.0)
    flat = low * mid
    bulk = flat * top
    share = jnp.clip(jnp.minimum(donor, 1.0 - donor), 0.0, 0.5)
    goal = bulk * share
    at = half - (0.25 * bulk - 0.5 * goal) * rcp(flat - square(over))
    low_6 = low * (1.0 / 6.0)
    mid_6 = mid * (1.0 / 6.0)
    last_6 = last * (1.0 / 6.0)
    for _ in range(NEWTON - 1):
        by_low = square(at - low)
        by_mid = square(at - mid)
        by_last = sign * square(at - last)
        growth = at * at - by_low - by_mid + by_last
        shift = goal - low_6 * by_low - mid_6 * by_mid + last_6 * by_last
        at = (5.0 / 6.0) * at + shift * rcp(growth)
    return at, low, high, pair, half, bulk


def face_flux(donor, along, soft_a, soft_b, moved):
    forward = moved > 0.0
    span = jnp.abs(along) + 0.2
    at, low, high, pair, half, bulk = plane(donor, span, soft_a, soft_b)
    light = donor <= 0.5
    slab = jnp.abs(moved) * span
    far = at - span
    near = far + slab
    rest = at - slab
    upper = cube(near) - cube(near - low) - cube(far) + cube(far - low)
    lower = (
        at * at * at
        - cube(at - low)
        - cube(at - high)
        + cube(at - pair)
        - cube(rest)
        + cube(rest - low)
        + cube(rest - high)
        - cube(rest - pair)
    )
    sense = jnp.where(jnp.logical_xor(light, forward), -1.0, 1.0)
    weight = jnp.clip(0.5 + (along * sense) * rcp(half), 0.0, 1.0)
    part = (lower + weight * (upper - lower)) * (sense * rcp(6.0 * bulk))
    return part + jnp.where(light, 0.0, moved)


def lane_of(value):
    return lax.broadcasted_iota(jnp.int32, value.shape, 1)


def from_above(pair):
    turned = [pltpu.roll(v, LANES - 1, 1) for v in pair]
    last = lane_of(pair[0]) == LANES - 1
    return [jnp.where(last, turned[1], turned[0]), jnp.where(last, turned[0], turned[1])]


def from_below(pair):
    turned = [pltpu.roll(v, 1, 1) for v in pair]
    first = lane_of(pair[0]) == 0
    return [jnp.where(first, turned[1], turned[0]), jnp.where(first, turned[0], turned[1])]


class Layer:
    def __init__(self, ref, index, padded=True):
        self.ref, self.index, self.pad = ref, index, PAD if padded else 0

    def read(self, half, row):
        return self.ref[self.index, half, pl.ds(self.pad + row, ROWS), :]

    def write(self, half, row, value):
        self.ref[self.index, half, pl.ds(self.pad + row, ROWS), :] = value

    def wrap(self):
        rows = self.ref.shape[2] - 2 * PAD
        for h in HALVES:
            self.ref[self.index, h, pl.ds(0, PAD), :] = self.ref[self.index, h, pl.ds(rows, PAD), :]
            self.ref[self.index, h, pl.ds(PAD + rows, PAD), :] = self.ref[self.index, h, pl.ds(PAD, PAD), :]


def copy_layer(source, target, rows):
    for r in range(0, rows, ROWS):
        for h in HALVES:
            target.write(h, r, source.read(h, r))


def fill(source, field, start, way, count, padded):
    rows = field.shape[2] - 2 * PAD

    @pl.loop(0, count)
    def _(k):
        target = Layer(field, start + way * k)
        copy_layer(Layer(source, k, padded), target, rows)
        target.wrap()


def normals(before, here, after, wall, row):
    centre = [here.read(h, row) for h in HALVES]
    n_x = [before.read(h, row) - after.read(h, row) for h in HALVES]
    n_y = [here.read(h, row - 1) - here.read(h, row + 1) for h in HALVES]
    above = from_above(centre)
    below = from_below(centre)
    lane = lane_of(centre[0])
    above[1] = jnp.where(lane == LANES - 1, centre[1], above[1])
    n_z = [below[h] - above[h] for h in HALVES]
    contact = wall[pl.ds(row, ROWS), :] * (jnp.abs(n_x[0]) + jnp.abs(n_y[0]))
    n_z[0] = jnp.where(lane == 0, contact, n_z[0])
    return centre, n_x, n_y, n_z


def soft(normal):
    return jnp.abs(normal) + 0.2


def own_index(odd, layer, count):
    return jnp.where(odd, OUTER + count - 1 - layer, layer - OUTER)


def natural(ref, index, half, row):
    return ref[index, pl.ds(row, ROWS), half * LANES : (half + 1) * LANES]


def peak_kernel(a_ref, b_ref, c_ref, out_ref):
    count, rows, width = a_ref.shape
    best = jnp.zeros((8, width), jnp.float32)
    for i in range(count):
        for ref in (a_ref, b_ref, c_ref):
            best = jnp.maximum(best, jnp.max(jnp.abs(ref[i]).reshape(rows // 8, 8, width), axis=0))
    out_ref[...] = jnp.maximum(best[:, :LANES], best[:, LANES:])


def begin_kernel(odd_ref, fraction, mask, first, state, send_outer, send_inner):
    odd = odd_ref[0] == 1
    count, rows, _ = fraction.shape
    for p in range(OUTER, OUTER + count):
        index = own_index(odd, p, count)
        to = [Layer(state, p - OUTER)]
        if p - OUTER < OUTER:
            to.append(Layer(send_outer, p - OUTER, False))
        if OUTER + count - 1 - p < INNER:
            to.append(Layer(send_inner, OUTER + count - 1 - p, False))
        for r in range(0, rows, ROWS):
            for h in HALVES:
                value = jnp.where(natural(mask, index, h, r) == 1, 1.0, natural(fraction, index, h, r))
                for target in to:
                    target.write(h, r, value)
        Layer(state, p - OUTER).wrap()
    near = jnp.where(odd, count - 2, 0)
    for r in range(0, rows, ROWS):
        for h in HALVES:
            Layer(send_outer, OUTER, False).write(h, r, natural(first, near, h, r))
            Layer(send_outer, OUTER + 1, False).write(h, r, natural(first, count - 1, h, r))
            Layer(send_inner, INNER, False).write(h, r, natural(first, count - 1, h, r))


def wall_kernel(where_ref, cosine, out):
    odd = where_ref[0] == 1
    total = cosine.shape[0]
    layers = out.shape[0]
    count = layers - OUTER - INNER
    for p in range(1, layers - 1):
        row = lax.rem(where_ref[1] + own_index(odd, p, count) + total, total)
        out[p] = jnp.transpose(jnp.broadcast_to(cosine[pl.ds(row, 1), :], (LANES, cosine.shape[1])))


def moved_kernel(odd_ref, peak, first, outer, inner, out, step_out):
    odd = odd_ref[0] == 1
    count, rows, _ = first.shape
    largest = jnp.max(peak[...])
    step = CFL_NUMBER / (jnp.full((8, LANES), largest, jnp.float32) + 1e-6)
    step_out[...] = step
    signed = jnp.where(odd, -step, step)[:1, :]
    for face in range(1, OUTER + count):
        for r in range(0, rows, ROWS):
            for h in HALVES:
                if face == 1:
                    value = Layer(outer, OUTER, False).read(h, r)
                elif face == OUTER - 1:
                    value = jnp.where(odd, natural(first, count - 1, h, r), Layer(outer, OUTER + 1, False).read(h, r))
                elif face == OUTER + count - 1:
                    value = jnp.where(odd, Layer(inner, INNER, False).read(h, r), natural(first, count - 1, h, r))
                else:
                    value = natural(first, jnp.where(odd, OUTER + count - 2 - face, face - OUTER), h, r)
                Layer(out, face - 1, False).write(h, r, value * signed)


def first_kernel(*refs, own_parts, layers):
    own, (outer, inner, moved, wall, out, send, field, n_s, n_a, n_b, flux) = refs[:own_parts], refs[own_parts:]
    rows = moved.shape[2]
    start = OUTER
    for ref in own:
        fill(ref, field, start, 1, ref.shape[0], True)
        start += ref.shape[0]
    fill(outer, field, OUTER - 1, -1, OUTER, False)
    fill(inner, field, start, 1, INNER, False)

    def slopes(i, r):
        _, n_x, n_y, n_z = normals(Layer(field, i - 1), Layer(field, i), Layer(field, i + 1), wall.at[i], r)
        for h in HALVES:
            Layer(n_s, i).write(h, r, n_x[h])
            Layer(n_a, i).write(h, r, soft(n_y[h]))
            Layer(n_b, i).write(h, r, soft(n_z[h]))

    @pl.loop(1, layers - 1)
    def _(i):
        for r in range(0, rows, ROWS):
            slopes(i, r)

    @pl.loop(1, layers - INNER)
    def _(i):
        for r in range(0, rows, ROWS):
            for h in HALVES:
                speed = Layer(moved, i - 1, False).read(h, r)
                ahead = speed > 0.0

                def donor(ref):
                    return jnp.where(ahead, Layer(ref, i).read(h, r), Layer(ref, i + 1).read(h, r))

                through = face_flux(donor(field), donor(n_s), donor(n_a), donor(n_b), speed)
                Layer(flux, i).write(h, r, through)

    @pl.loop(2, layers - INNER)
    def _(i):
        for r in range(0, rows, ROWS):
            for h in HALVES:
                through = Layer(flux, i).read(h, r)
                value = jnp.clip(Layer(field, i).read(h, r) - through + Layer(flux, i - 1).read(h, r), 0.0, 1.0)
                Layer(out, i - 1).write(h, r, value)
        Layer(out, i - 1).wrap()

    copy_layer(Layer(out, layers - INNER - 2), Layer(send, 0, False), rows)


def second_sweep(before, here, after, wall, speed, out, scratch):
    n_s, n_a, n_b, flux = scratch
    rows = out.ref.shape[2] - 2 * PAD
    for r in range(0, rows, ROWS):
        _, n_x, n_y, n_z = normals(before, here, after, wall, r)
        for h in HALVES:
            n_s.write(h, r, n_y[h])
            n_a.write(h, r, soft(n_x[h]))
            n_b.write(h, r, soft(n_z[h]))
    for s in (n_s, n_a, n_b):
        s.wrap()
    for r in range(0, rows, ROWS):
        for h in HALVES:
            moved = speed(h, r)
            ahead = moved > 0.0
            donor = [jnp.where(ahead, s.read(h, r), s.read(h, r + 1)) for s in (here, n_s, n_a, n_b)]
            flux.write(h, r, face_flux(*donor, moved))
    flux.wrap()
    for r in range(0, rows, ROWS):
        for h in HALVES:
            out.write(h, r, jnp.clip(here.read(h, r) - flux.read(h, r) + flux.read(h, r - 1), 0.0, 1.0))
    out.wrap()


def third_sweep(before, here, after, wall, speed, outs, rows):
    for r in range(0, rows, ROWS):
        centre, n_x, n_y, n_z = normals(before, here, after, wall, r)
        fields = [centre, n_z, [soft(v) for v in n_x], [soft(v) for v in n_y]]
        above = [from_above(f) for f in fields]
        lane = lane_of(centre[0])
        through = []
        for h in HALVES:
            moved = speed(h, r)
            if h == 1:
                moved = jnp.where(lane == LANES - 1, 0.0, moved)
            ahead = moved > 0.0
            through.append(face_flux(*[jnp.where(ahead, f[h], a[h]) for f, a in zip(fields, above)], moved))
        below = from_below(through)
        for h in HALVES:
            value = jnp.clip(centre[h] - through[h] + below[h], 0.0, 1.0)
            for write in outs:
                write(h, r, value)


def gather_layers(refs, places):
    found = {}
    for ref, (start, padded) in zip(refs, places):
        for k in range(ref.shape[0]):
            found[start + k] = Layer(ref, k, padded)
    return found


def second_kernel(odd_ref, step, speed_ref, wall, *refs, places, work, send_last):
    fields, rest = refs[: len(places)], refs[len(places) :]
    out, rest = rest[0], rest[1:]
    send, rest = (rest[0], rest[1:]) if send_last is not None else (None, rest)
    scratch = [Layer(ref, 0) for ref in rest]
    layers = gather_layers(fields, places)
    odd = odd_ref[0] == 1
    count, rows, _ = speed_ref.shape
    for k, p in enumerate(work):
        index = own_index(odd, p, count)
        second_sweep(
            layers[p - 1],
            layers[p],
            layers[p + 1],
            wall.at[p],
            lambda h, r: natural(speed_ref, index, h, r) * step[:1, :],
            Layer(out, k),
            scratch,
        )
    if send is not None:
        copy_layer(Layer(out, work.index(send_last)), Layer(send, 0, False), rows)


def third_kernel(odd_ref, step, speed_ref, wall, *refs, places, work, final):
    fields, outs = refs[: len(places)], refs[len(places) :]
    layers = gather_layers(fields, places)
    odd = odd_ref[0] == 1
    count, rows, _ = speed_ref.shape
    out = outs[0]
    for k, p in enumerate(work):
        index = own_index(odd, p, count)
        if final:
            def write(h, r, value, index=index):
                out[index, pl.ds(r, ROWS), h * LANES : (h + 1) * LANES] = value
        else:
            write = Layer(out, k).write
        third_sweep(
            layers[p - 1],
            layers[p],
            layers[p + 1],
            wall.at[p],
            lambda h, r: natural(speed_ref, index, h, r) * step[:1, :],
            [write],
            rows,
        )
        if not final:
            Layer(out, k).wrap()


IN_VMEM = pl.BlockSpec(memory_space=pltpu.VMEM)
IN_SMEM = pl.BlockSpec(memory_space=pltpu.SMEM)


def held(shape):
    return pltpu.VMEM(shape, jnp.float32)


def call(kernel, name, outs, scalars, arrays, scratch=(), faces=0.0, in_hbm=()):
    arrays = [pltpu.with_memory_space_constraint(a, pltpu.VMEM) for a in arrays]
    work = int(faces * 32 * 1024 * 220) + 1024
    return pl.pallas_call(
        kernel,
        out_shape=outs,
        in_specs=[IN_SMEM] * len(scalars) + [IN_VMEM] * len(arrays),
        out_specs=[IN_VMEM] * len(outs),
        scratch_shapes=list(scratch),
        compiler_params=pltpu.CompilerParams(vmem_limit_bytes=VMEM_LIMIT),
        cost_estimate=pl.CostEstimate(flops=work, bytes_accessed=1024, transcendentals=0),
        name=name,
    )(*scalars, *arrays)


def swap(array, outer):
    count = lax.axis_size("gx")
    if outer:
        pairs = [(i, (i + 1) % count if i % 2 else (i - 1) % count) for i in range(count)]
    else:
        pairs = [(i, i ^ 1) for i in range(count)]
    return lax.ppermute(array, "gx", pairs)


def largest_over(array):
    count = lax.axis_size("gx")
    reach = 1
    while reach < count:
        if count & (count - 1) == 0:
            pairs = [(i, i ^ reach) for i in range(count)]
        else:
            pairs = [(i, (i + reach) % count) for i in range(count)]
        array = jnp.maximum(array, lax.ppermute(array, "gx", pairs))
        reach *= 2
    return array


def shards(fraction, first, second, third, wall_class, seed_mask):
    count, rows, width = fraction.shape
    layers = OUTER + count + INNER
    own_end = OUTER + count
    device = lax.axis_index("gx")
    odd = (device % 2).astype(jnp.int32).reshape(1)
    place = jnp.stack([device % 2, device * count]).astype(jnp.int32)

    def padded(n):
        return (n, 2, rows + 2 * PAD, LANES)

    def plain(n):
        return (n, 2, rows, LANES)

    first, second, third = (pltpu.with_memory_space_constraint(v, pltpu.VMEM) for v in (first, second, third))
    (peak,) = call(peak_kernel, "peak", [held((8, LANES))], [], [first, second, third])
    peak = largest_over(peak)
    state, send_outer, send_inner = call(
        begin_kernel,
        "begin",
        [held(padded(count)), held(plain(OUTER + 2)), held(plain(INNER + 1))],
        [odd],
        [fraction, seed_mask, first],
    )
    outer = swap(send_outer, True)
    inner = swap(send_inner, False)
    cosine = jnp.cos(jnp.pi * (wall_class.astype(jnp.float32) + 1.0) / (WALL_CLASSES + 1))
    (wall,) = call(wall_kernel, "wall", [held((layers, rows, LANES))], [place], [cosine])
    moved, step = call(
        moved_kernel, "moved", [held(plain(layers - INNER - 1)), held((8, LANES))], [odd], [peak, first, outer, inner]
    )
    own = [state]
    line = [pltpu.VMEM(padded(1), jnp.float32)] * 4
    for turn in range(STEPS):
        final = turn == STEPS - 1
        swept, send = call(
            functools.partial(first_kernel, own_parts=len(own), layers=layers),
            "first",
            [held(padded(layers - INNER - 1)), held(plain(1))],
            [],
            [*own, outer, inner, moved, wall],
            [pltpu.VMEM(padded(layers), jnp.float32)] * 5,
            faces=layers - INNER - 1,
        )
        inner = swap(send, False)

        def second_call(work, fields, places, send_last):
            outs = [held(padded(len(work)))] + ([held(plain(1))] if send_last is not None else [])
            return call(
                functools.partial(second_kernel, places=places, work=work, send_last=send_last),
                "second",
                outs,
                [odd],
                [step, second, wall, *fields],
                line,
                faces=len(work),
            )

        edge, send_outer = second_call((OUTER,), [swept], [(1, True)], OUTER)
        outer = swap(send_outer, True)
        (middle,) = second_call(tuple(range(OUTER + 1, own_end - 1)), [swept], [(1, True)], None)
        last, send_inner = second_call(
            (own_end - 1,), [swept, inner], [(1, True), (own_end, False)], own_end - 1
        )
        inner = swap(send_inner, False)

        def third_call(work, fields, places, out):
            return call(
                functools.partial(third_kernel, places=places, work=work, final=False),
                "third",
                [out],
                [odd],
                [step, third, wall, *fields],
                faces=len(work),
            )[0]

        middle_new = third_call(
            tuple(range(OUTER + 1, own_end - 1)),
            [edge, middle, last],
            [(OUTER, True), (OUTER + 1, True), (own_end - 1, True)],
            held(padded(count - 2)),
        )
        last_new = third_call(
            (own_end - 1,),
            [middle, last, inner],
            [(OUTER + 1, True), (own_end - 1, True), (own_end, False)],
            held(padded(1)),
        )
        edge_new = third_call(
            (OUTER,),
            [outer, edge, middle],
            [(OUTER - 1, False), (OUTER, True), (OUTER + 1, True)],
            held(padded(1)),
        )
        own = [edge_new, middle_new, last_new]
        if not final:
            send_outer, send_inner = call(
                pack_kernel, "pack", [held(plain(OUTER)), held(plain(INNER))], [], own
            )
            outer = swap(send_outer, True)
            inner = swap(send_inner, False)
    (out,) = call(unpack_kernel, "unpack", [jax.ShapeDtypeStruct(fraction.shape, jnp.float32)], [odd], own)
    return out


def pack_kernel(edge, middle, last, send_outer, send_inner):
    rows = send_outer.shape[2]
    own = [Layer(ref, k) for ref in (edge, middle, last) for k in range(ref.shape[0])]
    for k in range(OUTER):
        copy_layer(own[k], Layer(send_outer, k, False), rows)
    for k in range(INNER):
        copy_layer(own[-1 - k], Layer(send_inner, k, False), rows)


def unpack_kernel(odd_ref, edge, middle, last, out):
    odd = odd_ref[0] == 1
    count, rows, _ = out.shape
    own = [Layer(ref, k) for ref in (edge, middle, last) for k in range(ref.shape[0])]
    for k, layer in enumerate(own):
        index = own_index(odd, OUTER + k, count)
        for r in range(0, rows, ROWS):
            for h in HALVES:
                out[index, pl.ds(r, ROWS), h * LANES : (h + 1) * LANES] = layer.read(h, r)


def solution(mesh):
    split = P(("ens", "gx"), None, None)
    return jax.shard_map(
        shards, mesh=mesh, in_specs=(split, split, split, split, P(), split), out_specs=split, check_vma=False
    )
```

```python
import functools

import jax
import jax.numpy as jnp
from jax import lax
from jax.experimental import pallas as pl
from jax.experimental.pallas import tpu as pltpu
from jax.sharding import PartitionSpec as P

STEPS = 2
NEWTON = 4
WALL_CLASSES = 4
CFL_NUMBER = 0.45

LANES = 128
PAD = 8
ROWS = 32
HALVES = (0, 1)
OUTER = 2
INNER = 2
VMEM_LIMIT = 24 * 1024 * 1024
SEND_ROUND = 2


def cube(t):
    t = jnp.maximum(t, 0.0)
    return t * t * t


def square(t):
    t = jnp.maximum(t, 0.0)
    return t * t


def rcp(x):
    return pl.reciprocal(x, approx=True)


def plane(donor, span, soft_a, soft_b):
    low = jnp.minimum(soft_a, soft_b)
    high = jnp.maximum(soft_a, soft_b)
    pair = soft_a + soft_b
    half = 0.5 * (span + pair)
    top = jnp.maximum(span, high)
    mid = jnp.minimum(span, high)
    over = half - top
    last = half - jnp.abs(over)
    sign = jnp.where(over > 0.0, -1.0, 1.0)
    flat = low * mid
    bulk = flat * top
    share = jnp.clip(jnp.minimum(donor, 1.0 - donor), 0.0, 0.5)
    goal = bulk * share
    at = half - (0.25 * bulk - 0.5 * goal) * rcp(flat - square(over))
    low_6 = low * (1.0 / 6.0)
    mid_6 = mid * (1.0 / 6.0)
    last_6 = last * (1.0 / 6.0)
    for _ in range(NEWTON - 1):
        by_low = square(at - low)
        by_mid = square(at - mid)
        by_last = sign * square(at - last)
        growth = at * at - by_low - by_mid + by_last
        shift = goal - low_6 * by_low - mid_6 * by_mid + last_6 * by_last
        at = (5.0 / 6.0) * at + shift * rcp(growth)
    return at, low, high, pair, half, bulk


def edge_sum(at, low):
    return cube(at) - cube(at - low)


def side_sum(at, low, high, pair):
    return cube(at) - cube(at - low) - cube(at - high) + cube(at - pair)


def prepare(donor, along, soft_a, soft_b, ahead):
    span = jnp.abs(along) + 0.2
    at, low, high, pair, half, bulk = plane(donor, span, soft_a, soft_b)
    light = donor <= 0.5
    sense = jnp.where(jnp.logical_xor(light, ahead), -1.0, 1.0)
    weight = jnp.clip(0.5 + (along * sense) * rcp(half), 0.0, 1.0)
    whole = side_sum(at, low, high, pair)
    whole = whole - weight * (whole + edge_sum(at - span, low))
    scale = sense * rcp(6.0 * bulk)
    heavy = jnp.where(light, 0.0, 1.0)
    return at, span, low, high, weight, scale, whole, heavy


def finish(at, span, low, high, weight, scale, whole, heavy, moved):
    slab = jnp.abs(moved) * span
    rest = side_sum(at - slab, low, high, low + high)
    near = edge_sum(at - span + slab, low)
    return (whole - rest + weight * (rest + near)) * scale + heavy * moved


def face_flux(donor, along, soft_a, soft_b, moved):
    return finish(*prepare(donor, along, soft_a, soft_b, moved > 0.0), moved)


def lane_of(value):
    return lax.broadcasted_iota(jnp.int32, value.shape, 1)


def from_above(pair):
    turned = [pltpu.roll(v, LANES - 1, 1) for v in pair]
    last = lane_of(pair[0]) == LANES - 1
    return [jnp.where(last, turned[1], turned[0]), jnp.where(last, turned[0], turned[1])]


def from_below(pair):
    turned = [pltpu.roll(v, 1, 1) for v in pair]
    first = lane_of(pair[0]) == 0
    return [jnp.where(first, turned[1], turned[0]), jnp.where(first, turned[0], turned[1])]


class Layer:
    def __init__(self, ref, index, padded=True):
        self.ref, self.index, self.pad = ref, index, PAD if padded else 0

    def read(self, half, row):
        return self.ref[self.index, half, pl.ds(self.pad + row, ROWS), :]

    def write(self, half, row, value):
        self.ref[self.index, half, pl.ds(self.pad + row, ROWS), :] = value

    def wrap(self):
        rows = self.ref.shape[2] - 2 * PAD
        for h in HALVES:
            self.ref[self.index, h, pl.ds(0, PAD), :] = self.ref[self.index, h, pl.ds(rows, PAD), :]
            self.ref[self.index, h, pl.ds(PAD + rows, PAD), :] = self.ref[self.index, h, pl.ds(PAD, PAD), :]


def copy_layer(source, target, rows):
    for r in range(0, rows, ROWS):
        for h in HALVES:
            target.write(h, r, source.read(h, r))


def fill(source, field, start, way, begin, end, padded):
    rows = field.shape[2] - 2 * PAD

    @pl.loop(begin, end)
    def _(k):
        target = Layer(field, start + way * k)
        copy_layer(Layer(source, k, padded), target, rows)
        target.wrap()


def normals(before, here, after, wall, row):
    centre = [here.read(h, row) for h in HALVES]
    n_x = [before.read(h, row) - after.read(h, row) for h in HALVES]
    n_y = [here.read(h, row - 1) - here.read(h, row + 1) for h in HALVES]
    above = from_above(centre)
    below = from_below(centre)
    lane = lane_of(centre[0])
    above[1] = jnp.where(lane == LANES - 1, centre[1], above[1])
    n_z = [below[h] - above[h] for h in HALVES]
    contact = wall[pl.ds(row, ROWS), :] * (jnp.abs(n_x[0]) + jnp.abs(n_y[0]))
    n_z[0] = jnp.where(lane == 0, contact, n_z[0])
    return centre, n_x, n_y, n_z


def soft(normal):
    return jnp.abs(normal) + 0.2


def own_index(odd, layer, count):
    return jnp.where(odd, OUTER + count - 1 - layer, layer - OUTER)


def natural(ref, index, half, row):
    return ref[index, pl.ds(row, ROWS), half * LANES : (half + 1) * LANES]


def begin_kernel(odd_ref, fraction_in, mask_in, *refs):
    speeds_in, (*speeds, peak, state, send_outer, send_inner, fraction, mask, sems) = refs[:3], refs[3:]
    odd = odd_ref[0] == 1
    count, rows, width = fraction.shape
    sources = (*speeds_in, fraction_in, mask_in)
    copies = [
        pltpu.make_async_copy(source, target, sems.at[n])
        for n, (source, target) in enumerate(zip(sources, (*speeds, fraction, mask)))
    ]
    for copy in copies:
        copy.start()
    best = jnp.zeros((8, width), jnp.float32)
    for n, ref in enumerate(speeds):
        copies[n].wait()
        for i in range(count):
            best = jnp.maximum(best, jnp.max(jnp.abs(ref[i]).reshape(rows // 8, 8, width), axis=0))
    peak[...] = jnp.maximum(best[:, :LANES], best[:, LANES:])
    copies[3].wait()
    copies[4].wait()
    for p in range(OUTER, OUTER + count):
        index = own_index(odd, p, count)
        to = [Layer(state, p - OUTER)]
        if p - OUTER < OUTER:
            to.append(Layer(send_outer, p - OUTER, False))
        if OUTER + count - 1 - p < INNER:
            to.append(Layer(send_inner, OUTER + count - 1 - p, False))
        for r in range(0, rows, ROWS):
            for h in HALVES:
                value = jnp.where(natural(mask, index, h, r) == 1, 1.0, natural(fraction, index, h, r))
                for target in to:
                    target.write(h, r, value)
        Layer(state, p - OUTER).wrap()
    first = speeds[0]
    for r in range(0, rows, ROWS):
        for h in HALVES:
            Layer(send_outer, OUTER, False).write(h, r, natural(first, count - 1, h, r))
            Layer(send_inner, INNER, False).write(h, r, natural(first, count - 1, h, r))


def wall_kernel(where_ref, cosine, out):
    odd = where_ref[0] == 1
    total = cosine.shape[0]
    layers = out.shape[0]
    count = layers - OUTER - INNER
    for p in range(1, layers - 1):
        row = lax.rem(where_ref[1] + own_index(odd, p, count) + total, total)
        out[p] = jnp.transpose(jnp.broadcast_to(cosine[pl.ds(row, 1), :], (LANES, cosine.shape[1])))


KEPT = 9


def prepare_kernel(odd_ref, *refs, kinds, faces, count):
    given = dict(zip(kinds, refs))
    wall = given["wall"]
    out, field, n_s, n_a, n_b = refs[len(kinds) :]
    rows = out.shape[2]
    odd = odd_ref[0] == 1
    sign = jnp.where(odd, -1.0, 1.0)
    start, stop = faces[0], faces[-1] + 1
    lowest, highest = start - 1, stop + 1
    for kind, first_layer, way, number, is_padded in (
        ("outer", OUTER - 1, -1, OUTER, False),
        ("own", OUTER, 1, count, True),
        ("inner", OUTER + count, 1, INNER, False),
    ):
        if kind not in given:
            continue
        used = [k for k in range(number) if lowest <= first_layer + way * k <= highest]
        if used:
            fill(given[kind], field, first_layer, way, used[0], used[-1] + 1, is_padded)

    @pl.loop(start, stop + 1)
    def _(i):
        for r in range(0, rows, ROWS):
            _, n_x, n_y, n_z = normals(Layer(field, i - 1), Layer(field, i), Layer(field, i + 1), wall.at[i], r)
            for h in HALVES:
                Layer(n_s, i, False).write(h, r, n_x[h])
                Layer(n_a, i, False).write(h, r, soft(n_y[h]))
                Layer(n_b, i, False).write(h, r, soft(n_z[h]))

    speed = KEPT - 1
    for k, face in enumerate(faces):
        for r in range(0, rows, ROWS):
            for h in HALVES:
                if face == OUTER - 1:
                    value = natural(given["first"], count - 1, h, r)
                    value = jnp.where(odd, value, Layer(given["outer"], OUTER, False).read(h, r))
                elif face == OUTER + count - 1:
                    value = natural(given["first"], count - 1, h, r)
                    value = jnp.where(odd, Layer(given["inner"], INNER, False).read(h, r), value)
                else:
                    value = natural(given["first"], jnp.where(odd, OUTER + count - 2 - face, face - OUTER), h, r)
                Layer(out, k * KEPT + speed, False).write(h, r, value * sign)

    @pl.loop(0, len(faces))
    def _(k):
        i = start + k
        for r in range(0, rows, ROWS):
            for h in HALVES:
                ahead = Layer(out, k * KEPT + speed, False).read(h, r) > 0.0

                def donor(ref, padded=False):
                    return jnp.where(ahead, Layer(ref, i, padded).read(h, r), Layer(ref, i + 1, padded).read(h, r))

                kept = prepare(donor(field, True), donor(n_s), donor(n_a), donor(n_b), ahead)
                for n, value in enumerate(kept):
                    Layer(out, k * KEPT + n, False).write(h, r, value)


def finish_faces(kept, step, flux, moved, start):
    rows = kept.shape[2]

    @pl.loop(0, kept.shape[0] // KEPT)
    def _(k):
        for r in range(0, rows, ROWS):
            for h in HALVES:
                values = [Layer(kept, k * KEPT + n, False).read(h, r) for n in range(KEPT)]
                values[-1] = values[-1] * step
                Layer(moved, start + k, False).write(h, r, values[-1])
                Layer(flux, start + k, False).write(h, r, finish(*values))


def update(target, here, inward, outward, rows):
    for r in range(0, rows, ROWS):
        for h in HALVES:
            target.write(h, r, jnp.clip(here.read(h, r) - outward.read(h, r) + inward.read(h, r), 0.0, 1.0))
    target.wrap()


def finish_kernel(peak, *refs, parts):
    kept, (state, out, moved, step_out, send_outer, send_inner, flux) = refs[:parts], refs[parts:]
    rows = moved.shape[2]
    largest = jnp.max(peak[...])
    step = CFL_NUMBER / (jnp.full((8, LANES), largest, jnp.float32) + 1e-6)
    step_out[...] = step
    start = 0
    for ref in kept:
        finish_faces(ref, step[:1, :], flux, moved, start)
        start += ref.shape[0] // KEPT

    @pl.loop(0, state.shape[0])
    def _(k):
        update(Layer(out, k), Layer(state, k), Layer(flux, k, False), Layer(flux, k + 1, False), rows)

    copy_layer(Layer(out, 0), Layer(send_outer, 0, False), rows)
    copy_layer(Layer(out, out.shape[0] - 1), Layer(send_inner, 0, False), rows)


def first_fluxes(field, wall, moved, n_s, n_a, n_b, flux, start, stop):
    rows = flux.shape[2]

    @pl.loop(start, stop + 1)
    def _(i):
        for r in range(0, rows, ROWS):
            _, n_x, n_y, n_z = normals(Layer(field, i - 1), Layer(field, i), Layer(field, i + 1), wall.at[i], r)
            for h in HALVES:
                Layer(n_s, i, False).write(h, r, n_x[h])
                Layer(n_a, i, False).write(h, r, soft(n_y[h]))
                Layer(n_b, i, False).write(h, r, soft(n_z[h]))

    @pl.loop(start, stop)
    def _(i):
        for r in range(0, rows, ROWS):
            for h in HALVES:
                speed = Layer(moved, i - 1, False).read(h, r)
                ahead = speed > 0.0

                def donor(ref, padded=False):
                    return jnp.where(ahead, Layer(ref, i, padded).read(h, r), Layer(ref, i + 1, padded).read(h, r))

                through = face_flux(donor(field, True), donor(n_s), donor(n_a), donor(n_b), speed)
                Layer(flux, i - 1, False).write(h, r, through)


def inside_kernel(edge, middle, last, inner, moved, wall, out, flux_out, send, field, n_s, n_a, n_b, flux):
    rows = moved.shape[2]
    count = middle.shape[0] + 2
    fill(edge, field, OUTER, 1, 0, 1, True)
    fill(middle, field, OUTER + 1, 1, 0, count - 2, True)
    fill(last, field, OUTER + count - 1, 1, 0, 1, True)
    fill(inner, field, OUTER + count, 1, 0, INNER, False)
    first_fluxes(field, wall, moved, n_s, n_a, n_b, flux, OUTER + 1, OUTER + count)
    copy_layer(Layer(flux, OUTER, False), Layer(flux_out, 0, False), rows)

    @pl.loop(OUTER + 2, OUTER + count)
    def _(i):
        update(Layer(out, i - OUTER - 2), Layer(field, i), Layer(flux, i - 2, False), Layer(flux, i - 1, False), rows)

    copy_layer(Layer(out, count - 3), Layer(send, 0, False), rows)


def outside_kernel(edge, middle, last, outer, moved, wall, flux_above, out, send, field, n_s, n_a, n_b, flux):
    rows = moved.shape[2]
    count = middle.shape[0] + 2
    fill(outer, field, OUTER - 1, -1, 0, OUTER, False)
    fill(edge, field, OUTER, 1, 0, 1, True)
    fill(middle, field, OUTER + 1, 1, 0, count - 2, True)
    if count < 4:
        fill(last, field, OUTER + count - 1, 1, 0, 1, True)
    first_fluxes(field, wall, moved, n_s, n_a, n_b, flux, OUTER - 1, OUTER + 1)
    edge_layer, next_layer = Layer(out, 0), Layer(out, 1)
    update(edge_layer, Layer(field, OUTER), Layer(flux, 0, False), Layer(flux, 1, False), rows)
    update(next_layer, Layer(field, OUTER + 1), Layer(flux, 1, False), Layer(flux_above, 0, False), rows)
    copy_layer(edge_layer, Layer(send, 0, False), rows)


def second_sweep(before, here, after, wall, speed, out, scratch):
    n_s, n_a, n_b, flux = scratch
    rows = out.ref.shape[2] - 2 * PAD
    for r in range(0, rows, ROWS):
        _, n_x, n_y, n_z = normals(before, here, after, wall, r)
        for h in HALVES:
            n_s.write(h, r, n_y[h])
            n_a.write(h, r, soft(n_x[h]))
            n_b.write(h, r, soft(n_z[h]))
    for s in (n_s, n_a, n_b):
        s.wrap()
    for r in range(0, rows, ROWS):
        for h in HALVES:
            moved = speed(h, r)
            ahead = moved > 0.0
            donor = [jnp.where(ahead, s.read(h, r), s.read(h, r + 1)) for s in (here, n_s, n_a, n_b)]
            flux.write(h, r, face_flux(*donor, moved))
    flux.wrap()
    for r in range(0, rows, ROWS):
        for h in HALVES:
            out.write(h, r, jnp.clip(here.read(h, r) - flux.read(h, r) + flux.read(h, r - 1), 0.0, 1.0))
    out.wrap()


def third_sweep(before, here, after, wall, speed, write, rows):
    for r in range(0, rows, ROWS):
        centre, n_x, n_y, n_z = normals(before, here, after, wall, r)
        fields = [centre, n_z, [soft(v) for v in n_x], [soft(v) for v in n_y]]
        above = [from_above(f) for f in fields]
        lane = lane_of(centre[0])
        through = []
        for h in HALVES:
            moved = speed(h, r)
            if h == 1:
                moved = jnp.where(lane == LANES - 1, 0.0, moved)
            ahead = moved > 0.0
            through.append(face_flux(*[jnp.where(ahead, f[h], a[h]) for f, a in zip(fields, above)], moved))
        below = from_below(through)
        for h in HALVES:
            value = jnp.clip(centre[h] - through[h] + below[h], 0.0, 1.0)
            write(h, r, value)


def gather_layers(refs, places):
    found = {}
    for ref, (start, padded) in zip(refs, places):
        for k in range(ref.shape[0]):
            found[start + k] = Layer(ref, k, padded)
    return found


def second_kernel(odd_ref, step, speed_ref, wall, *refs, places, work, send_last):
    fields, rest = refs[: len(places)], refs[len(places) :]
    out, rest = rest[0], rest[1:]
    send, rest = (rest[0], rest[1:]) if send_last is not None else (None, rest)
    scratch = [Layer(ref, 0) for ref in rest]
    layers = gather_layers(fields, places)
    odd = odd_ref[0] == 1
    count, rows, _ = speed_ref.shape
    for k, p in enumerate(work):
        index = own_index(odd, p, count)
        second_sweep(
            layers[p - 1],
            layers[p],
            layers[p + 1],
            wall.at[p],
            lambda h, r: natural(speed_ref, index, h, r) * step[:1, :],
            Layer(out, k),
            scratch,
        )
    if send is not None:
        copy_layer(Layer(out, work.index(send_last)), Layer(send, 0, False), rows)


def third_kernel(odd_ref, step, speed_ref, wall, *refs, places, work):
    fields, (out,) = refs[: len(places)], refs[len(places) :]
    layers = gather_layers(fields, places)
    odd = odd_ref[0] == 1
    count, rows, _ = speed_ref.shape
    for k, p in enumerate(work):
        index = own_index(odd, p, count)
        third_sweep(
            layers[p - 1],
            layers[p],
            layers[p + 1],
            wall.at[p],
            lambda h, r: natural(speed_ref, index, h, r) * step[:1, :],
            Layer(out, k).write,
            rows,
        )
        Layer(out, k).wrap()


def last_kernel(odd_ref, step, speed_ref, wall, *refs, places):
    fields, rest = refs[: len(places)], refs[len(places) :]
    done, (out, held_out, sems) = rest[:-3], rest[-3:]
    layers = gather_layers(fields, places)
    odd = odd_ref[0] == 1
    count, rows, _ = speed_ref.shape
    copies = []

    def send(source, layer, h):
        target = out.at[own_index(odd, layer, count), :, h * LANES : (h + 1) * LANES]
        copies.append(pltpu.make_async_copy(source, target, sems.at[len(copies)]))
        copies[-1].start()

    p = OUTER + 1
    for ref in done:
        for k in range(ref.shape[0]):
            for h in HALVES:
                send(ref.at[k, h, pl.ds(PAD, rows), :], p, h)
            p += 1

    def write(h, r, value):
        held_out[h, pl.ds(r, ROWS), :] = value

    index = own_index(odd, OUTER, count)
    third_sweep(
        layers[OUTER - 1],
        layers[OUTER],
        layers[OUTER + 1],
        wall.at[OUTER],
        lambda h, r: natural(speed_ref, index, h, r) * step[:1, :],
        write,
        rows,
    )
    for h in HALVES:
        send(held_out.at[h], OUTER, h)
    for copy in copies:
        copy.wait()


IN_VMEM = pl.BlockSpec(memory_space=pltpu.VMEM)
IN_SMEM = pl.BlockSpec(memory_space=pltpu.SMEM)


def held(shape):
    return pltpu.VMEM(shape, jnp.float32)


def call(kernel, name, outs, scalars, arrays, scratch=(), faces=0.1, resident=True):
    space = pltpu.VMEM if resident else pltpu.HBM
    arrays = [pltpu.with_memory_space_constraint(a, space) for a in arrays]
    work = int(faces * 1.1e9)
    return pl.pallas_call(
        kernel,
        out_shape=outs,
        in_specs=[IN_SMEM] * len(scalars) + [pl.BlockSpec(memory_space=space)] * len(arrays),
        out_specs=[IN_VMEM] * len(outs),
        scratch_shapes=list(scratch),
        compiler_params=pltpu.CompilerParams(vmem_limit_bytes=VMEM_LIMIT),
        cost_estimate=pl.CostEstimate(flops=work, bytes_accessed=1024, transcendentals=0),
        name=name,
    )(*scalars, *arrays)


def swap(array, outer):
    count = lax.axis_size("gx")
    if outer:
        pairs = [(i, (i + 1) % count if i % 2 else (i - 1) % count) for i in range(count)]
    else:
        pairs = [(i, i ^ 1) for i in range(count)]
    return lax.ppermute(array, "gx", pairs)


def largest_round(array, reach, beside):
    count = lax.axis_size("gx")
    if count & (count - 1) == 0:
        pairs = [(i, i ^ reach) for i in range(count)]
    else:
        pairs = [(i, (i + reach) % count) for i in range(count)]
    received = lax.ppermute(array, "gx", pairs)
    if beside:
        received, *_ = lax.optimization_barrier((received, *beside))
    return jnp.maximum(array, received)


def shards(fraction, first, second, third, wall_class, seed_mask):
    count, rows, width = fraction.shape
    layers = OUTER + count + INNER
    own_end = OUTER + count
    device = lax.axis_index("gx")
    odd = (device % 2).astype(jnp.int32).reshape(1)
    place = jnp.stack([device % 2, device * count]).astype(jnp.int32)

    def padded(n):
        return (n, 2, rows + 2 * PAD, LANES)

    def plain(n):
        return (n, 2, rows, LANES)

    natural_shape = (count, rows, width)
    first, second, third, peak, state, send_outer, send_inner = call(
        begin_kernel,
        "begin",
        [held(natural_shape)] * 3
        + [held((8, LANES)), held(padded(count)), held(plain(OUTER + 1)), held(plain(INNER + 1))],
        [odd],
        [fraction, seed_mask, first, second, third],
        [
            pltpu.VMEM(natural_shape, jnp.float32),
            pltpu.VMEM(natural_shape, jnp.int32),
            pltpu.SemaphoreType.DMA((5,)),
        ],
        resident=False,
    )
    inner = swap(send_inner, False)
    cosine = jnp.cos(jnp.pi * (wall_class.astype(jnp.float32) + 1.0) / (WALL_CLASSES + 1))
    (wall,) = call(wall_kernel, "wall", [held((layers, rows, LANES))], [place], [cosine])
    slopes = [pltpu.VMEM(padded(layers), jnp.float32)] + [pltpu.VMEM(plain(layers), jnp.float32)] * 3

    def prepare_call(faces, **given):
        return call(
            functools.partial(prepare_kernel, kinds=tuple(given), faces=faces, count=count),
            "prepare",
            [held(plain(KEPT * len(faces)))],
            [odd],
            list(given.values()),
            slopes,
            faces=len(faces),
        )[0]

    size = lax.axis_size("gx")
    prepare_inside = functools.partial(prepare_call, wall=wall, first=first, own=state, inner=inner)
    peak = largest_round(peak, 1, [])
    kept = [prepare_inside(tuple(range(OUTER + 2, own_end)))]
    if size > 2:
        peak = largest_round(peak, 2, kept)
    peak, send_outer = lax.optimization_barrier((peak, send_outer))
    outer = swap(send_outer, True)
    kept.insert(0, prepare_inside((OUTER + 1,)))
    kept.insert(0, prepare_call((OUTER - 1, OUTER), wall=wall, first=first, own=state, outer=outer))
    reach, beside = 4, [[kept[1]]]
    while reach < size:
        peak = largest_round(peak, reach, beside.pop() if beside else [])
        reach *= 2
    own, moved, step, send_outer, send_inner = call(
        functools.partial(finish_kernel, parts=len(kept)),
        "finish",
        [held(padded(count)), held(plain(count + 1)), held((8, LANES)), held(plain(1)), held(plain(1))],
        [],
        [peak, *kept, state],
        [pltpu.VMEM(plain(count + 1), jnp.float32)],
        faces=1,
    )
    swept, places = [own], [(OUTER, True)]
    line = [pltpu.VMEM(padded(1), jnp.float32)] * 4
    for turn in range(STEPS):
        final = turn == STEPS - 1
        if turn > 0:
            flux = pltpu.VMEM(plain(count + 1), jnp.float32)
            inside, flux_low, send_inner = call(
                inside_kernel,
                "inside",
                [held(padded(count - 2)), held(plain(1)), held(plain(1))],
                [],
                [*own, inner, moved, wall],
                [*slopes, flux],
                faces=count - 1,
            )
            outside, send_outer = call(
                outside_kernel,
                "outside",
                [held(padded(2)), held(plain(1))],
                [],
                [*own, outer, moved, wall, flux_low],
                [*slopes, flux],
                faces=2,
            )
            swept, places = [outside, inside], [(OUTER, True), (OUTER + 2, True)]
        inner = swap(send_inner, False)
        outer = swap(send_outer, True)

        def second_call(work, fields, places, send):
            return call(
                functools.partial(second_kernel, places=places, work=work, send_last=work[0] if send else None),
                "second",
                [held(padded(len(work)))] + ([held(plain(1))] if send else []),
                [odd],
                [step, second, wall, *fields],
                line,
                faces=len(work),
            )

        last, send_inner = second_call((own_end - 1,), [swept[-1], inner], [places[-1], (own_end, False)], True)
        inner = swap(send_inner, False)
        (middle,) = second_call(tuple(range(OUTER + 1, own_end - 1)), swept, places, False)
        edge, send_outer = second_call((OUTER,), [outer, swept[0]], [(OUTER - 1, False), places[0]], True)
        outer = swap(send_outer, True)

        fields = [edge, middle, last, inner]
        starts = [(OUTER, True), (OUTER + 1, True), (own_end - 1, True), (own_end, False)]
        inside_work = tuple(range(OUTER + 1, own_end))
        edge_fields, edge_starts = [outer, edge, middle], [(OUTER - 1, False), (OUTER, True), (OUTER + 1, True)]
        def third_call(work, fields, places):
            return call(
                functools.partial(third_kernel, places=places, work=work),
                "third",
                [held(padded(len(work)))],
                [odd],
                [step, third, wall, *fields],
                faces=len(work),
            )[0]

        middle_new = third_call(inside_work[:-1], fields[:-1], starts[:-1])
        last_new = third_call(inside_work[-1:], fields[1:], starts[1:])
        if final:
            return last_call(odd, step, third, wall, edge_fields, edge_starts, [middle_new, last_new], natural_shape)
        edge_new = third_call((OUTER,), edge_fields, edge_starts)
        own = [edge_new, middle_new, last_new]
        send_outer, send_inner = call(pack_kernel, "pack", [held(plain(OUTER)), held(plain(INNER))], [], own)
        outer = swap(send_outer, True)
        inner = swap(send_inner, False)


def last_call(odd, step, speed, wall, fields, places, done, shape):
    arrays = [pltpu.with_memory_space_constraint(a, pltpu.VMEM) for a in (step, speed, wall, *fields, *done)]
    return pl.pallas_call(
        functools.partial(last_kernel, places=places),
        out_shape=jax.ShapeDtypeStruct(shape, jnp.float32),
        in_specs=[IN_SMEM] + [IN_VMEM] * len(arrays),
        out_specs=pl.BlockSpec(memory_space=pltpu.HBM),
        scratch_shapes=[pltpu.VMEM((2, *shape[1:2], LANES), jnp.float32), pltpu.SemaphoreType.DMA((2 * shape[0],))],
        compiler_params=pltpu.CompilerParams(vmem_limit_bytes=VMEM_LIMIT),
        cost_estimate=pl.CostEstimate(flops=int(1.1e9), bytes_accessed=1024, transcendentals=0),
        name="last",
    )(odd, *arrays)


def pack_kernel(edge, middle, last, send_outer, send_inner):
    rows = send_outer.shape[2]
    own = [Layer(ref, k) for ref in (edge, middle, last) for k in range(ref.shape[0])]
    for k in range(OUTER):
        copy_layer(own[k], Layer(send_outer, k, False), rows)
    for k in range(INNER):
        copy_layer(own[-1 - k], Layer(send_inner, k, False), rows)


def solution(mesh):
    split = P(("ens", "gx"), None, None)
    return jax.shard_map(
        shards, mesh=mesh, in_specs=(split, split, split, split, P(), split), out_specs=split, check_vma=False
    )
```

```python
import functools

import jax
import jax.numpy as jnp
from jax import lax
from jax.experimental import pallas as pl
from jax.experimental.pallas import tpu as pltpu
from jax.sharding import PartitionSpec as P

STEPS = 2
NEWTON = 4
WALL_CLASSES = 4
CFL_NUMBER = 0.45

LANES = 128
PAD = 8
ROWS = 32
HALVES = (0, 1)
OUTER = 3
INNER = 2
VMEM_LIMIT = 24 * 1024 * 1024
SEND_ROUND = 2


def cube(t):
    t = jnp.maximum(t, 0.0)
    return t * t * t


def square(t):
    t = jnp.maximum(t, 0.0)
    return t * t


def rcp(x):
    return pl.reciprocal(x, approx=True)


def plane(donor, span, soft_a, soft_b):
    low = jnp.minimum(soft_a, soft_b)
    high = jnp.maximum(soft_a, soft_b)
    pair = soft_a + soft_b
    half = 0.5 * (span + pair)
    top = jnp.maximum(span, high)
    mid = jnp.minimum(span, high)
    over = half - top
    last = half - jnp.abs(over)
    sign = jnp.where(over > 0.0, -1.0, 1.0)
    flat = low * mid
    bulk = flat * top
    share = jnp.clip(jnp.minimum(donor, 1.0 - donor), 0.0, 0.5)
    goal = bulk * share
    at = half - (0.25 * bulk - 0.5 * goal) * rcp(flat - square(over))
    low_6 = low * (1.0 / 6.0)
    mid_6 = mid * (1.0 / 6.0)
    last_6 = last * (1.0 / 6.0)
    for _ in range(NEWTON - 1):
        by_low = square(at - low)
        by_mid = square(at - mid)
        by_last = sign * square(at - last)
        growth = at * at - by_low - by_mid + by_last
        shift = goal - low_6 * by_low - mid_6 * by_mid + last_6 * by_last
        at = (5.0 / 6.0) * at + shift * rcp(growth)
    return at, low, high, pair, half, bulk


def edge_sum(at, low):
    return cube(at) - cube(at - low)


def side_sum(at, low, high, pair):
    return cube(at) - cube(at - low) - cube(at - high) + cube(at - pair)


def prepare(donor, along, soft_a, soft_b, ahead):
    span = jnp.abs(along) + 0.2
    at, low, high, pair, half, bulk = plane(donor, span, soft_a, soft_b)
    light = donor <= 0.5
    sense = jnp.where(jnp.logical_xor(light, ahead), -1.0, 1.0)
    weight = jnp.clip(0.5 + (along * sense) * rcp(half), 0.0, 1.0)
    whole = side_sum(at, low, high, pair)
    whole = whole - weight * (whole + edge_sum(at - span, low))
    scale = sense * rcp(6.0 * bulk)
    heavy = jnp.where(light, 0.0, 1.0)
    return at, span, low, high, weight, scale, whole, heavy


def finish(at, span, low, high, weight, scale, whole, heavy, moved):
    slab = jnp.abs(moved) * span
    rest = side_sum(at - slab, low, high, low + high)
    near = edge_sum(at - span + slab, low)
    return (whole - rest + weight * (rest + near)) * scale + heavy * moved


def face_flux(donor, along, soft_a, soft_b, moved):
    return finish(*prepare(donor, along, soft_a, soft_b, moved > 0.0), moved)


def lane_of(value):
    return lax.broadcasted_iota(jnp.int32, value.shape, 1)


def from_above(pair):
    turned = [pltpu.roll(v, LANES - 1, 1) for v in pair]
    last = lane_of(pair[0]) == LANES - 1
    return [jnp.where(last, turned[1], turned[0]), jnp.where(last, turned[0], turned[1])]


def from_below(pair):
    turned = [pltpu.roll(v, 1, 1) for v in pair]
    first = lane_of(pair[0]) == 0
    return [jnp.where(first, turned[1], turned[0]), jnp.where(first, turned[0], turned[1])]


class Layer:
    def __init__(self, ref, index, padded=True):
        self.ref, self.index, self.pad = ref, index, PAD if padded else 0

    def read(self, half, row):
        return self.ref[self.index, half, pl.ds(self.pad + row, ROWS), :]

    def write(self, half, row, value):
        self.ref[self.index, half, pl.ds(self.pad + row, ROWS), :] = value

    def wrap(self):
        rows = self.ref.shape[2] - 2 * PAD
        for h in HALVES:
            self.ref[self.index, h, pl.ds(0, PAD), :] = self.ref[self.index, h, pl.ds(rows, PAD), :]
            self.ref[self.index, h, pl.ds(PAD + rows, PAD), :] = self.ref[self.index, h, pl.ds(PAD, PAD), :]


def copy_layer(source, target, rows):
    for r in range(0, rows, ROWS):
        for h in HALVES:
            target.write(h, r, source.read(h, r))


def fill(source, field, start, way, begin, end, padded):
    rows = field.shape[2] - 2 * PAD

    @pl.loop(begin, end)
    def _(k):
        target = Layer(field, start + way * k)
        copy_layer(Layer(source, k, padded), target, rows)
        target.wrap()


def normals(before, here, after, wall, row):
    centre = [here.read(h, row) for h in HALVES]
    n_x = [before.read(h, row) - after.read(h, row) for h in HALVES]
    n_y = [here.read(h, row - 1) - here.read(h, row + 1) for h in HALVES]
    above = from_above(centre)
    below = from_below(centre)
    lane = lane_of(centre[0])
    above[1] = jnp.where(lane == LANES - 1, centre[1], above[1])
    n_z = [below[h] - above[h] for h in HALVES]
    contact = wall[pl.ds(row, ROWS), :] * (jnp.abs(n_x[0]) + jnp.abs(n_y[0]))
    n_z[0] = jnp.where(lane == 0, contact, n_z[0])
    return centre, n_x, n_y, n_z


def soft(normal):
    return jnp.abs(normal) + 0.2


def own_index(odd, layer, count):
    return jnp.where(odd, OUTER + count - 1 - layer, layer - OUTER)


def natural(ref, index, half, row):
    return ref[index, pl.ds(row, ROWS), half * LANES : (half + 1) * LANES]


def begin_kernel(odd_ref, fraction_in, mask_in, *refs):
    speeds_in, (*speeds, peak, state, fraction, mask, sems) = refs[:3], refs[3:]
    odd = odd_ref[0] == 1
    count, rows, width = fraction.shape
    sources = (*speeds_in, fraction_in, mask_in)
    copies = [
        pltpu.make_async_copy(source, target, sems.at[n])
        for n, (source, target) in enumerate(zip(sources, (*speeds, fraction, mask)))
    ]
    for copy in copies:
        copy.start()
    best = jnp.zeros((8, width), jnp.float32)
    for n, ref in enumerate(speeds):
        copies[n].wait()
        for i in range(count):
            best = jnp.maximum(best, jnp.max(jnp.abs(ref[i]).reshape(rows // 8, 8, width), axis=0))
    peak[...] = jnp.maximum(best[:, :LANES], best[:, LANES:])
    copies[3].wait()
    copies[4].wait()
    for k in range(count):
        index = own_index(odd, OUTER + k, count)
        for r in range(0, rows, ROWS):
            for h in HALVES:
                value = jnp.where(natural(mask, index, h, r) == 1, 1.0, natural(fraction, index, h, r))
                Layer(state, k).write(h, r, value)
        Layer(state, k).wrap()


def first_send_kernel(odd_ref, first, state, send_outer, send_inner):
    odd = odd_ref[0] == 1
    count, rows, _ = first.shape
    for k in range(OUTER):
        copy_layer(Layer(state, k), Layer(send_outer, k, False), rows)
    for k in range(INNER):
        copy_layer(Layer(state, count - 1 - k), Layer(send_inner, k, False), rows)
    near = jnp.where(odd, count - 2, 0)
    for r in range(0, rows, ROWS):
        for h in HALVES:
            Layer(send_outer, OUTER, False).write(h, r, natural(first, near, h, r))
            Layer(send_outer, OUTER + 1, False).write(h, r, natural(first, count - 1, h, r))
            Layer(send_inner, INNER, False).write(h, r, natural(first, count - 1, h, r))


def wall_kernel(where_ref, cosine, out, turned):
    odd = where_ref[0] == 1
    total = cosine.shape[0]
    layers = out.shape[0]
    count = layers - OUTER - INNER
    turned[...] = jnp.zeros(turned.shape, jnp.float32)
    for p in range(1, layers - 1):
        row = lax.rem(where_ref[1] + own_index(odd, p, count) + total, total)
        turned[pl.ds(p, 1), :] = cosine[pl.ds(row, 1), :]
    columns = jnp.transpose(turned[...])
    for p in range(1, layers - 1):
        out[p] = pltpu.roll(columns, LANES - p, 1)


KEPT = 9


def prepare_kernel(odd_ref, *refs, kinds, faces, count):
    given = dict(zip(kinds, refs))
    wall = given["wall"]
    out, field, n_s, n_a, n_b = refs[len(kinds) :]
    rows = out.shape[2]
    odd = odd_ref[0] == 1
    sign = jnp.where(odd, -1.0, 1.0)
    start, stop = faces[0], faces[-1] + 1
    lowest, highest = start - 1, stop + 1
    for kind, first_layer, way, number, is_padded in (
        ("outer", OUTER - 1, -1, OUTER, False),
        ("own", OUTER, 1, count, True),
        ("inner", OUTER + count, 1, INNER, False),
    ):
        if kind not in given:
            continue
        used = [k for k in range(number) if lowest <= first_layer + way * k <= highest]
        if used:
            fill(given[kind], field, first_layer, way, used[0], used[-1] + 1, is_padded)

    @pl.loop(start, stop + 1)
    def _(i):
        for r in range(0, rows, ROWS):
            _, n_x, n_y, n_z = normals(Layer(field, i - 1), Layer(field, i), Layer(field, i + 1), wall.at[i], r)
            for h in HALVES:
                Layer(n_s, i, False).write(h, r, n_x[h])
                Layer(n_a, i, False).write(h, r, soft(n_y[h]))
                Layer(n_b, i, False).write(h, r, soft(n_z[h]))

    speed = KEPT - 1
    for k, face in enumerate(faces):
        for r in range(0, rows, ROWS):
            for h in HALVES:
                if face == OUTER - 2:
                    value = Layer(given["outer"], OUTER, False).read(h, r)
                elif face == OUTER - 1:
                    value = natural(given["first"], count - 1, h, r)
                    value = jnp.where(odd, value, Layer(given["outer"], OUTER + 1, False).read(h, r))
                elif face == OUTER + count - 1:
                    value = natural(given["first"], count - 1, h, r)
                    value = jnp.where(odd, Layer(given["inner"], INNER, False).read(h, r), value)
                else:
                    value = natural(given["first"], jnp.where(odd, OUTER + count - 2 - face, face - OUTER), h, r)
                Layer(out, k * KEPT + speed, False).write(h, r, value * sign)

    @pl.loop(0, len(faces))
    def _(k):
        i = start + k
        for r in range(0, rows, ROWS):
            for h in HALVES:
                ahead = Layer(out, k * KEPT + speed, False).read(h, r) > 0.0

                def donor(ref, padded=False):
                    return jnp.where(ahead, Layer(ref, i, padded).read(h, r), Layer(ref, i + 1, padded).read(h, r))

                kept = prepare(donor(field, True), donor(n_s), donor(n_a), donor(n_b), ahead)
                for n, value in enumerate(kept):
                    Layer(out, k * KEPT + n, False).write(h, r, value)


def finish_faces(kept, step, flux, moved, start):
    rows = kept.shape[2]

    @pl.loop(0, kept.shape[0] // KEPT)
    def _(k):
        for r in range(0, rows, ROWS):
            for h in HALVES:
                values = [Layer(kept, k * KEPT + n, False).read(h, r) for n in range(KEPT)]
                values[-1] = values[-1] * step
                Layer(moved, start + k, False).write(h, r, values[-1])
                Layer(flux, start + k, False).write(h, r, finish(*values))


def update(target, here, inward, outward, rows):
    for r in range(0, rows, ROWS):
        for h in HALVES:
            target.write(h, r, jnp.clip(here.read(h, r) - outward.read(h, r) + inward.read(h, r), 0.0, 1.0))


def finish_kernel(peak, *refs, parts):
    kept, (state, outer, out, above, moved, step_out, send, flux) = refs[:parts], refs[parts:]
    rows = moved.shape[2]
    largest = jnp.max(peak[...])
    step = CFL_NUMBER / (jnp.full((8, LANES), largest, jnp.float32) + 1e-6)
    step_out[...] = step
    start = 0
    for ref in kept:
        finish_faces(ref, step[:1, :], flux, moved, start)
        start += ref.shape[0] // KEPT

    @pl.loop(0, state.shape[0])
    def _(k):
        update(Layer(out, k), Layer(state, k), Layer(flux, k + 1, False), Layer(flux, k + 2, False), rows)
        Layer(out, k).wrap()

    update(Layer(above, 0, False), Layer(outer, 0, False), Layer(flux, 0, False), Layer(flux, 1, False), rows)
    copy_layer(Layer(out, out.shape[0] - 1), Layer(send, 0, False), rows)


def first_fluxes(field, wall, moved, n_s, n_a, n_b, flux, start, stop):
    rows = flux.shape[2]

    @pl.loop(start, stop + 1)
    def _(i):
        for r in range(0, rows, ROWS):
            _, n_x, n_y, n_z = normals(Layer(field, i - 1), Layer(field, i), Layer(field, i + 1), wall.at[i], r)
            for h in HALVES:
                Layer(n_s, i, False).write(h, r, n_x[h])
                Layer(n_a, i, False).write(h, r, soft(n_y[h]))
                Layer(n_b, i, False).write(h, r, soft(n_z[h]))

    @pl.loop(start, stop)
    def _(i):
        for r in range(0, rows, ROWS):
            for h in HALVES:
                speed = Layer(moved, i - 1, False).read(h, r)
                ahead = speed > 0.0

                def donor(ref, padded=False):
                    return jnp.where(ahead, Layer(ref, i, padded).read(h, r), Layer(ref, i + 1, padded).read(h, r))

                through = face_flux(donor(field, True), donor(n_s), donor(n_a), donor(n_b), speed)
                Layer(flux, i - 1, False).write(h, r, through)


def inside_kernel(edge, middle, last, inner, moved, wall, out, flux_out, send, field, n_s, n_a, n_b, flux):
    rows = moved.shape[2]
    count = middle.shape[0] + 2
    fill(edge, field, OUTER, 1, 0, 1, True)
    fill(middle, field, OUTER + 1, 1, 0, count - 2, True)
    fill(last, field, OUTER + count - 1, 1, 0, 1, True)
    fill(inner, field, OUTER + count, 1, 0, INNER, False)
    first_fluxes(field, wall, moved, n_s, n_a, n_b, flux, OUTER + 1, OUTER + count)
    copy_layer(Layer(flux, OUTER, False), Layer(flux_out, 0, False), rows)

    @pl.loop(OUTER + 2, OUTER + count)
    def _(i):
        update(Layer(out, i - OUTER - 2), Layer(field, i), Layer(flux, i - 2, False), Layer(flux, i - 1, False), rows)
        Layer(out, i - OUTER - 2).wrap()

    copy_layer(Layer(out, count - 3), Layer(send, 0, False), rows)


def outside_kernel(edge, middle, last, outer, moved, wall, flux_above, above, out, field, n_s, n_a, n_b, flux):
    rows = moved.shape[2]
    count = middle.shape[0] + 2
    fill(outer, field, OUTER - 1, -1, 0, OUTER, False)
    fill(edge, field, OUTER, 1, 0, 1, True)
    fill(middle, field, OUTER + 1, 1, 0, count - 2, True)
    if count < 4:
        fill(last, field, OUTER + count - 1, 1, 0, 1, True)
    first_fluxes(field, wall, moved, n_s, n_a, n_b, flux, OUTER - 2, OUTER + 1)
    fluxes = [Layer(flux, k, False) for k in range(OUTER)] + [Layer(flux_above, 0, False)]
    for k, target in enumerate((Layer(above, 0, False), Layer(out, 0), Layer(out, 1))):
        update(target, Layer(field, OUTER - 1 + k), fluxes[k], fluxes[k + 1], rows)
        if k > 0:
            target.wrap()


def second_sweep(before, here, after, wall, speed, out, scratch):
    n_s, n_a, n_b, flux = scratch
    rows = out.ref.shape[2] - 2 * PAD
    for r in range(0, rows, ROWS):
        _, n_x, n_y, n_z = normals(before, here, after, wall, r)
        for h in HALVES:
            n_s.write(h, r, n_y[h])
            n_a.write(h, r, soft(n_x[h]))
            n_b.write(h, r, soft(n_z[h]))
    for s in (n_s, n_a, n_b):
        s.wrap()
    for r in range(0, rows, ROWS):
        for h in HALVES:
            moved = speed(h, r)
            ahead = moved > 0.0
            donor = [jnp.where(ahead, s.read(h, r), s.read(h, r + 1)) for s in (here, n_s, n_a, n_b)]
            flux.write(h, r, face_flux(*donor, moved))
    flux.wrap()
    for r in range(0, rows, ROWS):
        for h in HALVES:
            out.write(h, r, jnp.clip(here.read(h, r) - flux.read(h, r) + flux.read(h, r - 1), 0.0, 1.0))
    out.wrap()


def third_sweep(before, here, after, wall, speed, write, rows):
    for r in range(0, rows, ROWS):
        centre, n_x, n_y, n_z = normals(before, here, after, wall, r)
        fields = [centre, n_z, [soft(v) for v in n_x], [soft(v) for v in n_y]]
        above = [from_above(f) for f in fields]
        lane = lane_of(centre[0])
        through = []
        for h in HALVES:
            moved = speed(h, r)
            if h == 1:
                moved = jnp.where(lane == LANES - 1, 0.0, moved)
            ahead = moved > 0.0
            through.append(face_flux(*[jnp.where(ahead, f[h], a[h]) for f, a in zip(fields, above)], moved))
        below = from_below(through)
        for h in HALVES:
            value = jnp.clip(centre[h] - through[h] + below[h], 0.0, 1.0)
            write(h, r, value)


def gather_layers(refs, places):
    found = {}
    for ref, (start, padded) in zip(refs, places):
        for k in range(ref.shape[0]):
            found[start + k] = Layer(ref, k, padded)
    return found


def second_kernel(odd_ref, step, speed_ref, wall, *refs, places, work, send_last):
    fields, rest = refs[: len(places)], refs[len(places) :]
    out, rest = rest[0], rest[1:]
    send, rest = (rest[0], rest[1:]) if send_last is not None else (None, rest)
    scratch = [Layer(ref, 0) for ref in rest]
    layers = gather_layers(fields, places)
    odd = odd_ref[0] == 1
    count, rows, _ = speed_ref.shape
    for k, p in enumerate(work):
        index = own_index(odd, p, count)
        second_sweep(
            layers[p - 1],
            layers[p],
            layers[p + 1],
            wall.at[p],
            lambda h, r: natural(speed_ref, index, h, r) * step[:1, :],
            Layer(out, k),
            scratch,
        )
    if send is not None:
        copy_layer(Layer(out, work.index(send_last)), Layer(send, 0, False), rows)


def third_kernel(odd_ref, step, speed_ref, wall, *refs, places, work):
    fields, (out,) = refs[: len(places)], refs[len(places) :]
    layers = gather_layers(fields, places)
    odd = odd_ref[0] == 1
    count, rows, _ = speed_ref.shape
    for k, p in enumerate(work):
        index = own_index(odd, p, count)
        third_sweep(
            layers[p - 1],
            layers[p],
            layers[p + 1],
            wall.at[p],
            lambda h, r: natural(speed_ref, index, h, r) * step[:1, :],
            Layer(out, k).write,
            rows,
        )
        Layer(out, k).wrap()


def last_kernel(odd_ref, step, speed_ref, wall, *refs, places):
    fields, rest = refs[: len(places)], refs[len(places) :]
    done, (out, held_out, sems) = rest[:-3], rest[-3:]
    layers = gather_layers(fields, places)
    odd = odd_ref[0] == 1
    count, rows, _ = speed_ref.shape
    copies = []

    def send(source, layer, h):
        target = out.at[own_index(odd, layer, count), :, h * LANES : (h + 1) * LANES]
        copies.append(pltpu.make_async_copy(source, target, sems.at[len(copies)]))
        copies[-1].start()

    p = OUTER + 1
    for ref in done:
        for k in range(ref.shape[0]):
            for h in HALVES:
                send(ref.at[k, h, pl.ds(PAD, rows), :], p, h)
            p += 1

    def write(h, r, value):
        held_out[h, pl.ds(r, ROWS), :] = value

    index = own_index(odd, OUTER, count)
    third_sweep(
        layers[OUTER - 1],
        layers[OUTER],
        layers[OUTER + 1],
        wall.at[OUTER],
        lambda h, r: natural(speed_ref, index, h, r) * step[:1, :],
        write,
        rows,
    )
    for h in HALVES:
        send(held_out.at[h], OUTER, h)
    for copy in copies:
        copy.wait()


IN_VMEM = pl.BlockSpec(memory_space=pltpu.VMEM)
IN_SMEM = pl.BlockSpec(memory_space=pltpu.SMEM)


def held(shape):
    return pltpu.VMEM(shape, jnp.float32)


def call(kernel, name, outs, scalars, arrays, scratch=(), faces=0.1, resident=True):
    space = pltpu.VMEM if resident else pltpu.HBM
    arrays = [pltpu.with_memory_space_constraint(a, space) for a in arrays]
    work = int(faces * 1.1e9)
    return pl.pallas_call(
        kernel,
        out_shape=outs,
        in_specs=[IN_SMEM] * len(scalars) + [pl.BlockSpec(memory_space=space)] * len(arrays),
        out_specs=[IN_VMEM] * len(outs),
        scratch_shapes=list(scratch),
        compiler_params=pltpu.CompilerParams(vmem_limit_bytes=VMEM_LIMIT),
        cost_estimate=pl.CostEstimate(flops=work, bytes_accessed=1024, transcendentals=0),
        name=name,
    )(*scalars, *arrays)


def swap(array, outer):
    count = lax.axis_size("gx")
    if outer:
        pairs = [(i, (i + 1) % count if i % 2 else (i - 1) % count) for i in range(count)]
    else:
        pairs = [(i, i ^ 1) for i in range(count)]
    return lax.ppermute(array, "gx", pairs)


def largest_round(array, reach, beside):
    count = lax.axis_size("gx")
    if count & (count - 1) == 0:
        pairs = [(i, i ^ reach) for i in range(count)]
    else:
        pairs = [(i, (i + reach) % count) for i in range(count)]
    received = lax.ppermute(array, "gx", pairs)
    if beside:
        received, *_ = lax.optimization_barrier((received, *beside))
    return jnp.maximum(array, received)


def shards(fraction, first, second, third, wall_class, seed_mask):
    count, rows, width = fraction.shape
    layers = OUTER + count + INNER
    own_end = OUTER + count
    device = lax.axis_index("gx")
    odd = (device % 2).astype(jnp.int32).reshape(1)
    place = jnp.stack([device % 2, device * count]).astype(jnp.int32)

    def padded(n):
        return (n, 2, rows + 2 * PAD, LANES)

    def plain(n):
        return (n, 2, rows, LANES)

    natural_shape = (count, rows, width)
    first, second, third, peak, state = call(
        begin_kernel,
        "begin",
        [held(natural_shape)] * 3
        + [held((8, LANES)), held(padded(count))],
        [odd],
        [fraction, seed_mask, first, second, third],
        [
            pltpu.VMEM(natural_shape, jnp.float32),
            pltpu.VMEM(natural_shape, jnp.int32),
            pltpu.SemaphoreType.DMA((5,)),
        ],
        resident=False,
    )
    send_outer, send_inner = call(
        first_send_kernel, "first_send", [held(plain(OUTER + 2)), held(plain(INNER + 1))], [odd], [first, state]
    )
    inner = swap(send_inner, False)
    cosine = jnp.cos(jnp.pi * (wall_class.astype(jnp.float32) + 1.0) / (WALL_CLASSES + 1))
    (wall,) = call(wall_kernel, "wall", [held((layers, rows, LANES))], [place], [cosine], [pltpu.VMEM((LANES, rows), jnp.float32)])
    slopes = [pltpu.VMEM(padded(layers), jnp.float32)] + [pltpu.VMEM(plain(layers), jnp.float32)] * 3

    def prepare_call(faces, **given):
        return call(
            functools.partial(prepare_kernel, kinds=tuple(given), faces=faces, count=count),
            "prepare",
            [held(plain(KEPT * len(faces)))],
            [odd],
            list(given.values()),
            slopes,
            faces=len(faces),
        )[0]

    size = lax.axis_size("gx")
    prepare_inside = functools.partial(prepare_call, wall=wall, first=first, own=state, inner=inner)
    outer = swap(send_outer, True)
    peak = largest_round(peak, 1, [])
    kept = [prepare_inside(tuple(range(OUTER + 2, own_end)))]
    peak = largest_round(peak, 8, kept)
    kept.insert(0, prepare_inside((OUTER + 1,)))
    kept.insert(0, prepare_call((OUTER - 2, OUTER - 1, OUTER), wall=wall, first=first, own=state, outer=outer))
    peak = largest_round(peak, 4, [kept[1]])
    peak = largest_round(peak, 2, [kept[0]])
    own, above, moved, step, send_inner = call(
        functools.partial(finish_kernel, parts=len(kept)),
        "finish",
        [held(padded(count)), held(plain(1)), held(plain(count + 2)), held((8, LANES)), held(plain(1))],
        [],
        [peak, *kept, state, outer],
        [pltpu.VMEM(plain(count + 2), jnp.float32)],
        faces=1,
    )
    swept, places = [above, own], [(OUTER - 1, False), (OUTER, True)]
    line = [pltpu.VMEM(padded(1), jnp.float32)] * 4
    for turn in range(STEPS):
        final = turn == STEPS - 1
        if turn > 0:
            flux = pltpu.VMEM(plain(count + 2), jnp.float32)
            inside, flux_low, send_inner = call(
                inside_kernel,
                "inside",
                [held(padded(count - 2)), held(plain(1)), held(plain(1))],
                [],
                [*own, inner, moved, wall],
                [*slopes, flux],
                faces=count - 1,
            )
            above, outside = call(
                outside_kernel,
                "outside",
                [held(plain(1)), held(padded(2))],
                [],
                [*own, outer, moved, wall, flux_low],
                [*slopes, flux],
                faces=3,
            )
            swept = [above, outside, inside]
            places = [(OUTER - 1, False), (OUTER, True), (OUTER + 2, True)]
        inner = swap(send_inner, False)

        def second_call(work, fields, places, send):
            return call(
                functools.partial(second_kernel, places=places, work=work, send_last=work[0] if send else None),
                "second",
                [held(padded(len(work)))] + ([held(plain(1))] if send else []),
                [odd],
                [step, second, wall, *fields],
                line,
                faces=len(work),
            )

        last, send_inner = second_call((own_end - 1,), [swept[-1], inner], [places[-1], (own_end, False)], True)
        inner = swap(send_inner, False)
        edge, send_outer = second_call((OUTER,), swept[:2], places[:2], True)
        after = lax.optimization_barrier((edge, *swept[1:]))[1:]
        (middle,) = second_call(tuple(range(OUTER + 1, own_end - 1)), after, places[1:], False)
        outer = swap(send_outer, True)

        fields = [edge, middle, last, inner]
        starts = [(OUTER, True), (OUTER + 1, True), (own_end - 1, True), (own_end, False)]
        inside_work = tuple(range(OUTER + 1, own_end))
        edge_fields, edge_starts = [outer, edge, middle], [(OUTER - 1, False), (OUTER, True), (OUTER + 1, True)]
        def third_call(work, fields, places):
            return call(
                functools.partial(third_kernel, places=places, work=work),
                "third",
                [held(padded(len(work)))],
                [odd],
                [step, third, wall, *fields],
                faces=len(work),
            )[0]

        middle_new = third_call(inside_work[:-1], fields[:-1], starts[:-1])
        last_new = third_call(inside_work[-1:], fields[1:], starts[1:])
        if final:
            return last_call(odd, step, third, wall, edge_fields, edge_starts, [middle_new, last_new], natural_shape)
        edge_new = third_call((OUTER,), edge_fields, edge_starts)
        own = [edge_new, middle_new, last_new]
        send_outer, send_inner = call(pack_kernel, "pack", [held(plain(OUTER)), held(plain(INNER))], [], own)
        outer = swap(send_outer, True)
        inner = swap(send_inner, False)


def last_call(odd, step, speed, wall, fields, places, done, shape):
    arrays = [pltpu.with_memory_space_constraint(a, pltpu.VMEM) for a in (step, speed, wall, *fields, *done)]
    return pl.pallas_call(
        functools.partial(last_kernel, places=places),
        out_shape=jax.ShapeDtypeStruct(shape, jnp.float32),
        in_specs=[IN_SMEM] + [IN_VMEM] * len(arrays),
        out_specs=pl.BlockSpec(memory_space=pltpu.HBM),
        scratch_shapes=[pltpu.VMEM((2, *shape[1:2], LANES), jnp.float32), pltpu.SemaphoreType.DMA((2 * shape[0],))],
        compiler_params=pltpu.CompilerParams(vmem_limit_bytes=VMEM_LIMIT),
        cost_estimate=pl.CostEstimate(flops=int(1.1e9), bytes_accessed=1024, transcendentals=0),
        name="last",
    )(odd, *arrays)


def pack_kernel(edge, middle, last, send_outer, send_inner):
    rows = send_outer.shape[2]
    own = [Layer(ref, k) for ref in (edge, middle, last) for k in range(ref.shape[0])]
    for k in range(OUTER):
        copy_layer(own[k], Layer(send_outer, k, False), rows)
    for k in range(INNER):
        copy_layer(own[-1 - k], Layer(send_inner, k, False), rows)


def solution(mesh):
    split = P(("ens", "gx"), None, None)
    return jax.shard_map(
        shards, mesh=mesh, in_specs=(split, split, split, split, P(), split), out_specs=split, check_vma=False
    )
```

```python
import functools

import jax
import jax.numpy as jnp
from jax import lax
from jax.experimental import pallas as pl
from jax.experimental.pallas import tpu as pltpu
from jax.sharding import PartitionSpec as P

STEPS = 2
NEWTON = 4
WALL_CLASSES = 4
CFL_NUMBER = 0.45

LANES = 128
PAD = 8
ROWS = 32
HALVES = (0, 1)
OUTER = 3
INNER = 2
VMEM_LIMIT = 24 * 1024 * 1024
SEND_ROUND = 2


def cube(t):
    t = jnp.maximum(t, 0.0)
    return t * t * t


def square(t):
    t = jnp.maximum(t, 0.0)
    return t * t


def rcp(x):
    return pl.reciprocal(x, approx=True)


def plane(donor, span, soft_a, soft_b):
    low = jnp.minimum(soft_a, soft_b)
    high = jnp.maximum(soft_a, soft_b)
    pair = soft_a + soft_b
    half = 0.5 * (span + pair)
    top = jnp.maximum(span, high)
    mid = jnp.minimum(span, high)
    over = half - top
    last = half - jnp.abs(over)
    sign = jnp.where(over > 0.0, -1.0, 1.0)
    flat = low * mid
    bulk = flat * top
    share = jnp.clip(jnp.minimum(donor, 1.0 - donor), 0.0, 0.5)
    goal = bulk * share
    at = half - (0.25 * bulk - 0.5 * goal) * rcp(flat - square(over))
    low_6 = low * (1.0 / 6.0)
    mid_6 = mid * (1.0 / 6.0)
    last_6 = last * (1.0 / 6.0)
    for _ in range(NEWTON - 1):
        by_low = square(at - low)
        by_mid = square(at - mid)
        by_last = sign * square(at - last)
        growth = at * at - by_low - by_mid + by_last
        shift = goal - low_6 * by_low - mid_6 * by_mid + last_6 * by_last
        at = (5.0 / 6.0) * at + shift * rcp(growth)
    return at, low, high, pair, half, bulk


def edge_sum(at, low):
    return cube(at) - cube(at - low)


def side_sum(at, low, high, pair):
    return cube(at) - cube(at - low) - cube(at - high) + cube(at - pair)


def prepare(donor, along, soft_a, soft_b, ahead):
    span = jnp.abs(along) + 0.2
    at, low, high, pair, half, bulk = plane(donor, span, soft_a, soft_b)
    light = donor <= 0.5
    sense = jnp.where(jnp.logical_xor(light, ahead), -1.0, 1.0)
    weight = jnp.clip(0.5 + (along * sense) * rcp(half), 0.0, 1.0)
    whole = side_sum(at, low, high, pair)
    whole = whole - weight * (whole + edge_sum(at - span, low))
    scale = sense * rcp(6.0 * bulk)
    heavy = jnp.where(light, 0.0, 1.0)
    return at, span, low, high, weight, scale, whole, heavy


def finish(at, span, low, high, weight, scale, whole, heavy, moved):
    slab = jnp.abs(moved) * span
    rest = side_sum(at - slab, low, high, low + high)
    near = edge_sum(at - span + slab, low)
    return (whole - rest + weight * (rest + near)) * scale + heavy * moved


def face_flux(donor, along, soft_a, soft_b, moved):
    return finish(*prepare(donor, along, soft_a, soft_b, moved > 0.0), moved)


def lane_of(value):
    return lax.broadcasted_iota(jnp.int32, value.shape, 1)


def from_above(pair):
    turned = [pltpu.roll(v, LANES - 1, 1) for v in pair]
    return [jnp.where(lane_of(pair[0]) == LANES - 1, turned[1], turned[0]), turned[1]]


def from_below(pair):
    turned = [pltpu.roll(v, 1, 1) for v in pair]
    first = lane_of(pair[0]) == 0
    return [jnp.where(first, turned[1], turned[0]), jnp.where(first, turned[0], turned[1])]


class Layer:
    def __init__(self, ref, index, padded=True):
        self.ref, self.index, self.pad = ref, index, PAD if padded else 0

    def read(self, half, row):
        return self.ref[self.index, half, pl.ds(self.pad + row, ROWS), :]

    def write(self, half, row, value):
        self.ref[self.index, half, pl.ds(self.pad + row, ROWS), :] = value

    def wrap(self):
        rows = self.ref.shape[2] - 2 * PAD
        for h in HALVES:
            self.ref[self.index, h, pl.ds(0, PAD), :] = self.ref[self.index, h, pl.ds(rows, PAD), :]
            self.ref[self.index, h, pl.ds(PAD + rows, PAD), :] = self.ref[self.index, h, pl.ds(PAD, PAD), :]


def copy_layer(source, target, rows):
    for r in range(0, rows, ROWS):
        for h in HALVES:
            target.write(h, r, source.read(h, r))


def padded_halo(source, field, numbers):
    found = {}
    for k, p in numbers:
        found[p] = Layer(field, p)
        copy_layer(Layer(source, k, False), found[p], field.shape[2] - 2 * PAD)
        found[p].wrap()
    return found


def normals(before, here, after, wall, row):
    centre = [here.read(h, row) for h in HALVES]
    n_x = [before.read(h, row) - after.read(h, row) for h in HALVES]
    n_y = [here.read(h, row - 1) - here.read(h, row + 1) for h in HALVES]
    lane = lane_of(centre[0])
    up = [pltpu.roll(v, LANES - 1, 1) for v in centre]
    down = [pltpu.roll(v, 1, 1) for v in centre]
    top, bottom = lane == LANES - 1, lane == 0
    n_z = [down[0] - jnp.where(top, up[1], up[0]), jnp.where(bottom, down[0], down[1]) - jnp.where(top, centre[1], up[1])]
    contact = wall[pl.ds(row, ROWS), :] * (jnp.abs(n_x[0]) + jnp.abs(n_y[0]))
    n_z[0] = jnp.where(bottom, contact, n_z[0])
    return centre, n_x, n_y, n_z


def soft(normal):
    return jnp.abs(normal) + 0.2


def own_index(odd, layer, count):
    return jnp.where(odd, OUTER + count - 1 - layer, layer - OUTER)


def natural(ref, index, half, row):
    return ref[index, pl.ds(row, ROWS), half * LANES : (half + 1) * LANES]


def begin_kernel(odd_ref, fraction_in, mask_in, class_in, *refs):
    speeds_in, (*speeds, peak, state, classes, fraction, mask, sems) = refs[:3], refs[3:]
    odd = odd_ref[0] == 1
    count, rows, width = fraction.shape
    sources = (*speeds_in, fraction_in, mask_in, class_in)
    copies = [
        pltpu.make_async_copy(source, target, sems.at[n])
        for n, (source, target) in enumerate(zip(sources, (*speeds, fraction, mask, classes)))
    ]
    for copy in copies:
        copy.start()
    best = jnp.zeros((8, width), jnp.float32)
    for n, ref in enumerate(speeds):
        copies[n].wait()
        for i in range(count):
            best = jnp.maximum(best, jnp.max(jnp.abs(ref[i]).reshape(rows // 8, 8, width), axis=0))
    peak[...] = jnp.maximum(best[:, :LANES], best[:, LANES:])
    copies[3].wait()
    copies[4].wait()
    for k in range(count):
        index = own_index(odd, OUTER + k, count)
        for r in range(0, rows, ROWS):
            for h in HALVES:
                value = jnp.where(natural(mask, index, h, r) == 1, 1.0, natural(fraction, index, h, r))
                Layer(state, k).write(h, r, value)
        Layer(state, k).wrap()
    copies[5].wait()


def first_send_kernel(odd_ref, first, state, send_outer, send_inner):
    odd = odd_ref[0] == 1
    count, rows, _ = first.shape
    for k in range(OUTER):
        copy_layer(Layer(state, k), Layer(send_outer, k, False), rows)
    for k in range(INNER):
        copy_layer(Layer(state, count - 1 - k), Layer(send_inner, k, False), rows)
    near = jnp.where(odd, count - 2, 0)
    for r in range(0, rows, ROWS):
        for h in HALVES:
            Layer(send_outer, OUTER, False).write(h, r, natural(first, near, h, r))
            Layer(send_outer, OUTER + 1, False).write(h, r, natural(first, count - 1, h, r))
            Layer(send_inner, INNER, False).write(h, r, natural(first, count - 1, h, r))


def wall_kernel(classes, out, turned):
    device = lax.axis_index("gx")
    odd = lax.rem(device, 2) == 1
    total = classes.shape[0]
    layers = out.shape[0]
    count = layers - OUTER - INNER
    turned[...] = jnp.zeros(turned.shape, jnp.float32)
    for p in range(1, layers - 1):
        row = lax.rem(device * count + own_index(odd, p, count) + total, total)
        turned[pl.ds(p, 1), :] = classes[pl.ds(row, 1), :].astype(jnp.float32)
    used = -(-layers // 8) * 8
    turned[:used, :] = jnp.cos(jnp.pi * (turned[:used, :] + 1.0) / (WALL_CLASSES + 1))
    columns = jnp.transpose(turned[...])
    for p in range(1, layers - 1):
        out[p] = pltpu.roll(columns, LANES - p, 1)


KEPT = 9


def face_work(layers, wall, slopes, faces, rows, work):
    n_s, n_a, n_b = slopes

    def slope(i):
        for r in range(0, rows, ROWS):
            _, n_x, n_y, n_z = normals(layers[i - 1], layers[i], layers[i + 1], wall.at[i], r)
            for h in HALVES:
                Layer(n_s, i, False).write(h, r, n_x[h])
                Layer(n_a, i, False).write(h, r, soft(n_y[h]))
                Layer(n_b, i, False).write(h, r, soft(n_z[h]))

    slope(faces[0])
    for i in faces:
        slope(i + 1)
        sides = [(layers[i], layers[i + 1])] + [(Layer(n, i, False), Layer(n, i + 1, False)) for n in slopes]
        for r in range(0, rows, ROWS):
            for h in HALVES:

                def donor(ahead):
                    return [jnp.where(ahead, low.read(h, r), high.read(h, r)) for low, high in sides]

                work(i, h, r, donor)


def prepare_kernel(odd_ref, *refs, kinds, faces, count):
    given = dict(zip(kinds, refs))
    out, field, *slopes = refs[len(kinds) :]
    rows = out.shape[2]
    odd = odd_ref[0] == 1
    sign = jnp.where(odd, -1.0, 1.0)
    layers = {OUTER + k: Layer(given["own"], k) for k in range(count)}
    needed = range(faces[0] - 1, faces[-1] + 3)
    for kind, first_layer, way, number in (("outer", OUTER - 1, -1, OUTER), ("inner", OUTER + count, 1, INNER)):
        if kind in given:
            numbers = [(k, first_layer + way * k) for k in range(number) if first_layer + way * k in needed]
            layers.update(padded_halo(given[kind], field, numbers))

    def work(face, h, r, donor):
        if face == OUTER - 2:
            speed = Layer(given["outer"], OUTER, False).read(h, r)
        elif face == OUTER - 1:
            speed = natural(given["first"], count - 1, h, r)
            speed = jnp.where(odd, speed, Layer(given["outer"], OUTER + 1, False).read(h, r))
        elif face == OUTER + count - 1:
            speed = natural(given["first"], count - 1, h, r)
            speed = jnp.where(odd, Layer(given["inner"], INNER, False).read(h, r), speed)
        else:
            speed = natural(given["first"], jnp.where(odd, OUTER + count - 2 - face, face - OUTER), h, r)
        speed = speed * sign
        ahead = speed > 0.0
        first_kept = (face - faces[0]) * KEPT
        for n, value in enumerate((*prepare(*donor(ahead), ahead), speed)):
            Layer(out, first_kept + n, False).write(h, r, value)

    face_work(layers, given["wall"], slopes, faces, rows, work)


def finish_faces(kept, step, flux, moved, start):
    rows = kept.shape[2]

    @pl.loop(0, kept.shape[0] // KEPT)
    def _(k):
        for r in range(0, rows, ROWS):
            for h in HALVES:
                values = [Layer(kept, k * KEPT + n, False).read(h, r) for n in range(KEPT)]
                values[-1] = values[-1] * step
                Layer(moved, start + k, False).write(h, r, values[-1])
                Layer(flux, start + k, False).write(h, r, finish(*values))


def update(target, here, inward, outward, rows):
    for r in range(0, rows, ROWS):
        for h in HALVES:
            target.write(h, r, jnp.clip(here.read(h, r) - outward.read(h, r) + inward.read(h, r), 0.0, 1.0))


def finish_kernel(peak, *refs, parts):
    kept, (state, outer, out, above, moved, step_out, send, flux) = refs[:parts], refs[parts:]
    rows = moved.shape[2]
    largest = jnp.max(peak[...])
    step = CFL_NUMBER / (jnp.full((8, LANES), largest, jnp.float32) + 1e-6)
    step_out[...] = step
    start = 0
    for ref in kept:
        finish_faces(ref, step[:1, :], flux, moved, start)
        start += ref.shape[0] // KEPT

    @pl.loop(0, state.shape[0])
    def _(k):
        update(Layer(out, k), Layer(state, k), Layer(flux, k + 1, False), Layer(flux, k + 2, False), rows)
        Layer(out, k).wrap()

    update(Layer(above, 0, False), Layer(outer, 0, False), Layer(flux, 0, False), Layer(flux, 1, False), rows)
    copy_layer(Layer(out, out.shape[0] - 1), Layer(send, 0, False), rows)


def first_fluxes(layers, wall, moved, slopes, flux, faces):
    def work(i, h, r, donor):
        speed = Layer(moved, i - 1, False).read(h, r)
        Layer(flux, i - 1, False).write(h, r, face_flux(*donor(speed > 0.0), speed))

    face_work(layers, wall, slopes, faces, flux.shape[2], work)


def own_layers(*refs):
    found = [Layer(ref, k) for ref in refs for k in range(ref.shape[0])]
    return {OUTER + k: layer for k, layer in enumerate(found)}


def inside_kernel(edge, middle, last, inner, moved, wall, out, flux_out, send, field, *more):
    *slopes, flux = more
    rows = moved.shape[2]
    layers = own_layers(edge, middle, last)
    count = len(layers)
    layers.update(padded_halo(inner, field, [(k, OUTER + count + k) for k in range(INNER)]))
    first_fluxes(layers, wall, moved, slopes, flux, range(OUTER + 1, OUTER + count))
    copy_layer(Layer(flux, OUTER, False), Layer(flux_out, 0, False), rows)
    for i in range(OUTER + 2, OUTER + count):
        target = Layer(out, i - OUTER - 2)
        update(target, layers[i], Layer(flux, i - 2, False), Layer(flux, i - 1, False), rows)
        target.wrap()
    copy_layer(Layer(out, count - 3), Layer(send, 0, False), rows)


def outside_kernel(edge, middle, last, outer, moved, wall, flux_above, above, out, field, *more):
    *slopes, flux = more
    rows = moved.shape[2]
    layers = own_layers(edge, middle, last)
    layers.update(padded_halo(outer, field, [(k, OUTER - 1 - k) for k in range(OUTER)]))
    first_fluxes(layers, wall, moved, slopes, flux, range(OUTER - 2, OUTER + 1))
    fluxes = [Layer(flux, k, False) for k in range(OUTER)] + [Layer(flux_above, 0, False)]
    for k, target in enumerate((Layer(above, 0, False), Layer(out, 0), Layer(out, 1))):
        update(target, layers[OUTER - 1 + k], fluxes[k], fluxes[k + 1], rows)
        if k > 0:
            target.wrap()


def second_sweep(before, here, after, wall, speed, out, scratch):
    n_s, n_a, n_b, flux = scratch
    rows = out.ref.shape[2] - 2 * PAD
    for r in range(0, rows, ROWS):
        _, n_x, n_y, n_z = normals(before, here, after, wall, r)
        for h in HALVES:
            n_s.write(h, r, n_y[h])
            n_a.write(h, r, soft(n_x[h]))
            n_b.write(h, r, soft(n_z[h]))
    for s in (n_s, n_a, n_b):
        s.wrap()
    for r in range(0, rows, ROWS):
        for h in HALVES:
            moved = speed(h, r)
            ahead = moved > 0.0
            donor = [jnp.where(ahead, s.read(h, r), s.read(h, r + 1)) for s in (here, n_s, n_a, n_b)]
            flux.write(h, r, face_flux(*donor, moved))
    flux.wrap()
    for r in range(0, rows, ROWS):
        for h in HALVES:
            out.write(h, r, jnp.clip(here.read(h, r) - flux.read(h, r) + flux.read(h, r - 1), 0.0, 1.0))
    out.wrap()


def third_sweep(before, here, after, wall, speed, write, rows):
    for r in range(0, rows, ROWS):
        centre, n_x, n_y, n_z = normals(before, here, after, wall, r)
        fields = [centre, n_z, [soft(v) for v in n_x], [soft(v) for v in n_y]]
        above = [from_above(f) for f in fields]
        lane = lane_of(centre[0])
        through = []
        for h in HALVES:
            moved = speed(h, r)
            ahead = moved > 0.0
            through.append(face_flux(*[jnp.where(ahead, f[h], a[h]) for f, a in zip(fields, above)], moved))
        through[1] = jnp.where(lane == LANES - 1, 0.0, through[1])
        below = from_below(through)
        for h in HALVES:
            value = jnp.clip(centre[h] - through[h] + below[h], 0.0, 1.0)
            write(h, r, value)


def gather_layers(refs, places):
    found = {}
    for ref, (start, padded) in zip(refs, places):
        for k in range(ref.shape[0]):
            found[start + k] = Layer(ref, k, padded)
    return found


def second_kernel(odd_ref, step, speed_ref, wall, *refs, places, work, send_last):
    fields, rest = refs[: len(places)], refs[len(places) :]
    out, rest = rest[0], rest[1:]
    send, rest = (rest[0], rest[1:]) if send_last is not None else (None, rest)
    scratch = [Layer(ref, 0) for ref in rest]
    layers = gather_layers(fields, places)
    odd = odd_ref[0] == 1
    count, rows, _ = speed_ref.shape
    for k, p in enumerate(work):
        index = own_index(odd, p, count)
        second_sweep(
            layers[p - 1],
            layers[p],
            layers[p + 1],
            wall.at[p],
            lambda h, r: natural(speed_ref, index, h, r) * step[:1, :],
            Layer(out, k),
            scratch,
        )
    if send is not None:
        copy_layer(Layer(out, work.index(send_last)), Layer(send, 0, False), rows)


def third_kernel(odd_ref, step, speed_ref, wall, *refs, places, work):
    fields, (out,) = refs[: len(places)], refs[len(places) :]
    layers = gather_layers(fields, places)
    odd = odd_ref[0] == 1
    count, rows, _ = speed_ref.shape
    for k, p in enumerate(work):
        index = own_index(odd, p, count)
        third_sweep(
            layers[p - 1],
            layers[p],
            layers[p + 1],
            wall.at[p],
            lambda h, r: natural(speed_ref, index, h, r) * step[:1, :],
            Layer(out, k).write,
            rows,
        )
        Layer(out, k).wrap()


def last_kernel(odd_ref, step, speed_ref, wall, *refs, places):
    fields, rest = refs[: len(places)], refs[len(places) :]
    done, (out, held_out, sems) = rest[:-3], rest[-3:]
    layers = gather_layers(fields, places)
    odd = odd_ref[0] == 1
    count, rows, _ = speed_ref.shape
    copies = []

    def send(source, layer, h):
        target = out.at[own_index(odd, layer, count), :, h * LANES : (h + 1) * LANES]
        copies.append(pltpu.make_async_copy(source, target, sems.at[len(copies)]))
        copies[-1].start()

    p = OUTER + 1
    for ref in done:
        for k in range(ref.shape[0]):
            for h in HALVES:
                send(ref.at[k, h, pl.ds(PAD, rows), :], p, h)
            p += 1

    def write(h, r, value):
        held_out[h, pl.ds(r, ROWS), :] = value

    index = own_index(odd, OUTER, count)
    third_sweep(
        layers[OUTER - 1],
        layers[OUTER],
        layers[OUTER + 1],
        wall.at[OUTER],
        lambda h, r: natural(speed_ref, index, h, r) * step[:1, :],
        write,
        rows,
    )
    for h in HALVES:
        send(held_out.at[h], OUTER, h)
    for copy in copies:
        copy.wait()


IN_VMEM = pl.BlockSpec(memory_space=pltpu.VMEM)
IN_SMEM = pl.BlockSpec(memory_space=pltpu.SMEM)


def held(shape):
    return pltpu.VMEM(shape, jnp.float32)


def call(kernel, name, outs, scalars, arrays, scratch=(), faces=0.1, resident=True):
    space = pltpu.VMEM if resident else pltpu.HBM
    arrays = [pltpu.with_memory_space_constraint(a, space) for a in arrays]
    work = int(faces * 1.1e9)
    return pl.pallas_call(
        kernel,
        out_shape=outs,
        in_specs=[IN_SMEM] * len(scalars) + [pl.BlockSpec(memory_space=space)] * len(arrays),
        out_specs=[IN_VMEM] * len(outs),
        scratch_shapes=list(scratch),
        compiler_params=pltpu.CompilerParams(vmem_limit_bytes=VMEM_LIMIT),
        cost_estimate=pl.CostEstimate(flops=work, bytes_accessed=1024, transcendentals=0),
        name=name,
    )(*scalars, *arrays)


def swap(array, outer):
    count = lax.axis_size("gx")
    if outer:
        pairs = [(i, (i + 1) % count if i % 2 else (i - 1) % count) for i in range(count)]
    else:
        pairs = [(i, i ^ 1) for i in range(count)]
    return lax.ppermute(array, "gx", pairs)


def largest_round(array, reach, beside):
    count = lax.axis_size("gx")
    if count & (count - 1) == 0:
        pairs = [(i, i ^ reach) for i in range(count)]
    else:
        pairs = [(i, (i + reach) % count) for i in range(count)]
    received = lax.ppermute(array, "gx", pairs)
    if beside:
        received, *_ = lax.optimization_barrier((received, *beside))
    return jnp.maximum(array, received)


def shards(fraction, first, second, third, wall_class, seed_mask):
    count, rows, width = fraction.shape
    layers = OUTER + count + INNER
    own_end = OUTER + count
    device = lax.axis_index("gx")
    odd = (device % 2).astype(jnp.int32).reshape(1)

    def padded(n):
        return (n, 2, rows + 2 * PAD, LANES)

    def plain(n):
        return (n, 2, rows, LANES)

    natural_shape = (count, rows, width)
    first, second, third, peak, state, classes = call(
        begin_kernel,
        "begin",
        [held(natural_shape)] * 3
        + [held((8, LANES)), held(padded(count)), pltpu.VMEM(wall_class.shape, jnp.int32)],
        [odd],
        [fraction, seed_mask, wall_class, first, second, third],
        [
            pltpu.VMEM(natural_shape, jnp.float32),
            pltpu.VMEM(natural_shape, jnp.int32),
            pltpu.SemaphoreType.DMA((6,)),
        ],
        resident=False,
    )
    send_outer, send_inner = call(
        first_send_kernel, "first_send", [held(plain(OUTER + 2)), held(plain(INNER + 1))], [odd], [first, state]
    )
    inner = swap(send_inner, False)
    (wall,) = call(
        wall_kernel, "wall", [held((layers, rows, LANES))], [], [classes], [pltpu.VMEM((LANES, rows), jnp.float32)]
    )
    slopes = [pltpu.VMEM(padded(layers), jnp.float32)] + [pltpu.VMEM(plain(layers), jnp.float32)] * 3

    def prepare_call(faces, **given):
        return call(
            functools.partial(prepare_kernel, kinds=tuple(given), faces=faces, count=count),
            "prepare",
            [held(plain(KEPT * len(faces)))],
            [odd],
            list(given.values()),
            slopes,
            faces=0.02,
        )[0]

    size = lax.axis_size("gx")
    prepare_inside = functools.partial(prepare_call, wall=wall, first=first, own=state, inner=inner)
    outer = swap(send_outer, True)
    peak = largest_round(peak, 1, [])
    kept = [prepare_inside(tuple(range(OUTER + 2, own_end)))]
    peak = largest_round(peak, 8, kept)
    kept.insert(0, prepare_inside((OUTER + 1,)))
    kept.insert(0, prepare_call((OUTER - 2, OUTER - 1, OUTER), wall=wall, first=first, own=state, outer=outer))
    peak = largest_round(peak, 4, [kept[1]])
    peak = largest_round(peak, 2, [kept[0]])
    own, above, moved, step, send_inner = call(
        functools.partial(finish_kernel, parts=len(kept)),
        "finish",
        [held(padded(count)), held(plain(1)), held(plain(count + 2)), held((8, LANES)), held(plain(1))],
        [],
        [peak, *kept, state, outer],
        [pltpu.VMEM(plain(count + 2), jnp.float32)],
        faces=1,
    )
    swept, places = [above, own], [(OUTER - 1, False), (OUTER, True)]
    line = [pltpu.VMEM(padded(1), jnp.float32)] * 4
    def second_call(work, fields, places, send):
        return call(
            functools.partial(second_kernel, places=places, work=work, send_last=work[0] if send else None),
            "second",
            [held(padded(len(work)))] + ([held(plain(1))] if send else []),
            [odd],
            [step, second, wall, *fields],
            line,
            faces=0.1 if own_end - 1 in work else len(work),
        )

    def last_second(part, place, send_inner):
        inner = swap(send_inner, False)
        last, send_inner = second_call((own_end - 1,), [part, inner], [place, (own_end, False)], True)
        return last, swap(send_inner, False)

    for turn in range(STEPS):
        final = turn == STEPS - 1
        if turn > 0:
            flux = pltpu.VMEM(plain(count + 2), jnp.float32)
            inside, flux_low, send_inner = call(
                inside_kernel,
                "inside",
                [held(padded(count - 2)), held(plain(1)), held(plain(1))],
                [],
                [*own, inner, moved, wall],
                [*slopes, flux],
                faces=0.1,
            )
            last, inner = last_second(inside, (OUTER + 2, True), send_inner)
            outer, last = lax.optimization_barrier((outer, last))
            above, outside = call(
                outside_kernel,
                "outside",
                [held(plain(1)), held(padded(2))],
                [],
                [*own, outer, moved, wall, flux_low],
                [*slopes, flux],
                faces=3,
            )
            swept = [above, outside, inside]
            places = [(OUTER - 1, False), (OUTER, True), (OUTER + 2, True)]
        else:
            last, inner = last_second(swept[-1], places[-1], send_inner)
        edge, send_outer = second_call((OUTER,), swept[:2], places[:2], True)
        after = lax.optimization_barrier((edge, *swept[1:]))[1:]
        (middle,) = second_call(tuple(range(OUTER + 1, own_end - 1)), after, places[1:], False)
        outer = swap(send_outer, True)

        fields = [edge, middle, last, inner]
        starts = [(OUTER, True), (OUTER + 1, True), (own_end - 1, True), (own_end, False)]
        inside_work = tuple(range(OUTER + 1, own_end))
        edge_fields, edge_starts = [outer, edge, middle], [(OUTER - 1, False), (OUTER, True), (OUTER + 1, True)]
        def third_call(work, fields, places):
            return call(
                functools.partial(third_kernel, places=places, work=work),
                "third",
                [held(padded(len(work)))],
                [odd],
                [step, third, wall, *fields],
                faces=len(work),
            )[0]

        middle_new = third_call(inside_work[:-1], fields[:-1], starts[:-1])
        if final:
            last_new = third_call(inside_work[-1:], fields[1:], starts[1:])
            return last_call(odd, step, third, wall, edge_fields, edge_starts, [middle_new, last_new], natural_shape)
        edge_new = third_call((OUTER,), edge_fields, edge_starts)
        (send_outer,) = call(pack_kernel, "pack", [held(plain(OUTER))], [], [edge_new, middle_new])
        outer = swap(send_outer, True)
        _, *after = lax.optimization_barrier((send_outer, *fields[1:]))
        last_new = third_call(inside_work[-1:], after, starts[1:])
        own = [edge_new, middle_new, last_new]
        (send_inner,) = call(pack_kernel, "pack", [held(plain(INNER))], [], [last_new, middle_new])
        inner = swap(send_inner, False)


def last_call(odd, step, speed, wall, fields, places, done, shape):
    arrays = [pltpu.with_memory_space_constraint(a, pltpu.VMEM) for a in (step, speed, wall, *fields, *done)]
    return pl.pallas_call(
        functools.partial(last_kernel, places=places),
        out_shape=jax.ShapeDtypeStruct(shape, jnp.float32),
        in_specs=[IN_SMEM] + [IN_VMEM] * len(arrays),
        out_specs=pl.BlockSpec(memory_space=pltpu.HBM),
        scratch_shapes=[pltpu.VMEM((2, *shape[1:2], LANES), jnp.float32), pltpu.SemaphoreType.DMA((2 * shape[0],))],
        compiler_params=pltpu.CompilerParams(vmem_limit_bytes=VMEM_LIMIT),
        cost_estimate=pl.CostEstimate(flops=int(1.1e9), bytes_accessed=1024, transcendentals=0),
        name="last",
    )(odd, *arrays)


def pack_kernel(edge, middle, send):
    rows = send.shape[2]
    copy_layer(Layer(edge, 0), Layer(send, 0, False), rows)
    number = send.shape[0] - 1
    for k in range(number):
        copy_layer(Layer(middle, k if number == OUTER - 1 else middle.shape[0] - 1 - k), Layer(send, 1 + k, False), rows)


def solution(mesh):
    split = P(("ens", "gx"), None, None)
    return jax.shard_map(
        shards, mesh=mesh, in_specs=(split, split, split, split, P(), split), out_specs=split, check_vma=False
    )
```

```python
import functools

import jax
import jax.numpy as jnp
from jax import lax
from jax.experimental import pallas as pl
from jax.experimental.pallas import tpu as pltpu
from jax.sharding import PartitionSpec as P

STEPS = 2
NEWTON = 4
WALL_CLASSES = 4
CFL_NUMBER = 0.45

LANES = 128
PAD = 8
ROWS = 32
HALVES = (0, 1)
OUTER = 3
INNER = 2
VMEM_LIMIT = 24 * 1024 * 1024
SEND_ROUND = 2


def cube(t):
    t = jnp.maximum(t, 0.0)
    return t * t * t


def square(t):
    t = jnp.maximum(t, 0.0)
    return t * t


def rcp(x):
    return pl.reciprocal(x, approx=True)


def plane(donor, span, soft_a, soft_b):
    low = jnp.minimum(soft_a, soft_b)
    high = jnp.maximum(soft_a, soft_b)
    pair = soft_a + soft_b
    half = 0.5 * (span + pair)
    top = jnp.maximum(span, high)
    mid = jnp.minimum(span, high)
    over = half - top
    last = half - jnp.abs(over)
    sign = jnp.where(over > 0.0, -1.0, 1.0)
    flat = low * mid
    bulk = flat * top
    share = jnp.clip(jnp.minimum(donor, 1.0 - donor), 0.0, 0.5)
    goal = bulk * share
    at = half - (0.25 * bulk - 0.5 * goal) * rcp(flat - square(over))
    low_6 = low * (1.0 / 6.0)
    mid_6 = mid * (1.0 / 6.0)
    last_6 = last * (1.0 / 6.0)
    for _ in range(NEWTON - 1):
        by_low = square(at - low)
        by_mid = square(at - mid)
        by_last = sign * square(at - last)
        growth = at * at - by_low - by_mid + by_last
        shift = goal - low_6 * by_low - mid_6 * by_mid + last_6 * by_last
        at = (5.0 / 6.0) * at + shift * rcp(growth)
    return at, low, high, pair, half, bulk


def edge_sum(at, low):
    return cube(at) - cube(at - low)


def side_sum(at, low, high, pair):
    return cube(at) - cube(at - low) - cube(at - high) + cube(at - pair)


def prepare(donor, along, soft_a, soft_b, ahead):
    span = jnp.abs(along) + 0.2
    at, low, high, pair, half, bulk = plane(donor, span, soft_a, soft_b)
    light = donor <= 0.5
    sense = jnp.where(jnp.logical_xor(light, ahead), -1.0, 1.0)
    weight = jnp.clip(0.5 + (along * sense) * rcp(half), 0.0, 1.0)
    whole = side_sum(at, low, high, pair)
    whole = whole - weight * (whole + edge_sum(at - span, low))
    scale = sense * rcp(6.0 * bulk)
    heavy = jnp.where(light, 0.0, 1.0)
    return at, span, low, high, weight, scale, whole, heavy


def finish(at, span, low, high, weight, scale, whole, heavy, moved):
    slab = jnp.abs(moved) * span
    rest = side_sum(at - slab, low, high, low + high)
    near = edge_sum(at - span + slab, low)
    return (whole - rest + weight * (rest + near)) * scale + heavy * moved


def face_flux(donor, along, soft_a, soft_b, moved):
    return finish(*prepare(donor, along, soft_a, soft_b, moved > 0.0), moved)


def lane_of(value):
    return lax.broadcasted_iota(jnp.int32, value.shape, 1)


def from_above(pair):
    turned = [pltpu.roll(v, LANES - 1, 1) for v in pair]
    return [jnp.where(lane_of(pair[0]) == LANES - 1, turned[1], turned[0]), turned[1]]


def from_below(pair):
    turned = [pltpu.roll(v, 1, 1) for v in pair]
    first = lane_of(pair[0]) == 0
    return [jnp.where(first, turned[1], turned[0]), jnp.where(first, turned[0], turned[1])]


class Layer:
    def __init__(self, ref, index, padded=True):
        self.ref, self.index, self.pad = ref, index, PAD if padded else 0

    def read(self, half, row):
        return self.ref[self.index, half, pl.ds(self.pad + row, ROWS), :]

    def write(self, half, row, value):
        self.ref[self.index, half, pl.ds(self.pad + row, ROWS), :] = value

    def wrap(self):
        rows = self.ref.shape[2] - 2 * PAD
        for h in HALVES:
            self.ref[self.index, h, pl.ds(0, PAD), :] = self.ref[self.index, h, pl.ds(rows, PAD), :]
            self.ref[self.index, h, pl.ds(PAD + rows, PAD), :] = self.ref[self.index, h, pl.ds(PAD, PAD), :]


def copy_layer(source, target, rows):
    for r in range(0, rows, ROWS):
        for h in HALVES:
            target.write(h, r, source.read(h, r))


def padded_halo(source, field, numbers):
    found = {}
    for k, p in numbers:
        found[p] = Layer(field, p)
        copy_layer(Layer(source, k, False), found[p], field.shape[2] - 2 * PAD)
        found[p].wrap()
    return found


def normals(before, here, after, wall, row):
    centre = [here.read(h, row) for h in HALVES]
    n_x = [before.read(h, row) - after.read(h, row) for h in HALVES]
    n_y = [here.read(h, row - 1) - here.read(h, row + 1) for h in HALVES]
    lane = lane_of(centre[0])
    up = [pltpu.roll(v, LANES - 1, 1) for v in centre]
    down = [pltpu.roll(v, 1, 1) for v in centre]
    top, bottom = lane == LANES - 1, lane == 0
    n_z = [down[0] - jnp.where(top, up[1], up[0]), jnp.where(bottom, down[0], down[1]) - jnp.where(top, centre[1], up[1])]
    contact = wall[pl.ds(row, ROWS), :] * (jnp.abs(n_x[0]) + jnp.abs(n_y[0]))
    n_z[0] = jnp.where(bottom, contact, n_z[0])
    return centre, n_x, n_y, n_z


def soft(normal):
    return jnp.abs(normal) + 0.2


def own_index(odd, layer, count):
    return jnp.where(odd, OUTER + count - 1 - layer, layer - OUTER)


def natural(ref, index, half, row):
    return ref[index, pl.ds(row, ROWS), half * LANES : (half + 1) * LANES]


def begin_kernel(odd_ref, fraction_in, mask_in, class_in, *refs):
    speeds_in, (*speeds, peak, state, classes, fraction, mask, sems) = refs[:3], refs[3:]
    odd = odd_ref[0] == 1
    count, rows, width = fraction.shape
    sources = (*speeds_in, fraction_in, mask_in, class_in)
    copies = [
        pltpu.make_async_copy(source, target, sems.at[n])
        for n, (source, target) in enumerate(zip(sources, (*speeds, fraction, mask, classes)))
    ]
    for copy in copies:
        copy.start()
    best = jnp.zeros((8, width), jnp.float32)
    for n, ref in enumerate(speeds):
        copies[n].wait()
        for i in range(count):
            best = jnp.maximum(best, jnp.max(jnp.abs(ref[i]).reshape(rows // 8, 8, width), axis=0))
    peak[...] = jnp.maximum(best[:, :LANES], best[:, LANES:])
    copies[3].wait()
    copies[4].wait()
    for k in range(count):
        index = own_index(odd, OUTER + k, count)
        for r in range(0, rows, ROWS):
            for h in HALVES:
                value = jnp.where(natural(mask, index, h, r) == 1, 1.0, natural(fraction, index, h, r))
                Layer(state, k).write(h, r, value)
        Layer(state, k).wrap()
    copies[5].wait()


def first_send_kernel(odd_ref, first, state, send_outer, send_inner):
    odd = odd_ref[0] == 1
    count, rows, _ = first.shape
    for k in range(OUTER):
        copy_layer(Layer(state, k), Layer(send_outer, k, False), rows)
    for k in range(INNER):
        copy_layer(Layer(state, count - 1 - k), Layer(send_inner, k, False), rows)
    near = jnp.where(odd, count - 2, 0)
    for r in range(0, rows, ROWS):
        for h in HALVES:
            Layer(send_outer, OUTER, False).write(h, r, natural(first, near, h, r))
            Layer(send_outer, OUTER + 1, False).write(h, r, natural(first, count - 1, h, r))
            Layer(send_inner, INNER, False).write(h, r, natural(first, count - 1, h, r))


def wall_kernel(classes, out, turned):
    device = lax.axis_index("gx")
    odd = lax.rem(device, 2) == 1
    total = classes.shape[0]
    layers = out.shape[0]
    count = layers - OUTER - INNER
    turned[...] = jnp.zeros(turned.shape, jnp.float32)
    for p in range(1, layers - 1):
        row = lax.rem(device * count + own_index(odd, p, count) + total, total)
        turned[pl.ds(p, 1), :] = classes[pl.ds(row, 1), :].astype(jnp.float32)
    used = -(-layers // 8) * 8
    turned[:used, :] = jnp.cos(jnp.pi * (turned[:used, :] + 1.0) / (WALL_CLASSES + 1))
    columns = jnp.transpose(turned[...])
    for p in range(1, layers - 1):
        out[p] = pltpu.roll(columns, LANES - p, 1)


KEPT = 9


def face_work(layers, wall, slopes, faces, rows, work):
    n_s, n_a, n_b = slopes

    def slope(i):
        for r in range(0, rows, ROWS):
            _, n_x, n_y, n_z = normals(layers[i - 1], layers[i], layers[i + 1], wall.at[i], r)
            for h in HALVES:
                Layer(n_s, i, False).write(h, r, n_x[h])
                Layer(n_a, i, False).write(h, r, soft(n_y[h]))
                Layer(n_b, i, False).write(h, r, soft(n_z[h]))

    slope(faces[0])
    for i in faces:
        slope(i + 1)
        sides = [(layers[i], layers[i + 1])] + [(Layer(n, i, False), Layer(n, i + 1, False)) for n in slopes]
        for r in range(0, rows, ROWS):
            for h in HALVES:

                def donor(ahead):
                    return [jnp.where(ahead, low.read(h, r), high.read(h, r)) for low, high in sides]

                work(i, h, r, donor)


def prepare_kernel(odd_ref, *refs, kinds, faces, count):
    given = dict(zip(kinds, refs))
    out, field, *slopes = refs[len(kinds) :]
    rows = out.shape[2]
    odd = odd_ref[0] == 1
    sign = jnp.where(odd, -1.0, 1.0)
    layers = {OUTER + k: Layer(given["own"], k) for k in range(count)}
    needed = range(faces[0] - 1, faces[-1] + 3)
    for kind, first_layer, way, number in (("outer", OUTER - 1, -1, OUTER), ("inner", OUTER + count, 1, INNER)):
        if kind in given:
            numbers = [(k, first_layer + way * k) for k in range(number) if first_layer + way * k in needed]
            layers.update(padded_halo(given[kind], field, numbers))

    def work(face, h, r, donor):
        if face == OUTER - 2:
            speed = Layer(given["outer"], OUTER, False).read(h, r)
        elif face == OUTER - 1:
            speed = natural(given["first"], count - 1, h, r)
            speed = jnp.where(odd, speed, Layer(given["outer"], OUTER + 1, False).read(h, r))
        elif face == OUTER + count - 1:
            speed = natural(given["first"], count - 1, h, r)
            speed = jnp.where(odd, Layer(given["inner"], INNER, False).read(h, r), speed)
        else:
            speed = natural(given["first"], jnp.where(odd, OUTER + count - 2 - face, face - OUTER), h, r)
        speed = speed * sign
        ahead = speed > 0.0
        first_kept = (face - faces[0]) * KEPT
        for n, value in enumerate((*prepare(*donor(ahead), ahead), speed)):
            Layer(out, first_kept + n, False).write(h, r, value)

    face_work(layers, given["wall"], slopes, faces, rows, work)


def finish_faces(kept, step, flux, moved, start):
    rows = kept.shape[2]

    @pl.loop(0, kept.shape[0] // KEPT)
    def _(k):
        for r in range(0, rows, ROWS):
            for h in HALVES:
                values = [Layer(kept, k * KEPT + n, False).read(h, r) for n in range(KEPT)]
                values[-1] = values[-1] * step
                Layer(moved, start + k, False).write(h, r, values[-1])
                Layer(flux, start + k, False).write(h, r, finish(*values))


def update(target, here, inward, outward, rows):
    for r in range(0, rows, ROWS):
        for h in HALVES:
            target.write(h, r, jnp.clip(here.read(h, r) - outward.read(h, r) + inward.read(h, r), 0.0, 1.0))


def finish_kernel(peak, *refs, parts):
    kept, (state, outer, out, above, moved, step_out, send, flux) = refs[:parts], refs[parts:]
    rows = moved.shape[2]
    largest = jnp.max(peak[...])
    step = CFL_NUMBER / (jnp.full((8, LANES), largest, jnp.float32) + 1e-6)
    step_out[...] = step
    start = 0
    for ref in kept:
        finish_faces(ref, step[:1, :], flux, moved, start)
        start += ref.shape[0] // KEPT

    @pl.loop(0, state.shape[0])
    def _(k):
        update(Layer(out, k), Layer(state, k), Layer(flux, k + 1, False), Layer(flux, k + 2, False), rows)
        Layer(out, k).wrap()

    update(Layer(above, 0, False), Layer(outer, 0, False), Layer(flux, 0, False), Layer(flux, 1, False), rows)
    copy_layer(Layer(out, out.shape[0] - 1), Layer(send, 0, False), rows)


def first_fluxes(layers, wall, moved, slopes, flux, faces):
    def work(i, h, r, donor):
        speed = Layer(moved, i - 1, False).read(h, r)
        Layer(flux, i - 1, False).write(h, r, face_flux(*donor(speed > 0.0), speed))

    face_work(layers, wall, slopes, faces, flux.shape[2], work)


def own_layers(*refs):
    found = [Layer(ref, k) for ref in refs for k in range(ref.shape[0])]
    return {OUTER + k: layer for k, layer in enumerate(found)}


def inside_kernel(edge, middle, last, inner, beyond, moved, wall, out, flux_out, send, field, *more):
    *slopes, flux = more
    rows = moved.shape[2]
    layers = own_layers(edge, middle, last)
    count = len(layers)
    layers.update(padded_halo(inner, field, [(0, OUTER + count)]))
    layers[OUTER + count + 1] = Layer(beyond, 0, False)
    first_fluxes(layers, wall, moved, slopes, flux, range(OUTER + 1, OUTER + count))
    copy_layer(Layer(flux, OUTER, False), Layer(flux_out, 0, False), rows)
    for i in range(OUTER + 2, OUTER + count):
        target = Layer(out, i - OUTER - 2)
        update(target, layers[i], Layer(flux, i - 2, False), Layer(flux, i - 1, False), rows)
        target.wrap()
    copy_layer(Layer(out, count - 3), Layer(send, 0, False), rows)


def outside_kernel(edge, middle, last, outer, moved, wall, flux_above, above, out, field, *more):
    *slopes, flux = more
    rows = moved.shape[2]
    layers = own_layers(edge, middle, last)
    layers.update(padded_halo(outer, field, [(k, OUTER - 1 - k) for k in range(OUTER)]))
    first_fluxes(layers, wall, moved, slopes, flux, range(OUTER - 2, OUTER + 1))
    fluxes = [Layer(flux, k, False) for k in range(OUTER)] + [Layer(flux_above, 0, False)]
    for k, target in enumerate((Layer(above, 0, False), Layer(out, 0), Layer(out, 1))):
        update(target, layers[OUTER - 1 + k], fluxes[k], fluxes[k + 1], rows)
        if k > 0:
            target.wrap()


def second_sweep(before, here, after, wall, speed, out, scratch):
    n_s, n_a, n_b, flux = scratch
    rows = out.ref.shape[2] - 2 * PAD
    for r in range(0, rows, ROWS):
        _, n_x, n_y, n_z = normals(before, here, after, wall, r)
        for h in HALVES:
            n_s.write(h, r, n_y[h])
            n_a.write(h, r, soft(n_x[h]))
            n_b.write(h, r, soft(n_z[h]))
    for s in (n_s, n_a, n_b):
        s.wrap()
    for r in range(0, rows, ROWS):
        for h in HALVES:
            moved = speed(h, r)
            ahead = moved > 0.0
            donor = [jnp.where(ahead, s.read(h, r), s.read(h, r + 1)) for s in (here, n_s, n_a, n_b)]
            flux.write(h, r, face_flux(*donor, moved))
    flux.wrap()
    for r in range(0, rows, ROWS):
        for h in HALVES:
            out.write(h, r, jnp.clip(here.read(h, r) - flux.read(h, r) + flux.read(h, r - 1), 0.0, 1.0))
    out.wrap()


def third_sweep(before, here, after, wall, speed, write, rows):
    for r in range(0, rows, ROWS):
        centre, n_x, n_y, n_z = normals(before, here, after, wall, r)
        fields = [centre, n_z, [soft(v) for v in n_x], [soft(v) for v in n_y]]
        above = [from_above(f) for f in fields]
        lane = lane_of(centre[0])
        through = []
        for h in HALVES:
            moved = speed(h, r)
            ahead = moved > 0.0
            through.append(face_flux(*[jnp.where(ahead, f[h], a[h]) for f, a in zip(fields, above)], moved))
        through[1] = jnp.where(lane == LANES - 1, 0.0, through[1])
        below = from_below(through)
        for h in HALVES:
            value = jnp.clip(centre[h] - through[h] + below[h], 0.0, 1.0)
            write(h, r, value)


def gather_layers(refs, places):
    found = {}
    for ref, (start, padded) in zip(refs, places):
        for k in range(ref.shape[0]):
            found[start + k] = Layer(ref, k, padded)
    return found


def second_kernel(odd_ref, step, speed_ref, wall, *refs, places, work, send_last):
    fields, rest = refs[: len(places)], refs[len(places) :]
    out, rest = rest[0], rest[1:]
    send, rest = (rest[0], rest[1:]) if send_last is not None else (None, rest)
    scratch = [Layer(ref, 0) for ref in rest]
    layers = gather_layers(fields, places)
    odd = odd_ref[0] == 1
    count, rows, _ = speed_ref.shape
    for k, p in enumerate(work):
        index = own_index(odd, p, count)
        second_sweep(
            layers[p - 1],
            layers[p],
            layers[p + 1],
            wall.at[p],
            lambda h, r: natural(speed_ref, index, h, r) * step[:1, :],
            Layer(out, k),
            scratch,
        )
    if send is not None:
        copy_layer(Layer(out, work.index(send_last)), Layer(send, 0, False), rows)


def third_kernel(odd_ref, step, speed_ref, wall, *refs, places, work):
    fields, (out,) = refs[: len(places)], refs[len(places) :]
    layers = gather_layers(fields, places)
    odd = odd_ref[0] == 1
    count, rows, _ = speed_ref.shape
    for k, p in enumerate(work):
        index = own_index(odd, p, count)
        third_sweep(
            layers[p - 1],
            layers[p],
            layers[p + 1],
            wall.at[p],
            lambda h, r: natural(speed_ref, index, h, r) * step[:1, :],
            Layer(out, k).write,
            rows,
        )
        Layer(out, k).wrap()


def last_kernel(odd_ref, step, speed_ref, wall, *refs, places):
    fields, rest = refs[: len(places)], refs[len(places) :]
    done, (out, held_out, sems) = rest[:-3], rest[-3:]
    layers = gather_layers(fields, places)
    odd = odd_ref[0] == 1
    count, rows, _ = speed_ref.shape
    copies = []

    def send(source, layer, h, first_row=0):
        rows_here = pl.ds(first_row, source.shape[0])
        target = out.at[own_index(odd, layer, count), rows_here, h * LANES : (h + 1) * LANES]
        copies.append(pltpu.make_async_copy(source, target, sems.at[len(copies)]))
        copies[-1].start()

    p = OUTER + 1
    for ref in done:
        for k in range(ref.shape[0]):
            for h in HALVES:
                send(ref.at[k, h, pl.ds(PAD, rows), :], p, h)
            p += 1

    piece = rows // 2

    def write(h, r, value):
        held_out[h, pl.ds(r, ROWS), :] = value
        if (r + ROWS) % piece == 0:
            start = r + ROWS - piece
            send(held_out.at[h, pl.ds(start, piece), :], OUTER, h, start)

    index = own_index(odd, OUTER, count)
    third_sweep(
        layers[OUTER - 1],
        layers[OUTER],
        layers[OUTER + 1],
        wall.at[OUTER],
        lambda h, r: natural(speed_ref, index, h, r) * step[:1, :],
        write,
        rows,
    )
    for copy in copies:
        copy.wait()


IN_VMEM = pl.BlockSpec(memory_space=pltpu.VMEM)
IN_SMEM = pl.BlockSpec(memory_space=pltpu.SMEM)


def held(shape):
    return pltpu.VMEM(shape, jnp.float32)


def call(kernel, name, outs, scalars, arrays, scratch=(), faces=0.1, resident=True):
    space = pltpu.VMEM if resident else pltpu.HBM
    arrays = [pltpu.with_memory_space_constraint(a, space) for a in arrays]
    work = int(faces * 1.1e9)
    return pl.pallas_call(
        kernel,
        out_shape=outs,
        in_specs=[IN_SMEM] * len(scalars) + [pl.BlockSpec(memory_space=space)] * len(arrays),
        out_specs=[IN_VMEM] * len(outs),
        scratch_shapes=list(scratch),
        compiler_params=pltpu.CompilerParams(vmem_limit_bytes=VMEM_LIMIT),
        cost_estimate=pl.CostEstimate(flops=work, bytes_accessed=1024, transcendentals=0),
        name=name,
    )(*scalars, *arrays)


def swap(array, outer):
    count = lax.axis_size("gx")
    if outer:
        pairs = [(i, (i + 1) % count if i % 2 else (i - 1) % count) for i in range(count)]
    else:
        pairs = [(i, i ^ 1) for i in range(count)]
    return lax.ppermute(array, "gx", pairs)


def largest_round(array, reach, beside):
    count = lax.axis_size("gx")
    if count & (count - 1) == 0:
        pairs = [(i, i ^ reach) for i in range(count)]
    else:
        pairs = [(i, (i + reach) % count) for i in range(count)]
    received = lax.ppermute(array, "gx", pairs)
    if beside:
        received, *_ = lax.optimization_barrier((received, *beside))
    return jnp.maximum(array, received)


def shards(fraction, first, second, third, wall_class, seed_mask):
    count, rows, width = fraction.shape
    layers = OUTER + count + INNER
    own_end = OUTER + count
    device = lax.axis_index("gx")
    odd = (device % 2).astype(jnp.int32).reshape(1)

    def padded(n):
        return (n, 2, rows + 2 * PAD, LANES)

    def plain(n):
        return (n, 2, rows, LANES)

    natural_shape = (count, rows, width)
    first, second, third, peak, state, classes = call(
        begin_kernel,
        "begin",
        [held(natural_shape)] * 3
        + [held((8, LANES)), held(padded(count)), pltpu.VMEM(wall_class.shape, jnp.int32)],
        [odd],
        [fraction, seed_mask, wall_class, first, second, third],
        [
            pltpu.VMEM(natural_shape, jnp.float32),
            pltpu.VMEM(natural_shape, jnp.int32),
            pltpu.SemaphoreType.DMA((6,)),
        ],
        resident=False,
    )
    send_outer, send_inner = call(
        first_send_kernel, "first_send", [held(plain(OUTER + 2)), held(plain(INNER + 1))], [odd], [first, state]
    )
    inner = swap(send_inner, False)
    (wall,) = call(
        wall_kernel, "wall", [held((layers, rows, LANES))], [], [classes], [pltpu.VMEM((LANES, rows), jnp.float32)]
    )
    slopes = [pltpu.VMEM(padded(layers), jnp.float32)] + [pltpu.VMEM(plain(layers), jnp.float32)] * 3

    def prepare_call(faces, **given):
        return call(
            functools.partial(prepare_kernel, kinds=tuple(given), faces=faces, count=count),
            "prepare",
            [held(plain(KEPT * len(faces)))],
            [odd],
            list(given.values()),
            slopes,
            faces=0.02,
        )[0]

    prepare_inside = functools.partial(prepare_call, wall=wall, first=first, own=state, inner=inner)
    outer = swap(send_outer, True)
    size = lax.axis_size("gx")
    reaches = [1 << k for k in range(1, size.bit_length()) if 1 << k < size]
    peak = largest_round(peak, 1, [])
    kept = [prepare_inside(tuple(range(OUTER + 2, own_end)))]
    kept.insert(0, prepare_inside((OUTER + 1,)))
    kept.insert(0, prepare_call((OUTER - 2, OUTER - 1, OUTER), wall=wall, first=first, own=state, outer=outer))
    beside = [[kept[2]], [kept[1]], [kept[0]]]
    for n, reach in enumerate(reaches[::-1]):
        left = len(reaches) - n
        peak = largest_round(peak, reach, beside[-left] if left <= len(beside) else [])
    own, above, moved, step, send_inner = call(
        functools.partial(finish_kernel, parts=len(kept)),
        "finish",
        [held(padded(count)), held(plain(1)), held(plain(count + 2)), held((8, LANES)), held(plain(1))],
        [],
        [peak, *kept, state, outer],
        [pltpu.VMEM(plain(count + 2), jnp.float32)],
        faces=1,
    )
    swept, places = [above, own], [(OUTER - 1, False), (OUTER, True)]
    line = [pltpu.VMEM(padded(1), jnp.float32)] * 4
    def second_call(work, fields, places, send):
        return call(
            functools.partial(second_kernel, places=places, work=work, send_last=work[0] if send else None),
            "second",
            [held(padded(len(work)))] + ([held(plain(1))] if send else []),
            [odd],
            [step, second, wall, *fields],
            line,
            faces=0.1 if own_end - 1 in work else len(work),
        )

    def last_second(part, place, send_inner):
        inner = swap(send_inner, False)
        last, send_inner = second_call((own_end - 1,), [part, inner], [place, (own_end, False)], True)
        return last, swap(send_inner, False)

    for turn in range(STEPS):
        final = turn == STEPS - 1
        if turn > 0:
            flux = pltpu.VMEM(plain(count + 2), jnp.float32)
            inside, flux_low, send_inner = call(
                inside_kernel,
                "inside",
                [held(padded(count - 2)), held(plain(1)), held(plain(1))],
                [],
                [*own, inner, beyond, moved, wall],
                [*slopes, flux],
                faces=0.1,
            )
            last, inner = last_second(inside, (OUTER + 2, True), send_inner)
            outer, last = lax.optimization_barrier((outer, last))
            above, outside = call(
                outside_kernel,
                "outside",
                [held(plain(1)), held(padded(2))],
                [],
                [*own, outer, moved, wall, flux_low],
                [*slopes, flux],
                faces=3,
            )
            swept = [above, outside, inside]
            places = [(OUTER - 1, False), (OUTER, True), (OUTER + 2, True)]
        else:
            last, inner = last_second(swept[-1], places[-1], send_inner)
        edge, send_outer = second_call((OUTER,), swept[:2], places[:2], True)
        after = lax.optimization_barrier((edge, *swept[1:]))[1:]
        (middle,) = second_call(tuple(range(OUTER + 1, own_end - 1)), after, places[1:], False)
        outer = swap(send_outer, True)

        fields = [edge, middle, last, inner]
        starts = [(OUTER, True), (OUTER + 1, True), (own_end - 1, True), (own_end, False)]
        inside_work = tuple(range(OUTER + 1, own_end))
        edge_fields, edge_starts = [outer, edge, middle], [(OUTER - 1, False), (OUTER, True), (OUTER + 1, True)]
        def third_call(work, fields, places):
            return call(
                functools.partial(third_kernel, places=places, work=work),
                "third",
                [held(padded(len(work)))],
                [odd],
                [step, third, wall, *fields],
                faces=len(work),
            )[0]

        middle_new = third_call(inside_work[:-1], fields[:-1], starts[:-1])
        if final:
            last_new = third_call(inside_work[-1:], fields[1:], starts[1:])
            return last_call(odd, step, third, wall, edge_fields, edge_starts, [middle_new, last_new], natural_shape)
        edge_new = third_call((OUTER,), edge_fields, edge_starts)
        send_outer, send_beyond = call(
            pack_kernel, "pack", [held(plain(OUTER)), held(plain(1))], [], [edge_new, middle_new]
        )
        outer = swap(send_outer, True)
        beyond = swap(send_beyond, False)
        beyond, *after = lax.optimization_barrier((beyond, *fields[1:]))
        last_new = third_call(inside_work[-1:], after, starts[1:])
        own = [edge_new, middle_new, last_new]
        (send_inner,) = call(strip_kernel, "strip", [held(plain(1))], [], [last_new])
        inner = swap(send_inner, False)


def last_call(odd, step, speed, wall, fields, places, done, shape):
    arrays = [pltpu.with_memory_space_constraint(a, pltpu.VMEM) for a in (step, speed, wall, *fields, *done)]
    return pl.pallas_call(
        functools.partial(last_kernel, places=places),
        out_shape=jax.ShapeDtypeStruct(shape, jnp.float32),
        in_specs=[IN_SMEM] + [IN_VMEM] * len(arrays),
        out_specs=pl.BlockSpec(memory_space=pltpu.HBM),
        scratch_shapes=[pltpu.VMEM((2, *shape[1:2], LANES), jnp.float32), pltpu.SemaphoreType.DMA((2 * shape[0] + 2,))],
        compiler_params=pltpu.CompilerParams(vmem_limit_bytes=VMEM_LIMIT),
        cost_estimate=pl.CostEstimate(flops=int(1.1e9), bytes_accessed=1024, transcendentals=0),
        name="last",
    )(odd, *arrays)


def pack_kernel(edge, middle, send_outer, send_beyond):
    rows = send_outer.shape[2]
    copy_layer(Layer(edge, 0), Layer(send_outer, 0, False), rows)
    for k in range(OUTER - 1):
        copy_layer(Layer(middle, k), Layer(send_outer, 1 + k, False), rows)
    copy_layer(Layer(middle, middle.shape[0] - 1), Layer(send_beyond, 0, False), rows)


def strip_kernel(last, send):
    copy_layer(Layer(last, 0), Layer(send, 0, False), send.shape[2])


def solution(mesh):
    split = P(("ens", "gx"), None, None)
    return jax.shard_map(
        shards, mesh=mesh, in_specs=(split, split, split, split, P(), split), out_specs=split, check_vma=False
    )
```

```python
import functools

import jax
import jax.numpy as jnp
from jax import lax
from jax.experimental import pallas as pl
from jax.experimental.pallas import tpu as pltpu
from jax.sharding import PartitionSpec as P

STEPS = 2
NEWTON = 4
WALL_CLASSES = 4
CFL_NUMBER = 0.45

LANES = 128
PAD = 8
ROWS = 32
HALVES = (0, 1)
OUTER = 3
INNER = 2
VMEM_LIMIT = 24 * 1024 * 1024
SEND_ROUND = 2


def cube(t):
    t = jnp.maximum(t, 0.0)
    return t * t * t


def square(t):
    t = jnp.maximum(t, 0.0)
    return t * t


def rcp(x):
    return pl.reciprocal(x, approx=True)


def plane(donor, span, soft_a, soft_b):
    low = jnp.minimum(soft_a, soft_b)
    high = jnp.maximum(soft_a, soft_b)
    pair = soft_a + soft_b
    half = 0.5 * (span + pair)
    top = jnp.maximum(span, high)
    mid = jnp.minimum(span, high)
    over = half - top
    last = half - jnp.abs(over)
    sign = jnp.where(over > 0.0, -1.0, 1.0)
    flat = low * mid
    bulk = flat * top
    share = jnp.clip(jnp.minimum(donor, 1.0 - donor), 0.0, 0.5)
    goal = bulk * share
    at = half - (0.25 * bulk - 0.5 * goal) * rcp(flat - square(over))
    low_6 = low * (1.0 / 6.0)
    mid_6 = mid * (1.0 / 6.0)
    last_6 = last * (1.0 / 6.0)
    for _ in range(NEWTON - 1):
        by_low = square(at - low)
        by_mid = square(at - mid)
        by_last = sign * square(at - last)
        growth = at * at - by_low - by_mid + by_last
        shift = goal - low_6 * by_low - mid_6 * by_mid + last_6 * by_last
        at = (5.0 / 6.0) * at + shift * rcp(growth)
    return at, low, high, pair, half, bulk


def edge_sum(at, low):
    return cube(at) - cube(at - low)


def side_sum(at, low, high, pair):
    return cube(at) - cube(at - low) - cube(at - high) + cube(at - pair)


def prepare(donor, along, soft_a, soft_b, ahead):
    span = jnp.abs(along) + 0.2
    at, low, high, pair, half, bulk = plane(donor, span, soft_a, soft_b)
    light = donor <= 0.5
    sense = jnp.where(jnp.logical_xor(light, ahead), -1.0, 1.0)
    weight = jnp.clip(0.5 + (along * sense) * rcp(half), 0.0, 1.0)
    whole = side_sum(at, low, high, pair)
    whole = whole - weight * (whole + edge_sum(at - span, low))
    scale = sense * rcp(6.0 * bulk)
    heavy = jnp.where(light, 0.0, 1.0)
    return at, span, low, high, weight, scale, whole, heavy


def finish(at, span, low, high, weight, scale, whole, heavy, moved):
    slab = jnp.abs(moved) * span
    rest = side_sum(at - slab, low, high, low + high)
    near = edge_sum(at - span + slab, low)
    return (whole - rest + weight * (rest + near)) * scale + heavy * moved


def face_flux(donor, along, soft_a, soft_b, moved):
    return finish(*prepare(donor, along, soft_a, soft_b, moved > 0.0), moved)


def lane_of(value):
    return lax.broadcasted_iota(jnp.int32, value.shape, 1)


def from_above(pair):
    turned = [pltpu.roll(v, LANES - 1, 1) for v in pair]
    return [jnp.where(lane_of(pair[0]) == LANES - 1, turned[1], turned[0]), turned[1]]


def from_below(pair):
    turned = [pltpu.roll(v, 1, 1) for v in pair]
    first = lane_of(pair[0]) == 0
    return [jnp.where(first, turned[1], turned[0]), jnp.where(first, turned[0], turned[1])]


class Layer:
    def __init__(self, ref, index, padded=True):
        self.ref, self.index, self.pad = ref, index, PAD if padded else 0

    def read(self, half, row):
        return self.ref[self.index, half, pl.ds(self.pad + row, ROWS), :]

    def write(self, half, row, value):
        self.ref[self.index, half, pl.ds(self.pad + row, ROWS), :] = value

    def wrap(self):
        rows = self.ref.shape[2] - 2 * PAD
        for h in HALVES:
            self.ref[self.index, h, pl.ds(0, PAD), :] = self.ref[self.index, h, pl.ds(rows, PAD), :]
            self.ref[self.index, h, pl.ds(PAD + rows, PAD), :] = self.ref[self.index, h, pl.ds(PAD, PAD), :]


def copy_layer(source, target, rows):
    for r in range(0, rows, ROWS):
        for h in HALVES:
            target.write(h, r, source.read(h, r))


def padded_halo(source, field, numbers):
    found = {}
    for k, p in numbers:
        found[p] = Layer(field, p)
        copy_layer(Layer(source, k, False), found[p], field.shape[2] - 2 * PAD)
        found[p].wrap()
    return found


def normals(before, here, after, wall, row):
    centre = [here.read(h, row) for h in HALVES]
    n_x = [before.read(h, row) - after.read(h, row) for h in HALVES]
    n_y = [here.read(h, row - 1) - here.read(h, row + 1) for h in HALVES]
    lane = lane_of(centre[0])
    up = [pltpu.roll(v, LANES - 1, 1) for v in centre]
    down = [pltpu.roll(v, 1, 1) for v in centre]
    top, bottom = lane == LANES - 1, lane == 0
    n_z = [down[0] - jnp.where(top, up[1], up[0]), jnp.where(bottom, down[0], down[1]) - jnp.where(top, centre[1], up[1])]
    contact = wall[pl.ds(row, ROWS), :] * (jnp.abs(n_x[0]) + jnp.abs(n_y[0]))
    n_z[0] = jnp.where(bottom, contact, n_z[0])
    return centre, n_x, n_y, n_z


def soft(normal):
    return jnp.abs(normal) + 0.2


def own_index(odd, layer, count):
    return jnp.where(odd, OUTER + count - 1 - layer, layer - OUTER)


def natural(ref, index, half, row):
    return ref[index, pl.ds(row, ROWS), half * LANES : (half + 1) * LANES]


def begin_kernel(odd_ref, fraction_in, mask_in, class_in, *refs):
    speeds_in, (*speeds, peak, state, classes, fraction, mask, sems) = refs[:3], refs[3:]
    odd = odd_ref[0] == 1
    count, rows, width = fraction.shape
    sources = (*speeds_in, fraction_in, mask_in, class_in)
    copies = [
        pltpu.make_async_copy(source, target, sems.at[n])
        for n, (source, target) in enumerate(zip(sources, (*speeds, fraction, mask, classes)))
    ]
    for copy in copies:
        copy.start()
    best = jnp.zeros((8, width), jnp.float32)
    for n, ref in enumerate(speeds):
        copies[n].wait()
        for i in range(count):
            best = jnp.maximum(best, jnp.max(jnp.abs(ref[i]).reshape(rows // 8, 8, width), axis=0))
    peak[...] = jnp.maximum(best[:, :LANES], best[:, LANES:])
    copies[3].wait()
    copies[4].wait()
    for k in range(count):
        index = own_index(odd, OUTER + k, count)
        for r in range(0, rows, ROWS):
            for h in HALVES:
                value = jnp.where(natural(mask, index, h, r) == 1, 1.0, natural(fraction, index, h, r))
                Layer(state, k).write(h, r, value)
        Layer(state, k).wrap()
    copies[5].wait()


def first_send_kernel(odd_ref, first, state, send_outer, send_inner):
    odd = odd_ref[0] == 1
    count, rows, _ = first.shape
    for k in range(OUTER):
        copy_layer(Layer(state, k), Layer(send_outer, k, False), rows)
    for k in range(INNER):
        copy_layer(Layer(state, count - 1 - k), Layer(send_inner, k, False), rows)
    near = jnp.where(odd, count - 2, 0)
    for r in range(0, rows, ROWS):
        for h in HALVES:
            Layer(send_outer, OUTER, False).write(h, r, natural(first, near, h, r))
            Layer(send_outer, OUTER + 1, False).write(h, r, natural(first, count - 1, h, r))
            Layer(send_inner, INNER, False).write(h, r, natural(first, count - 1, h, r))


def wall_kernel(classes, out, turned):
    device = lax.axis_index("gx")
    odd = lax.rem(device, 2) == 1
    total = classes.shape[0]
    layers = out.shape[0]
    count = layers - OUTER - INNER
    turned[...] = jnp.zeros(turned.shape, jnp.float32)
    for p in range(1, layers - 1):
        row = lax.rem(device * count + own_index(odd, p, count) + total, total)
        turned[pl.ds(p, 1), :] = classes[pl.ds(row, 1), :].astype(jnp.float32)
    used = -(-layers // 8) * 8
    turned[:used, :] = jnp.cos(jnp.pi * (turned[:used, :] + 1.0) / (WALL_CLASSES + 1))
    columns = jnp.transpose(turned[...])
    for p in range(1, layers - 1):
        out[p] = pltpu.roll(columns, LANES - p, 1)


KEPT = 9


def face_work(layers, wall, slopes, faces, rows, work):
    n_s, n_a, n_b = slopes

    def slope(i):
        for r in range(0, rows, ROWS):
            _, n_x, n_y, n_z = normals(layers[i - 1], layers[i], layers[i + 1], wall.at[i], r)
            for h in HALVES:
                Layer(n_s, i, False).write(h, r, n_x[h])
                Layer(n_a, i, False).write(h, r, soft(n_y[h]))
                Layer(n_b, i, False).write(h, r, soft(n_z[h]))

    slope(faces[0])
    for i in faces:
        slope(i + 1)
        sides = [(layers[i], layers[i + 1])] + [(Layer(n, i, False), Layer(n, i + 1, False)) for n in slopes]
        for r in range(0, rows, ROWS):
            for h in HALVES:

                def donor(ahead):
                    return [jnp.where(ahead, low.read(h, r), high.read(h, r)) for low, high in sides]

                work(i, h, r, donor)


def prepare_kernel(odd_ref, *refs, kinds, faces, count):
    given = dict(zip(kinds, refs))
    out, field, *slopes = refs[len(kinds) :]
    rows = out.shape[2]
    odd = odd_ref[0] == 1
    sign = jnp.where(odd, -1.0, 1.0)
    layers = {OUTER + k: Layer(given["own"], k) for k in range(count)}
    needed = range(faces[0] - 1, faces[-1] + 3)
    for kind, first_layer, way, number in (("outer", OUTER - 1, -1, OUTER), ("inner", OUTER + count, 1, INNER)):
        if kind in given:
            numbers = [(k, first_layer + way * k) for k in range(number) if first_layer + way * k in needed]
            layers.update(padded_halo(given[kind], field, numbers))

    def work(face, h, r, donor):
        if face == OUTER - 2:
            speed = Layer(given["outer"], OUTER, False).read(h, r)
        elif face == OUTER - 1:
            speed = natural(given["first"], count - 1, h, r)
            speed = jnp.where(odd, speed, Layer(given["outer"], OUTER + 1, False).read(h, r))
        elif face == OUTER + count - 1:
            speed = natural(given["first"], count - 1, h, r)
            speed = jnp.where(odd, Layer(given["inner"], INNER, False).read(h, r), speed)
        else:
            speed = natural(given["first"], jnp.where(odd, OUTER + count - 2 - face, face - OUTER), h, r)
        speed = speed * sign
        ahead = speed > 0.0
        first_kept = (face - faces[0]) * KEPT
        for n, value in enumerate((*prepare(*donor(ahead), ahead), speed)):
            Layer(out, first_kept + n, False).write(h, r, value)

    face_work(layers, given["wall"], slopes, faces, rows, work)


def finish_faces(kept, step, flux, moved, start):
    rows = kept.shape[2]

    @pl.loop(0, kept.shape[0] // KEPT)
    def _(k):
        for r in range(0, rows, ROWS):
            for h in HALVES:
                values = [Layer(kept, k * KEPT + n, False).read(h, r) for n in range(KEPT)]
                values[-1] = values[-1] * step
                Layer(moved, start + k, False).write(h, r, values[-1])
                Layer(flux, start + k, False).write(h, r, finish(*values))


def update(target, here, inward, outward, rows):
    for r in range(0, rows, ROWS):
        for h in HALVES:
            target.write(h, r, jnp.clip(here.read(h, r) - outward.read(h, r) + inward.read(h, r), 0.0, 1.0))


def finish_kernel(peak, *refs, parts):
    kept, (state, outer, out, above, moved, step_out, send, flux) = refs[:parts], refs[parts:]
    rows = moved.shape[2]
    largest = jnp.max(peak[...])
    step = CFL_NUMBER / (jnp.full((8, LANES), largest, jnp.float32) + 1e-6)
    step_out[...] = step
    start = 0
    for ref in kept:
        finish_faces(ref, step[:1, :], flux, moved, start)
        start += ref.shape[0] // KEPT

    @pl.loop(0, state.shape[0])
    def _(k):
        update(Layer(out, k), Layer(state, k), Layer(flux, k + 1, False), Layer(flux, k + 2, False), rows)
        Layer(out, k).wrap()

    update(Layer(above, 0, False), Layer(outer, 0, False), Layer(flux, 0, False), Layer(flux, 1, False), rows)
    copy_layer(Layer(out, out.shape[0] - 1), Layer(send, 0, False), rows)


def first_fluxes(layers, wall, moved, slopes, flux, faces):
    def work(i, h, r, donor):
        speed = Layer(moved, i - 1, False).read(h, r)
        Layer(flux, i - 1, False).write(h, r, face_flux(*donor(speed > 0.0), speed))

    face_work(layers, wall, slopes, faces, flux.shape[2], work)


def own_layers(*refs):
    found = [Layer(ref, k) for ref in refs for k in range(ref.shape[0])]
    return {OUTER + k: layer for k, layer in enumerate(found)}


def middle_kernel(edge, middle, last, moved, wall, flux_out, *slopes):
    rows = moved.shape[2]

    def work(i, h, r, donor):
        speed = Layer(moved, i - 1, False).read(h, r)
        Layer(flux_out, 0, False).write(h, r, face_flux(*donor(speed > 0.0), speed))

    face_work(own_layers(edge, middle, last), wall, slopes, (OUTER + 1,), rows, work)


def inside_kernel(edge, middle, last, inner, beyond, moved, wall, flux_low, out, send, field, *more):
    *slopes, flux = more
    rows = moved.shape[2]
    layers = own_layers(edge, middle, last)
    count = len(layers)
    layers.update(padded_halo(inner, field, [(0, OUTER + count)]))
    layers[OUTER + count + 1] = Layer(beyond, 0, False)
    first_fluxes(layers, wall, moved, slopes, flux, range(OUTER + 2, OUTER + count))
    fluxes = [Layer(flux_low, 0, False)] + [Layer(flux, i - 1, False) for i in range(OUTER + 2, OUTER + count)]
    for k, i in enumerate(range(OUTER + 2, OUTER + count)):
        target = Layer(out, k)
        update(target, layers[i], fluxes[k], fluxes[k + 1], rows)
        target.wrap()
    copy_layer(Layer(out, count - 3), Layer(send, 0, False), rows)


def outside_kernel(edge, middle, last, outer, moved, wall, flux_above, above, out, field, *more):
    *slopes, flux = more
    rows = moved.shape[2]
    layers = own_layers(edge, middle, last)
    layers.update(padded_halo(outer, field, [(k, OUTER - 1 - k) for k in range(OUTER)]))
    first_fluxes(layers, wall, moved, slopes, flux, range(OUTER - 2, OUTER + 1))
    fluxes = [Layer(flux, k, False) for k in range(OUTER)] + [Layer(flux_above, 0, False)]
    for k, target in enumerate((Layer(above, 0, False), Layer(out, 0), Layer(out, 1))):
        update(target, layers[OUTER - 1 + k], fluxes[k], fluxes[k + 1], rows)
        if k > 0:
            target.wrap()


def second_sweep(before, here, after, wall, speed, out, scratch):
    n_s, n_a, n_b, flux = scratch
    rows = out.ref.shape[2] - 2 * PAD
    for r in range(0, rows, ROWS):
        _, n_x, n_y, n_z = normals(before, here, after, wall, r)
        for h in HALVES:
            n_s.write(h, r, n_y[h])
            n_a.write(h, r, soft(n_x[h]))
            n_b.write(h, r, soft(n_z[h]))
    for s in (n_s, n_a, n_b):
        s.wrap()
    for r in range(0, rows, ROWS):
        for h in HALVES:
            moved = speed(h, r)
            ahead = moved > 0.0
            donor = [jnp.where(ahead, s.read(h, r), s.read(h, r + 1)) for s in (here, n_s, n_a, n_b)]
            flux.write(h, r, face_flux(*donor, moved))
    flux.wrap()
    for r in range(0, rows, ROWS):
        for h in HALVES:
            out.write(h, r, jnp.clip(here.read(h, r) - flux.read(h, r) + flux.read(h, r - 1), 0.0, 1.0))
    out.wrap()


def third_sweep(before, here, after, wall, speed, write, rows):
    for r in range(0, rows, ROWS):
        centre, n_x, n_y, n_z = normals(before, here, after, wall, r)
        fields = [centre, n_z, [soft(v) for v in n_x], [soft(v) for v in n_y]]
        above = [from_above(f) for f in fields]
        lane = lane_of(centre[0])
        through = []
        for h in HALVES:
            moved = speed(h, r)
            ahead = moved > 0.0
            through.append(face_flux(*[jnp.where(ahead, f[h], a[h]) for f, a in zip(fields, above)], moved))
        through[1] = jnp.where(lane == LANES - 1, 0.0, through[1])
        below = from_below(through)
        for h in HALVES:
            value = jnp.clip(centre[h] - through[h] + below[h], 0.0, 1.0)
            write(h, r, value)


def gather_layers(refs, places):
    found = {}
    for ref, (start, padded) in zip(refs, places):
        for k in range(ref.shape[0]):
            found[start + k] = Layer(ref, k, padded)
    return found


def second_kernel(odd_ref, step, speed_ref, wall, *refs, places, work, send_last):
    fields, rest = refs[: len(places)], refs[len(places) :]
    out, rest = rest[0], rest[1:]
    send, rest = (rest[0], rest[1:]) if send_last is not None else (None, rest)
    scratch = [Layer(ref, 0) for ref in rest]
    layers = gather_layers(fields, places)
    odd = odd_ref[0] == 1
    count, rows, _ = speed_ref.shape
    for k, p in enumerate(work):
        index = own_index(odd, p, count)
        second_sweep(
            layers[p - 1],
            layers[p],
            layers[p + 1],
            wall.at[p],
            lambda h, r: natural(speed_ref, index, h, r) * step[:1, :],
            Layer(out, k),
            scratch,
        )
    if send is not None:
        copy_layer(Layer(out, work.index(send_last)), Layer(send, 0, False), rows)


def third_kernel(odd_ref, step, speed_ref, wall, *refs, places, work):
    fields, (out,) = refs[: len(places)], refs[len(places) :]
    layers = gather_layers(fields, places)
    odd = odd_ref[0] == 1
    count, rows, _ = speed_ref.shape
    for k, p in enumerate(work):
        index = own_index(odd, p, count)
        third_sweep(
            layers[p - 1],
            layers[p],
            layers[p + 1],
            wall.at[p],
            lambda h, r: natural(speed_ref, index, h, r) * step[:1, :],
            Layer(out, k).write,
            rows,
        )
        Layer(out, k).wrap()


def last_kernel(odd_ref, step, speed_ref, wall, *refs, places):
    fields, rest = refs[: len(places)], refs[len(places) :]
    done, (out, held_out, sems) = rest[:-3], rest[-3:]
    layers = gather_layers(fields, places)
    odd = odd_ref[0] == 1
    count, rows, _ = speed_ref.shape
    copies = []

    def send(source, layer, h, first_row=0):
        rows_here = pl.ds(first_row, source.shape[0])
        target = out.at[own_index(odd, layer, count), rows_here, h * LANES : (h + 1) * LANES]
        copies.append(pltpu.make_async_copy(source, target, sems.at[len(copies)]))
        copies[-1].start()

    p = OUTER + 1
    for ref in done:
        for k in range(ref.shape[0]):
            for h in HALVES:
                send(ref.at[k, h, pl.ds(PAD, rows), :], p, h)
            p += 1

    piece = rows // 2

    def write(h, r, value):
        held_out[h, pl.ds(r, ROWS), :] = value
        if (r + ROWS) % piece == 0:
            start = r + ROWS - piece
            send(held_out.at[h, pl.ds(start, piece), :], OUTER, h, start)

    index = own_index(odd, OUTER, count)
    third_sweep(
        layers[OUTER - 1],
        layers[OUTER],
        layers[OUTER + 1],
        wall.at[OUTER],
        lambda h, r: natural(speed_ref, index, h, r) * step[:1, :],
        write,
        rows,
    )
    for copy in copies:
        copy.wait()


IN_VMEM = pl.BlockSpec(memory_space=pltpu.VMEM)
IN_SMEM = pl.BlockSpec(memory_space=pltpu.SMEM)


def held(shape):
    return pltpu.VMEM(shape, jnp.float32)


def call(kernel, name, outs, scalars, arrays, scratch=(), faces=0.1, resident=True):
    space = pltpu.VMEM if resident else pltpu.HBM
    arrays = [pltpu.with_memory_space_constraint(a, space) for a in arrays]
    work = int(faces * 1.1e9)
    return pl.pallas_call(
        kernel,
        out_shape=outs,
        in_specs=[IN_SMEM] * len(scalars) + [pl.BlockSpec(memory_space=space)] * len(arrays),
        out_specs=[IN_VMEM] * len(outs),
        scratch_shapes=list(scratch),
        compiler_params=pltpu.CompilerParams(vmem_limit_bytes=VMEM_LIMIT),
        cost_estimate=pl.CostEstimate(flops=work, bytes_accessed=1024, transcendentals=0),
        name=name,
    )(*scalars, *arrays)


def swap(array, outer):
    count = lax.axis_size("gx")
    if outer:
        pairs = [(i, (i + 1) % count if i % 2 else (i - 1) % count) for i in range(count)]
    else:
        pairs = [(i, i ^ 1) for i in range(count)]
    return lax.ppermute(array, "gx", pairs)


def largest_round(array, reach, beside):
    count = lax.axis_size("gx")
    if count & (count - 1) == 0:
        pairs = [(i, i ^ reach) for i in range(count)]
    else:
        pairs = [(i, (i + reach) % count) for i in range(count)]
    received = lax.ppermute(array, "gx", pairs)
    if beside:
        received, *_ = lax.optimization_barrier((received, *beside))
    return jnp.maximum(array, received)


def shards(fraction, first, second, third, wall_class, seed_mask):
    count, rows, width = fraction.shape
    layers = OUTER + count + INNER
    own_end = OUTER + count
    device = lax.axis_index("gx")
    odd = (device % 2).astype(jnp.int32).reshape(1)

    def padded(n):
        return (n, 2, rows + 2 * PAD, LANES)

    def plain(n):
        return (n, 2, rows, LANES)

    natural_shape = (count, rows, width)
    first, second, third, peak, state, classes = call(
        begin_kernel,
        "begin",
        [held(natural_shape)] * 3
        + [held((8, LANES)), held(padded(count)), pltpu.VMEM(wall_class.shape, jnp.int32)],
        [odd],
        [fraction, seed_mask, wall_class, first, second, third],
        [
            pltpu.VMEM(natural_shape, jnp.float32),
            pltpu.VMEM(natural_shape, jnp.int32),
            pltpu.SemaphoreType.DMA((6,)),
        ],
        resident=False,
    )
    send_outer, send_inner = call(
        first_send_kernel, "first_send", [held(plain(OUTER + 2)), held(plain(INNER + 1))], [odd], [first, state]
    )
    inner = swap(send_inner, False)
    (wall,) = call(
        wall_kernel, "wall", [held((layers, rows, LANES))], [], [classes], [pltpu.VMEM((LANES, rows), jnp.float32)]
    )
    slopes = [pltpu.VMEM(padded(layers), jnp.float32)] + [pltpu.VMEM(plain(layers), jnp.float32)] * 3

    def prepare_call(faces, **given):
        return call(
            functools.partial(prepare_kernel, kinds=tuple(given), faces=faces, count=count),
            "prepare",
            [held(plain(KEPT * len(faces)))],
            [odd],
            list(given.values()),
            slopes,
            faces=0.02,
        )[0]

    prepare_inside = functools.partial(prepare_call, wall=wall, first=first, own=state, inner=inner)
    outer = swap(send_outer, True)
    size = lax.axis_size("gx")
    reaches = [1 << k for k in range(1, size.bit_length()) if 1 << k < size]
    peak = largest_round(peak, 1, [])
    kept = [prepare_inside(tuple(range(OUTER + 2, own_end)))]
    kept.insert(0, prepare_inside((OUTER + 1,)))
    kept.insert(0, prepare_call((OUTER - 2, OUTER - 1, OUTER), wall=wall, first=first, own=state, outer=outer))
    beside = [[kept[2]], [kept[1]], [kept[0]]]
    for n, reach in enumerate(reaches[::-1]):
        left = len(reaches) - n
        peak = largest_round(peak, reach, beside[-left] if left <= len(beside) else [])
    own, above, moved, step, send_inner = call(
        functools.partial(finish_kernel, parts=len(kept)),
        "finish",
        [held(padded(count)), held(plain(1)), held(plain(count + 2)), held((8, LANES)), held(plain(1))],
        [],
        [peak, *kept, state, outer],
        [pltpu.VMEM(plain(count + 2), jnp.float32)],
        faces=1,
    )
    swept, places = [above, own], [(OUTER - 1, False), (OUTER, True)]
    line = [pltpu.VMEM(padded(1), jnp.float32)] * 4
    def second_call(work, fields, places, send):
        return call(
            functools.partial(second_kernel, places=places, work=work, send_last=work[0] if send else None),
            "second",
            [held(padded(len(work)))] + ([held(plain(1))] if send else []),
            [odd],
            [step, second, wall, *fields],
            line,
            faces=0.1 if own_end - 1 in work else len(work),
        )

    def last_second(part, place, send_inner):
        inner = swap(send_inner, False)
        last, send_inner = second_call((own_end - 1,), [part, inner], [place, (own_end, False)], True)
        return last, swap(send_inner, False)

    for turn in range(STEPS):
        final = turn == STEPS - 1
        if turn > 0:
            flux = pltpu.VMEM(plain(count + 2), jnp.float32)
            (flux_low,) = call(middle_kernel, "middle", [held(plain(1))], [], [*own, moved, wall], slopes[1:])
            inside, send_inner = call(
                inside_kernel,
                "inside",
                [held(padded(count - 2)), held(plain(1))],
                [],
                [*own, inner, beyond, moved, wall, flux_low],
                [*slopes, flux],
                faces=0.1,
            )
            last, inner = last_second(inside, (OUTER + 2, True), send_inner)
            above, outside = call(
                outside_kernel,
                "outside",
                [held(plain(1)), held(padded(2))],
                [],
                [*own, outer, moved, wall, flux_low],
                [*slopes, flux],
                faces=3,
            )
            swept = [above, outside, inside]
            places = [(OUTER - 1, False), (OUTER, True), (OUTER + 2, True)]
        else:
            last, inner = last_second(swept[-1], places[-1], send_inner)
        edge, send_outer = second_call((OUTER,), swept[:2], places[:2], True)
        after = lax.optimization_barrier((edge, *swept[1:]))[1:]
        (middle,) = second_call(tuple(range(OUTER + 1, own_end - 1)), after, places[1:], False)
        outer = swap(send_outer, True)

        fields = [edge, middle, last, inner]
        starts = [(OUTER, True), (OUTER + 1, True), (own_end - 1, True), (own_end, False)]
        inside_work = tuple(range(OUTER + 1, own_end))
        edge_fields, edge_starts = [outer, edge, middle], [(OUTER - 1, False), (OUTER, True), (OUTER + 1, True)]
        def third_call(work, fields, places):
            return call(
                functools.partial(third_kernel, places=places, work=work),
                "third",
                [held(padded(len(work)))],
                [odd],
                [step, third, wall, *fields],
                faces=len(work),
            )[0]

        middle_new = third_call(inside_work[:-1], fields[:-1], starts[:-1])
        if final:
            last_new = third_call(inside_work[-1:], fields[1:], starts[1:])
            return last_call(odd, step, third, wall, edge_fields, edge_starts, [middle_new, last_new], natural_shape)
        edge_new = third_call((OUTER,), edge_fields, edge_starts)
        send_outer, send_beyond = call(
            pack_kernel, "pack", [held(plain(OUTER)), held(plain(1))], [], [edge_new, middle_new]
        )
        outer = swap(send_outer, True)
        beyond = swap(send_beyond, False)
        beyond, *after = lax.optimization_barrier((beyond, *fields[1:]))
        last_new = third_call(inside_work[-1:], after, starts[1:])
        own = [edge_new, middle_new, last_new]
        (send_inner,) = call(strip_kernel, "strip", [held(plain(1))], [], [last_new])
        inner = swap(send_inner, False)


def last_call(odd, step, speed, wall, fields, places, done, shape):
    arrays = [pltpu.with_memory_space_constraint(a, pltpu.VMEM) for a in (step, speed, wall, *fields, *done)]
    return pl.pallas_call(
        functools.partial(last_kernel, places=places),
        out_shape=jax.ShapeDtypeStruct(shape, jnp.float32),
        in_specs=[IN_SMEM] + [IN_VMEM] * len(arrays),
        out_specs=pl.BlockSpec(memory_space=pltpu.HBM),
        scratch_shapes=[pltpu.VMEM((2, *shape[1:2], LANES), jnp.float32), pltpu.SemaphoreType.DMA((2 * shape[0] + 2,))],
        compiler_params=pltpu.CompilerParams(vmem_limit_bytes=VMEM_LIMIT),
        cost_estimate=pl.CostEstimate(flops=int(1.1e9), bytes_accessed=1024, transcendentals=0),
        name="last",
    )(odd, *arrays)


def pack_kernel(edge, middle, send_outer, send_beyond):
    rows = send_outer.shape[2]
    copy_layer(Layer(edge, 0), Layer(send_outer, 0, False), rows)
    for k in range(OUTER - 1):
        copy_layer(Layer(middle, k), Layer(send_outer, 1 + k, False), rows)
    copy_layer(Layer(middle, middle.shape[0] - 1), Layer(send_beyond, 0, False), rows)


def strip_kernel(last, send):
    copy_layer(Layer(last, 0), Layer(send, 0, False), send.shape[2])


def solution(mesh):
    split = P(("ens", "gx"), None, None)
    return jax.shard_map(
        shards, mesh=mesh, in_specs=(split, split, split, split, P(), split), out_specs=split, check_vma=False
    )
```

```python
import functools

import jax
import jax.numpy as jnp
from jax import lax
from jax.experimental import pallas as pl
from jax.experimental.pallas import tpu as pltpu
from jax.sharding import PartitionSpec as P

STEPS = 2
NEWTON = 4
WALL_CLASSES = 4
CFL_NUMBER = 0.45

LANES = 128
PAD = 8
ROWS = 32
HALVES = (0, 1)
OUTER = 3
INNER = 2
VMEM_LIMIT = 24 * 1024 * 1024
SEND_ROUND = 2


def cube(t):
    t = jnp.maximum(t, 0.0)
    return t * t * t


def square(t):
    t = jnp.maximum(t, 0.0)
    return t * t


def rcp(x):
    return pl.reciprocal(x, approx=True)


def plane(donor, span, soft_a, soft_b):
    low = jnp.minimum(soft_a, soft_b)
    high = jnp.maximum(soft_a, soft_b)
    pair = soft_a + soft_b
    half = 0.5 * (span + pair)
    top = jnp.maximum(span, high)
    mid = jnp.minimum(span, high)
    over = half - top
    last = half - jnp.abs(over)
    sign = jnp.where(over > 0.0, -1.0, 1.0)
    flat = low * mid
    bulk = flat * top
    share = jnp.clip(jnp.minimum(donor, 1.0 - donor), 0.0, 0.5)
    goal = bulk * share
    at = half - (0.25 * bulk - 0.5 * goal) * rcp(flat - square(over))
    low_6 = low * (1.0 / 6.0)
    mid_6 = mid * (1.0 / 6.0)
    last_6 = last * (1.0 / 6.0)
    for _ in range(NEWTON - 1):
        by_low = square(at - low)
        by_mid = square(at - mid)
        by_last = sign * square(at - last)
        growth = at * at - by_low - by_mid + by_last
        shift = goal - low_6 * by_low - mid_6 * by_mid + last_6 * by_last
        at = (5.0 / 6.0) * at + shift * rcp(growth)
    return at, low, high, pair, half, bulk


def edge_sum(at, low):
    return cube(at) - cube(at - low)


def side_sum(at, low, high, pair):
    return cube(at) - cube(at - low) - cube(at - high) + cube(at - pair)


def prepare(donor, along, soft_a, soft_b, ahead):
    span = jnp.abs(along) + 0.2
    at, low, high, pair, half, bulk = plane(donor, span, soft_a, soft_b)
    light = donor <= 0.5
    sense = jnp.where(jnp.logical_xor(light, ahead), -1.0, 1.0)
    weight = jnp.clip(0.5 + (along * sense) * rcp(half), 0.0, 1.0)
    whole = side_sum(at, low, high, pair)
    whole = whole - weight * (whole + edge_sum(at - span, low))
    scale = sense * rcp(6.0 * bulk)
    heavy = jnp.where(light, 0.0, 1.0)
    return at, span, low, high, weight, scale, whole, heavy


def finish(at, span, low, high, weight, scale, whole, heavy, moved):
    slab = jnp.abs(moved) * span
    rest = side_sum(at - slab, low, high, low + high)
    near = edge_sum(at - span + slab, low)
    return (whole - rest + weight * (rest + near)) * scale + heavy * moved


def face_flux(donor, along, soft_a, soft_b, moved):
    return finish(*prepare(donor, along, soft_a, soft_b, moved > 0.0), moved)


def lane_of(value):
    return lax.broadcasted_iota(jnp.int32, value.shape, 1)


def from_above(pair):
    turned = [pltpu.roll(v, LANES - 1, 1) for v in pair]
    return [jnp.where(lane_of(pair[0]) == LANES - 1, turned[1], turned[0]), turned[1]]


def from_below(pair):
    turned = [pltpu.roll(v, 1, 1) for v in pair]
    first = lane_of(pair[0]) == 0
    return [jnp.where(first, turned[1], turned[0]), jnp.where(first, turned[0], turned[1])]


class Layer:
    def __init__(self, ref, index, padded=True):
        self.ref, self.index, self.pad = ref, index, PAD if padded else 0

    def read(self, half, row):
        return self.ref[self.index, half, pl.ds(self.pad + row, ROWS), :]

    def write(self, half, row, value):
        self.ref[self.index, half, pl.ds(self.pad + row, ROWS), :] = value

    def wrap(self):
        rows = self.ref.shape[2] - 2 * PAD
        for h in HALVES:
            self.ref[self.index, h, pl.ds(0, PAD), :] = self.ref[self.index, h, pl.ds(rows, PAD), :]
            self.ref[self.index, h, pl.ds(PAD + rows, PAD), :] = self.ref[self.index, h, pl.ds(PAD, PAD), :]


def copy_layer(source, target, rows):
    for r in range(0, rows, ROWS):
        for h in HALVES:
            target.write(h, r, source.read(h, r))


def padded_halo(source, field, numbers):
    found = {}
    for k, p in numbers:
        found[p] = Layer(field, p)
        copy_layer(Layer(source, k, False), found[p], field.shape[2] - 2 * PAD)
        found[p].wrap()
    return found


def normals(before, here, after, wall, row):
    centre = [here.read(h, row) for h in HALVES]
    n_x = [before.read(h, row) - after.read(h, row) for h in HALVES]
    n_y = [here.read(h, row - 1) - here.read(h, row + 1) for h in HALVES]
    lane = lane_of(centre[0])
    up = [pltpu.roll(v, LANES - 1, 1) for v in centre]
    down = [pltpu.roll(v, 1, 1) for v in centre]
    top, bottom = lane == LANES - 1, lane == 0
    n_z = [down[0] - jnp.where(top, up[1], up[0]), jnp.where(bottom, down[0], down[1]) - jnp.where(top, centre[1], up[1])]
    contact = wall[pl.ds(row, ROWS), :] * (jnp.abs(n_x[0]) + jnp.abs(n_y[0]))
    n_z[0] = jnp.where(bottom, contact, n_z[0])
    return centre, n_x, n_y, n_z


def soft(normal):
    return jnp.abs(normal) + 0.2


def own_index(odd, layer, count):
    return jnp.where(odd, OUTER + count - 1 - layer, layer - OUTER)


def natural(ref, index, half, row):
    return ref[index, pl.ds(row, ROWS), half * LANES : (half + 1) * LANES]


def begin_kernel(odd_ref, fraction_in, mask_in, class_in, *refs):
    speeds_in, (*speeds, peak, state, classes, fraction, mask, sems) = refs[:3], refs[3:]
    odd = odd_ref[0] == 1
    count, rows, width = fraction.shape
    sources = (*speeds_in, fraction_in, mask_in, class_in)
    copies = [
        pltpu.make_async_copy(source, target, sems.at[n])
        for n, (source, target) in enumerate(zip(sources, (*speeds, fraction, mask, classes)))
    ]
    for copy in copies:
        copy.start()
    best = jnp.zeros((8, width), jnp.float32)
    for n, ref in enumerate(speeds):
        copies[n].wait()
        for i in range(count):
            best = jnp.maximum(best, jnp.max(jnp.abs(ref[i]).reshape(rows // 8, 8, width), axis=0))
    peak[...] = jnp.maximum(best[:, :LANES], best[:, LANES:])
    copies[3].wait()
    copies[4].wait()
    for k in range(count):
        index = own_index(odd, OUTER + k, count)
        for r in range(0, rows, ROWS):
            for h in HALVES:
                value = jnp.where(natural(mask, index, h, r) == 1, 1.0, natural(fraction, index, h, r))
                Layer(state, k).write(h, r, value)
        Layer(state, k).wrap()
    copies[5].wait()


def first_send_kernel(odd_ref, first, state, send_outer, send_inner):
    odd = odd_ref[0] == 1
    count, rows, _ = first.shape
    for k in range(OUTER):
        copy_layer(Layer(state, k), Layer(send_outer, k, False), rows)
    for k in range(INNER):
        copy_layer(Layer(state, count - 1 - k), Layer(send_inner, k, False), rows)
    near = jnp.where(odd, count - 2, 0)
    for r in range(0, rows, ROWS):
        for h in HALVES:
            Layer(send_outer, OUTER, False).write(h, r, natural(first, near, h, r))
            Layer(send_outer, OUTER + 1, False).write(h, r, natural(first, count - 1, h, r))
            Layer(send_inner, INNER, False).write(h, r, natural(first, count - 1, h, r))


def wall_kernel(classes, out, turned):
    device = lax.axis_index("gx")
    odd = lax.rem(device, 2) == 1
    total = classes.shape[0]
    layers = out.shape[0]
    count = layers - OUTER - INNER
    turned[...] = jnp.zeros(turned.shape, jnp.float32)
    for p in range(1, layers - 1):
        row = lax.rem(device * count + own_index(odd, p, count) + total, total)
        turned[pl.ds(p, 1), :] = classes[pl.ds(row, 1), :].astype(jnp.float32)
    used = -(-layers // 8) * 8
    turned[:used, :] = jnp.cos(jnp.pi * (turned[:used, :] + 1.0) / (WALL_CLASSES + 1))
    columns = jnp.transpose(turned[...])
    for p in range(1, layers - 1):
        out[p] = pltpu.roll(columns, LANES - p, 1)


KEPT = 9


def face_work(layers, wall, slopes, faces, rows, work):
    n_s, n_a, n_b = slopes

    def slope(i):
        for r in range(0, rows, ROWS):
            _, n_x, n_y, n_z = normals(layers[i - 1], layers[i], layers[i + 1], wall.at[i], r)
            for h in HALVES:
                Layer(n_s, i, False).write(h, r, n_x[h])
                Layer(n_a, i, False).write(h, r, soft(n_y[h]))
                Layer(n_b, i, False).write(h, r, soft(n_z[h]))

    slope(faces[0])
    for i in faces:
        slope(i + 1)
        sides = [(layers[i], layers[i + 1])] + [(Layer(n, i, False), Layer(n, i + 1, False)) for n in slopes]
        for r in range(0, rows, ROWS):
            for h in HALVES:

                def donor(ahead):
                    return [jnp.where(ahead, low.read(h, r), high.read(h, r)) for low, high in sides]

                work(i, h, r, donor)


def prepare_kernel(odd_ref, *refs, kinds, faces, count):
    given = dict(zip(kinds, refs))
    out, field, *slopes = refs[len(kinds) :]
    rows = out.shape[2]
    odd = odd_ref[0] == 1
    sign = jnp.where(odd, -1.0, 1.0)
    layers = {OUTER + k: Layer(given["own"], k) for k in range(count)}
    needed = range(faces[0] - 1, faces[-1] + 3)
    for kind, first_layer, way, number in (("outer", OUTER - 1, -1, OUTER), ("inner", OUTER + count, 1, INNER)):
        if kind in given:
            numbers = [(k, first_layer + way * k) for k in range(number) if first_layer + way * k in needed]
            layers.update(padded_halo(given[kind], field, numbers))

    def work(face, h, r, donor):
        if face == OUTER - 2:
            speed = Layer(given["outer"], OUTER, False).read(h, r)
        elif face == OUTER - 1:
            speed = natural(given["first"], count - 1, h, r)
            speed = jnp.where(odd, speed, Layer(given["outer"], OUTER + 1, False).read(h, r))
        elif face == OUTER + count - 1:
            speed = natural(given["first"], count - 1, h, r)
            speed = jnp.where(odd, Layer(given["inner"], INNER, False).read(h, r), speed)
        else:
            speed = natural(given["first"], jnp.where(odd, OUTER + count - 2 - face, face - OUTER), h, r)
        speed = speed * sign
        ahead = speed > 0.0
        first_kept = (face - faces[0]) * KEPT
        for n, value in enumerate((*prepare(*donor(ahead), ahead), speed)):
            Layer(out, first_kept + n, False).write(h, r, value)

    face_work(layers, given["wall"], slopes, faces, rows, work)


def finish_faces(kept, step, flux, moved, start):
    rows = kept.shape[2]

    @pl.loop(0, kept.shape[0] // KEPT)
    def _(k):
        for r in range(0, rows, ROWS):
            for h in HALVES:
                values = [Layer(kept, k * KEPT + n, False).read(h, r) for n in range(KEPT)]
                values[-1] = values[-1] * step
                Layer(moved, start + k, False).write(h, r, values[-1])
                Layer(flux, start + k, False).write(h, r, finish(*values))


def update(target, here, inward, outward, rows):
    for r in range(0, rows, ROWS):
        for h in HALVES:
            target.write(h, r, jnp.clip(here.read(h, r) - outward.read(h, r) + inward.read(h, r), 0.0, 1.0))


def finish_kernel(peak, *refs, parts):
    kept, (state, outer, out, above, moved, step_out, send, flux) = refs[:parts], refs[parts:]
    rows = moved.shape[2]
    largest = jnp.max(peak[...])
    step = CFL_NUMBER / (jnp.full((8, LANES), largest, jnp.float32) + 1e-6)
    step_out[...] = step
    start = 0
    for ref in kept:
        finish_faces(ref, step[:1, :], flux, moved, start)
        start += ref.shape[0] // KEPT

    @pl.loop(0, state.shape[0])
    def _(k):
        update(Layer(out, k), Layer(state, k), Layer(flux, k + 1, False), Layer(flux, k + 2, False), rows)
        Layer(out, k).wrap()

    update(Layer(above, 0, False), Layer(outer, 0, False), Layer(flux, 0, False), Layer(flux, 1, False), rows)
    copy_layer(Layer(out, out.shape[0] - 1), Layer(send, 0, False), rows)


def first_fluxes(layers, wall, moved, slopes, flux, faces):
    def work(i, h, r, donor):
        speed = Layer(moved, i - 1, False).read(h, r)
        Layer(flux, i - 1, False).write(h, r, face_flux(*donor(speed > 0.0), speed))

    face_work(layers, wall, slopes, faces, flux.shape[2], work)


def own_layers(*refs):
    found = [Layer(ref, k) for ref in refs for k in range(ref.shape[0])]
    return {OUTER + k: layer for k, layer in enumerate(found)}


def middle_kernel(edge, middle, last, moved, wall, flux_out, *slopes):
    rows = moved.shape[2]

    def work(i, h, r, donor):
        speed = Layer(moved, i - 1, False).read(h, r)
        Layer(flux_out, 0, False).write(h, r, face_flux(*donor(speed > 0.0), speed))

    face_work(own_layers(edge, middle, last), wall, slopes, (OUTER + 1,), rows, work)


def inside_kernel(edge, middle, last, inner, beyond, moved, wall, flux_low, out, send, field, *more):
    *slopes, flux = more
    rows = moved.shape[2]
    layers = own_layers(edge, middle, last)
    count = len(layers)
    layers.update(padded_halo(inner, field, [(0, OUTER + count)]))
    layers[OUTER + count + 1] = Layer(beyond, 0, False)
    first_fluxes(layers, wall, moved, slopes, flux, range(OUTER + 2, OUTER + count))
    fluxes = [Layer(flux_low, 0, False)] + [Layer(flux, i - 1, False) for i in range(OUTER + 2, OUTER + count)]
    for k, i in enumerate(range(OUTER + 2, OUTER + count)):
        target = Layer(out, k)
        update(target, layers[i], fluxes[k], fluxes[k + 1], rows)
        target.wrap()
    copy_layer(Layer(out, count - 3), Layer(send, 0, False), rows)


def outside_kernel(edge, middle, last, outer, moved, wall, flux_above, above, out, field, *more):
    *slopes, flux = more
    rows = moved.shape[2]
    layers = own_layers(edge, middle, last)
    layers.update(padded_halo(outer, field, [(k, OUTER - 1 - k) for k in range(OUTER)]))
    first_fluxes(layers, wall, moved, slopes, flux, range(OUTER - 2, OUTER + 1))
    fluxes = [Layer(flux, k, False) for k in range(OUTER)] + [Layer(flux_above, 0, False)]
    for k, target in enumerate((Layer(above, 0, False), Layer(out, 0), Layer(out, 1))):
        update(target, layers[OUTER - 1 + k], fluxes[k], fluxes[k + 1], rows)
        if k > 0:
            target.wrap()


def second_sweep(before, here, after, wall, speed, out, scratch):
    n_s, n_a, n_b, flux = scratch
    rows = out.ref.shape[2] - 2 * PAD
    for r in range(0, rows, ROWS):
        _, n_x, n_y, n_z = normals(before, here, after, wall, r)
        for h in HALVES:
            n_s.write(h, r, n_y[h])
            n_a.write(h, r, soft(n_x[h]))
            n_b.write(h, r, soft(n_z[h]))
    for s in (n_s, n_a, n_b):
        s.wrap()
    for r in range(0, rows, ROWS):
        for h in HALVES:
            moved = speed(h, r)
            ahead = moved > 0.0
            donor = [jnp.where(ahead, s.read(h, r), s.read(h, r + 1)) for s in (here, n_s, n_a, n_b)]
            flux.write(h, r, face_flux(*donor, moved))
    flux.wrap()
    for r in range(0, rows, ROWS):
        for h in HALVES:
            out.write(h, r, jnp.clip(here.read(h, r) - flux.read(h, r) + flux.read(h, r - 1), 0.0, 1.0))
    out.wrap()


def third_sweep(before, here, after, wall, speed, write, rows):
    for r in range(0, rows, ROWS):
        centre, n_x, n_y, n_z = normals(before, here, after, wall, r)
        fields = [centre, n_z, [soft(v) for v in n_x], [soft(v) for v in n_y]]
        above = [from_above(f) for f in fields]
        lane = lane_of(centre[0])
        through = []
        for h in HALVES:
            moved = speed(h, r)
            ahead = moved > 0.0
            through.append(face_flux(*[jnp.where(ahead, f[h], a[h]) for f, a in zip(fields, above)], moved))
        through[1] = jnp.where(lane == LANES - 1, 0.0, through[1])
        below = from_below(through)
        for h in HALVES:
            value = jnp.clip(centre[h] - through[h] + below[h], 0.0, 1.0)
            write(h, r, value)


def gather_layers(refs, places):
    found = {}
    for ref, (start, padded) in zip(refs, places):
        for k in range(ref.shape[0]):
            found[start + k] = Layer(ref, k, padded)
    return found


def second_kernel(odd_ref, step, speed_ref, wall, *refs, places, work, send_last):
    fields, rest = refs[: len(places)], refs[len(places) :]
    out, rest = rest[0], rest[1:]
    send, rest = (rest[0], rest[1:]) if send_last is not None else (None, rest)
    scratch = [Layer(ref, 0) for ref in rest]
    layers = gather_layers(fields, places)
    odd = odd_ref[0] == 1
    count, rows, _ = speed_ref.shape
    for k, p in enumerate(work):
        index = own_index(odd, p, count)
        second_sweep(
            layers[p - 1],
            layers[p],
            layers[p + 1],
            wall.at[p],
            lambda h, r: natural(speed_ref, index, h, r) * step[:1, :],
            Layer(out, k),
            scratch,
        )
    if send is not None:
        copy_layer(Layer(out, work.index(send_last)), Layer(send, 0, False), rows)


def third_kernel(odd_ref, step, speed_ref, wall, *refs, places, work):
    fields, (out,) = refs[: len(places)], refs[len(places) :]
    layers = gather_layers(fields, places)
    odd = odd_ref[0] == 1
    count, rows, _ = speed_ref.shape
    for k, p in enumerate(work):
        index = own_index(odd, p, count)
        third_sweep(
            layers[p - 1],
            layers[p],
            layers[p + 1],
            wall.at[p],
            lambda h, r: natural(speed_ref, index, h, r) * step[:1, :],
            Layer(out, k).write,
            rows,
        )
        Layer(out, k).wrap()


def last_kernel(odd_ref, step, speed_ref, wall, *refs, places):
    fields, rest = refs[: len(places)], refs[len(places) :]
    done, (out, held_out, sems) = rest[:-3], rest[-3:]
    layers = gather_layers(fields, places)
    odd = odd_ref[0] == 1
    count, rows, _ = speed_ref.shape
    copies = []

    def send(source, layer, h, first_row=0):
        rows_here = pl.ds(first_row, source.shape[0])
        target = out.at[own_index(odd, layer, count), rows_here, h * LANES : (h + 1) * LANES]
        copies.append(pltpu.make_async_copy(source, target, sems.at[len(copies)]))
        copies[-1].start()

    p = OUTER + 1
    for ref in done:
        for k in range(ref.shape[0]):
            for h in HALVES:
                send(ref.at[k, h, pl.ds(PAD, rows), :], p, h)
            p += 1

    piece = rows // 2

    def write(h, r, value):
        held_out[h, pl.ds(r, ROWS), :] = value
        if (r + ROWS) % piece == 0:
            start = r + ROWS - piece
            send(held_out.at[h, pl.ds(start, piece), :], OUTER, h, start)

    index = own_index(odd, OUTER, count)
    third_sweep(
        layers[OUTER - 1],
        layers[OUTER],
        layers[OUTER + 1],
        wall.at[OUTER],
        lambda h, r: natural(speed_ref, index, h, r) * step[:1, :],
        write,
        rows,
    )
    for copy in copies:
        copy.wait()


IN_VMEM = pl.BlockSpec(memory_space=pltpu.VMEM)
IN_SMEM = pl.BlockSpec(memory_space=pltpu.SMEM)


def held(shape):
    return pltpu.VMEM(shape, jnp.float32)


def call(kernel, name, outs, scalars, arrays, scratch=(), faces=0.1, resident=True):
    space = pltpu.VMEM if resident else pltpu.HBM
    arrays = [pltpu.with_memory_space_constraint(a, space) for a in arrays]
    work = int(faces * 1.1e9)
    return pl.pallas_call(
        kernel,
        out_shape=outs,
        in_specs=[IN_SMEM] * len(scalars) + [pl.BlockSpec(memory_space=space)] * len(arrays),
        out_specs=[IN_VMEM] * len(outs),
        scratch_shapes=list(scratch),
        compiler_params=pltpu.CompilerParams(vmem_limit_bytes=VMEM_LIMIT),
        cost_estimate=pl.CostEstimate(flops=work, bytes_accessed=1024, transcendentals=0),
        name=name,
    )(*scalars, *arrays)


def swap(array, outer):
    count = lax.axis_size("gx")
    if outer:
        pairs = [(i, (i + 1) % count if i % 2 else (i - 1) % count) for i in range(count)]
    else:
        pairs = [(i, i ^ 1) for i in range(count)]
    return lax.ppermute(array, "gx", pairs)


def largest_round(array, reach, beside):
    count = lax.axis_size("gx")
    if count & (count - 1) == 0:
        pairs = [(i, i ^ reach) for i in range(count)]
    else:
        pairs = [(i, (i + reach) % count) for i in range(count)]
    received = lax.ppermute(array, "gx", pairs)
    if beside:
        received, *_ = lax.optimization_barrier((received, *beside))
    return jnp.maximum(array, received)


def shards(fraction, first, second, third, wall_class, seed_mask):
    count, rows, width = fraction.shape
    layers = OUTER + count + INNER
    own_end = OUTER + count
    device = lax.axis_index("gx")
    odd = (device % 2).astype(jnp.int32).reshape(1)

    def padded(n):
        return (n, 2, rows + 2 * PAD, LANES)

    def plain(n):
        return (n, 2, rows, LANES)

    natural_shape = (count, rows, width)
    first, second, third, peak, state, classes = call(
        begin_kernel,
        "begin",
        [held(natural_shape)] * 3
        + [held((8, LANES)), held(padded(count)), pltpu.VMEM(wall_class.shape, jnp.int32)],
        [odd],
        [fraction, seed_mask, wall_class, first, second, third],
        [
            pltpu.VMEM(natural_shape, jnp.float32),
            pltpu.VMEM(natural_shape, jnp.int32),
            pltpu.SemaphoreType.DMA((6,)),
        ],
        resident=False,
    )
    send_outer, send_inner = call(
        first_send_kernel, "first_send", [held(plain(OUTER + 2)), held(plain(INNER + 1))], [odd], [first, state]
    )
    inner = swap(send_inner, False)
    (wall,) = call(
        wall_kernel, "wall", [held((layers, rows, LANES))], [], [classes], [pltpu.VMEM((LANES, rows), jnp.float32)]
    )
    slopes = [pltpu.VMEM(padded(layers), jnp.float32)] + [pltpu.VMEM(plain(layers), jnp.float32)] * 3

    def prepare_call(faces, **given):
        return call(
            functools.partial(prepare_kernel, kinds=tuple(given), faces=faces, count=count),
            "prepare",
            [held(plain(KEPT * len(faces)))],
            [odd],
            list(given.values()),
            slopes,
            faces=0.02,
        )[0]

    prepare_inside = functools.partial(prepare_call, wall=wall, first=first, own=state, inner=inner)
    outer = swap(send_outer, True)
    size = lax.axis_size("gx")
    reaches = [1 << k for k in range(1, size.bit_length()) if 1 << k < size]
    peak = largest_round(peak, 1, [])
    kept = [prepare_inside(tuple(range(OUTER + 2, own_end)))]
    kept.insert(0, prepare_inside((OUTER + 1,)))
    kept.insert(0, prepare_call((OUTER - 2, OUTER - 1, OUTER), wall=wall, first=first, own=state, outer=outer))
    beside = [[kept[2]], [kept[1]], [kept[0]]]
    for n, reach in enumerate(reaches[::-1]):
        left = len(reaches) - n
        peak = largest_round(peak, reach, beside[-left] if left <= len(beside) else [])
    own, above, moved, step, send_inner = call(
        functools.partial(finish_kernel, parts=len(kept)),
        "finish",
        [held(padded(count)), held(plain(1)), held(plain(count + 2)), held((8, LANES)), held(plain(1))],
        [],
        [peak, *kept, state, outer],
        [pltpu.VMEM(plain(count + 2), jnp.float32)],
        faces=1,
    )
    swept, places = [above, own], [(OUTER - 1, False), (OUTER, True)]
    line = [pltpu.VMEM(padded(1), jnp.float32)] * 4
    def second_call(work, fields, places, send):
        return call(
            functools.partial(second_kernel, places=places, work=work, send_last=work[0] if send else None),
            "second",
            [held(padded(len(work)))] + ([held(plain(1))] if send else []),
            [odd],
            [step, second, wall, *fields],
            line,
            faces=0.1 if own_end - 1 in work else len(work),
        )

    def last_second(part, place, send_inner):
        inner = swap(send_inner, False)
        last, send_inner = second_call((own_end - 1,), [part, inner], [place, (own_end, False)], True)
        return last, swap(send_inner, False)

    for turn in range(STEPS):
        final = turn == STEPS - 1
        if turn > 0:
            flux = pltpu.VMEM(plain(count + 2), jnp.float32)
            (flux_low,) = call(middle_kernel, "middle", [held(plain(1))], [], [*own, moved, wall], slopes[1:])
            inside, send_inner = call(
                inside_kernel,
                "inside",
                [held(padded(count - 2)), held(plain(1))],
                [],
                [*own, inner, beyond, moved, wall, flux_low],
                [*slopes, flux],
                faces=0.1,
            )
            last, inner = last_second(inside, (OUTER + 2, True), send_inner)
            above, outside = call(
                outside_kernel,
                "outside",
                [held(plain(1)), held(padded(2))],
                [],
                [*own, outer, moved, wall, flux_low],
                [*slopes, flux],
                faces=3,
            )
            swept = [above, outside, inside]
            places = [(OUTER - 1, False), (OUTER, True), (OUTER + 2, True)]
        edge, send_outer = second_call((OUTER,), swept[:2], places[:2], True)
        if turn == 0:
            send_outer, send_inner = lax.optimization_barrier((send_outer, send_inner))
            last, inner = last_second(swept[-1], places[-1], send_inner)
        after = lax.optimization_barrier((edge, *swept[1:]))[1:]
        (middle,) = second_call(tuple(range(OUTER + 1, own_end - 1)), after, places[1:], False)
        outer = swap(send_outer, True)

        fields = [edge, middle, last, inner]
        starts = [(OUTER, True), (OUTER + 1, True), (own_end - 1, True), (own_end, False)]
        inside_work = tuple(range(OUTER + 1, own_end))
        edge_fields, edge_starts = [outer, edge, middle], [(OUTER - 1, False), (OUTER, True), (OUTER + 1, True)]
        def third_call(work, fields, places):
            return call(
                functools.partial(third_kernel, places=places, work=work),
                "third",
                [held(padded(len(work)))],
                [odd],
                [step, third, wall, *fields],
                faces=len(work),
            )[0]

        middle_new = third_call(inside_work[:-1], fields[:-1], starts[:-1])
        if final:
            last_new = third_call(inside_work[-1:], fields[1:], starts[1:])
            return last_call(odd, step, third, wall, edge_fields, edge_starts, [middle_new, last_new], natural_shape)
        edge_new = third_call((OUTER,), edge_fields, edge_starts)
        send_outer, send_beyond = call(
            pack_kernel, "pack", [held(plain(OUTER)), held(plain(1))], [], [edge_new, middle_new]
        )
        outer = swap(send_outer, True)
        beyond = swap(send_beyond, False)
        beyond, *after = lax.optimization_barrier((beyond, *fields[1:]))
        last_new = third_call(inside_work[-1:], after, starts[1:])
        own = [edge_new, middle_new, last_new]
        (send_inner,) = call(strip_kernel, "strip", [held(plain(1))], [], [last_new])
        inner = swap(send_inner, False)


def last_call(odd, step, speed, wall, fields, places, done, shape):
    arrays = [pltpu.with_memory_space_constraint(a, pltpu.VMEM) for a in (step, speed, wall, *fields, *done)]
    return pl.pallas_call(
        functools.partial(last_kernel, places=places),
        out_shape=jax.ShapeDtypeStruct(shape, jnp.float32),
        in_specs=[IN_SMEM] + [IN_VMEM] * len(arrays),
        out_specs=pl.BlockSpec(memory_space=pltpu.HBM),
        scratch_shapes=[pltpu.VMEM((2, *shape[1:2], LANES), jnp.float32), pltpu.SemaphoreType.DMA((2 * shape[0] + 2,))],
        compiler_params=pltpu.CompilerParams(vmem_limit_bytes=VMEM_LIMIT),
        cost_estimate=pl.CostEstimate(flops=int(1.1e9), bytes_accessed=1024, transcendentals=0),
        name="last",
    )(odd, *arrays)


def pack_kernel(edge, middle, send_outer, send_beyond):
    rows = send_outer.shape[2]
    copy_layer(Layer(edge, 0), Layer(send_outer, 0, False), rows)
    for k in range(OUTER - 1):
        copy_layer(Layer(middle, k), Layer(send_outer, 1 + k, False), rows)
    copy_layer(Layer(middle, middle.shape[0] - 1), Layer(send_beyond, 0, False), rows)


def strip_kernel(last, send):
    copy_layer(Layer(last, 0), Layer(send, 0, False), send.shape[2])


def solution(mesh):
    split = P(("ens", "gx"), None, None)
    return jax.shard_map(
        shards, mesh=mesh, in_specs=(split, split, split, split, P(), split), out_specs=split, check_vma=False
    )
```

```python
import functools

import jax
import jax.numpy as jnp
from jax import lax
from jax.experimental import pallas as pl
from jax.experimental.pallas import tpu as pltpu
from jax.sharding import PartitionSpec as P

STEPS = 2
NEWTON = 4
WALL_CLASSES = 4
CFL_NUMBER = 0.45

LANES = 128
PAD = 8
ROWS = 32
HALVES = (0, 1)
OUTER = 3
INNER = 2
VMEM_LIMIT = 24 * 1024 * 1024
SEND_ROUND = 2


def cube(t):
    t = jnp.maximum(t, 0.0)
    return t * t * t


def square(t):
    t = jnp.maximum(t, 0.0)
    return t * t


def rcp(x):
    return pl.reciprocal(x, approx=True)


def plane(donor, span, soft_a, soft_b):
    low = jnp.minimum(soft_a, soft_b)
    high = jnp.maximum(soft_a, soft_b)
    pair = soft_a + soft_b
    half = 0.5 * (span + pair)
    top = jnp.maximum(span, high)
    mid = jnp.minimum(span, high)
    over = half - top
    last = half - jnp.abs(over)
    sign = jnp.where(over > 0.0, -1.0, 1.0)
    flat = low * mid
    bulk = flat * top
    share = jnp.clip(jnp.minimum(donor, 1.0 - donor), 0.0, 0.5)
    goal = bulk * share
    at = half - (0.25 * bulk - 0.5 * goal) * rcp(flat - square(over))
    low_6 = low * (1.0 / 6.0)
    mid_6 = mid * (1.0 / 6.0)
    last_6 = last * (1.0 / 6.0)
    for _ in range(NEWTON - 1):
        by_low = square(at - low)
        by_mid = square(at - mid)
        by_last = sign * square(at - last)
        growth = at * at - by_low - by_mid + by_last
        shift = goal - low_6 * by_low - mid_6 * by_mid + last_6 * by_last
        at = (5.0 / 6.0) * at + shift * rcp(growth)
    return at, low, high, pair, half, bulk


def edge_sum(at, low):
    return cube(at) - cube(at - low)


def side_sum(at, low, high, pair):
    return cube(at) - cube(at - low) - cube(at - high) + cube(at - pair)


def prepare(donor, along, soft_a, soft_b, ahead):
    span = jnp.abs(along) + 0.2
    at, low, high, pair, half, bulk = plane(donor, span, soft_a, soft_b)
    light = donor <= 0.5
    sense = jnp.where(jnp.logical_xor(light, ahead), -1.0, 1.0)
    weight = jnp.clip(0.5 + (along * sense) * rcp(half), 0.0, 1.0)
    whole = side_sum(at, low, high, pair)
    whole = whole - weight * (whole + edge_sum(at - span, low))
    scale = sense * rcp(6.0 * bulk)
    heavy = jnp.where(light, 0.0, 1.0)
    return at, span, low, high, weight, scale, whole, heavy


def finish(at, span, low, high, weight, scale, whole, heavy, moved):
    slab = jnp.abs(moved) * span
    rest = side_sum(at - slab, low, high, low + high)
    near = edge_sum(at - span + slab, low)
    return (whole - rest + weight * (rest + near)) * scale + heavy * moved


def face_flux(donor, along, soft_a, soft_b, moved):
    return finish(*prepare(donor, along, soft_a, soft_b, moved > 0.0), moved)


def lane_of(value):
    return lax.broadcasted_iota(jnp.int32, value.shape, 1)


def from_above(pair):
    turned = [pltpu.roll(v, LANES - 1, 1) for v in pair]
    return [jnp.where(lane_of(pair[0]) == LANES - 1, turned[1], turned[0]), turned[1]]


def from_below(pair):
    turned = [pltpu.roll(v, 1, 1) for v in pair]
    first = lane_of(pair[0]) == 0
    return [jnp.where(first, turned[1], turned[0]), jnp.where(first, turned[0], turned[1])]


class Layer:
    def __init__(self, ref, index, padded=True):
        self.ref, self.index, self.pad = ref, index, PAD if padded else 0

    def read(self, half, row):
        return self.ref[self.index, half, pl.ds(self.pad + row, ROWS), :]

    def write(self, half, row, value):
        self.ref[self.index, half, pl.ds(self.pad + row, ROWS), :] = value

    def wrap(self):
        rows = self.ref.shape[2] - 2 * PAD
        for h in HALVES:
            self.ref[self.index, h, pl.ds(0, PAD), :] = self.ref[self.index, h, pl.ds(rows, PAD), :]
            self.ref[self.index, h, pl.ds(PAD + rows, PAD), :] = self.ref[self.index, h, pl.ds(PAD, PAD), :]


def copy_layer(source, target, rows):
    for r in range(0, rows, ROWS):
        for h in HALVES:
            target.write(h, r, source.read(h, r))


def padded_halo(source, field, numbers):
    found = {}
    for k, p in numbers:
        found[p] = Layer(field, p)
        copy_layer(Layer(source, k, False), found[p], field.shape[2] - 2 * PAD)
        found[p].wrap()
    return found


def normals(before, here, after, wall, row):
    centre = [here.read(h, row) for h in HALVES]
    n_x = [before.read(h, row) - after.read(h, row) for h in HALVES]
    n_y = [here.read(h, row - 1) - here.read(h, row + 1) for h in HALVES]
    lane = lane_of(centre[0])
    up = [pltpu.roll(v, LANES - 1, 1) for v in centre]
    down = [pltpu.roll(v, 1, 1) for v in centre]
    top, bottom = lane == LANES - 1, lane == 0
    n_z = [down[0] - jnp.where(top, up[1], up[0]), jnp.where(bottom, down[0], down[1]) - jnp.where(top, centre[1], up[1])]
    contact = wall[pl.ds(row, ROWS), :] * (jnp.abs(n_x[0]) + jnp.abs(n_y[0]))
    n_z[0] = jnp.where(bottom, contact, n_z[0])
    return centre, n_x, n_y, n_z


def soft(normal):
    return jnp.abs(normal) + 0.2


def own_index(odd, layer, count):
    return jnp.where(odd, OUTER + count - 1 - layer, layer - OUTER)


def natural(ref, index, half, row):
    return ref[index, pl.ds(row, ROWS), half * LANES : (half + 1) * LANES]


def begin_kernel(odd_ref, fraction_in, mask_in, class_in, *refs):
    speeds_in, (*speeds, peak, state, classes, fraction, mask, sems) = refs[:3], refs[3:]
    odd = odd_ref[0] == 1
    count, rows, width = fraction.shape
    sources = (*speeds_in, fraction_in, mask_in, class_in)
    copies = [
        pltpu.make_async_copy(source, target, sems.at[n])
        for n, (source, target) in enumerate(zip(sources, (*speeds, fraction, mask, classes)))
    ]
    for copy in copies:
        copy.start()
    best = jnp.zeros((8, width), jnp.float32)
    for n, ref in enumerate(speeds):
        copies[n].wait()
        for i in range(count):
            best = jnp.maximum(best, jnp.max(jnp.abs(ref[i]).reshape(rows // 8, 8, width), axis=0))
    peak[...] = jnp.maximum(best[:, :LANES], best[:, LANES:])
    copies[3].wait()
    copies[4].wait()
    for k in range(count):
        index = own_index(odd, OUTER + k, count)
        for r in range(0, rows, ROWS):
            for h in HALVES:
                value = jnp.where(natural(mask, index, h, r) == 1, 1.0, natural(fraction, index, h, r))
                Layer(state, k).write(h, r, value)
        Layer(state, k).wrap()
    copies[5].wait()


def first_send_kernel(odd_ref, first, state, send_outer, send_inner):
    odd = odd_ref[0] == 1
    count, rows, _ = first.shape
    for k in range(OUTER):
        copy_layer(Layer(state, k), Layer(send_outer, k, False), rows)
    for k in range(INNER):
        copy_layer(Layer(state, count - 1 - k), Layer(send_inner, k, False), rows)
    near = jnp.where(odd, count - 2, 0)
    for r in range(0, rows, ROWS):
        for h in HALVES:
            Layer(send_outer, OUTER, False).write(h, r, natural(first, near, h, r))
            Layer(send_outer, OUTER + 1, False).write(h, r, natural(first, count - 1, h, r))
            Layer(send_inner, INNER, False).write(h, r, natural(first, count - 1, h, r))


def wall_kernel(classes, out, turned):
    device = lax.axis_index("gx")
    odd = lax.rem(device, 2) == 1
    total = classes.shape[0]
    layers = out.shape[0]
    count = layers - OUTER - INNER
    turned[...] = jnp.zeros(turned.shape, jnp.float32)
    for p in range(1, layers - 1):
        row = lax.rem(device * count + own_index(odd, p, count) + total, total)
        turned[pl.ds(p, 1), :] = classes[pl.ds(row, 1), :].astype(jnp.float32)
    used = -(-layers // 8) * 8
    turned[:used, :] = jnp.cos(jnp.pi * (turned[:used, :] + 1.0) / (WALL_CLASSES + 1))
    columns = jnp.transpose(turned[...])
    for p in range(1, layers - 1):
        out[p] = pltpu.roll(columns, LANES - p, 1)


KEPT = 9


def face_work(layers, wall, slopes, faces, rows, work):
    n_s, n_a, n_b = slopes

    def slope(i):
        for r in range(0, rows, ROWS):
            _, n_x, n_y, n_z = normals(layers[i - 1], layers[i], layers[i + 1], wall.at[i], r)
            for h in HALVES:
                Layer(n_s, i, False).write(h, r, n_x[h])
                Layer(n_a, i, False).write(h, r, soft(n_y[h]))
                Layer(n_b, i, False).write(h, r, soft(n_z[h]))

    slope(faces[0])
    for i in faces:
        slope(i + 1)
        sides = [(layers[i], layers[i + 1])] + [(Layer(n, i, False), Layer(n, i + 1, False)) for n in slopes]
        for r in range(0, rows, ROWS):
            for h in HALVES:

                def donor(ahead):
                    return [jnp.where(ahead, low.read(h, r), high.read(h, r)) for low, high in sides]

                work(i, h, r, donor)


def prepare_kernel(odd_ref, *refs, kinds, faces, count):
    given = dict(zip(kinds, refs))
    out, field, *slopes = refs[len(kinds) :]
    rows = out.shape[2]
    odd = odd_ref[0] == 1
    sign = jnp.where(odd, -1.0, 1.0)
    layers = {OUTER + k: Layer(given["own"], k) for k in range(count)}
    needed = range(faces[0] - 1, faces[-1] + 3)
    for kind, first_layer, way, number in (("outer", OUTER - 1, -1, OUTER), ("inner", OUTER + count, 1, INNER)):
        if kind in given:
            numbers = [(k, first_layer + way * k) for k in range(number) if first_layer + way * k in needed]
            layers.update(padded_halo(given[kind], field, numbers))

    def work(face, h, r, donor):
        if face == OUTER - 2:
            speed = Layer(given["outer"], OUTER, False).read(h, r)
        elif face == OUTER - 1:
            speed = natural(given["first"], count - 1, h, r)
            speed = jnp.where(odd, speed, Layer(given["outer"], OUTER + 1, False).read(h, r))
        elif face == OUTER + count - 1:
            speed = natural(given["first"], count - 1, h, r)
            speed = jnp.where(odd, Layer(given["inner"], INNER, False).read(h, r), speed)
        else:
            speed = natural(given["first"], jnp.where(odd, OUTER + count - 2 - face, face - OUTER), h, r)
        speed = speed * sign
        ahead = speed > 0.0
        first_kept = (face - faces[0]) * KEPT
        for n, value in enumerate((*prepare(*donor(ahead), ahead), speed)):
            Layer(out, first_kept + n, False).write(h, r, value)

    face_work(layers, given["wall"], slopes, faces, rows, work)


def finish_faces(kept, step, flux, moved, start):
    rows = kept.shape[2]

    @pl.loop(0, kept.shape[0] // KEPT)
    def _(k):
        for r in range(0, rows, ROWS):
            for h in HALVES:
                values = [Layer(kept, k * KEPT + n, False).read(h, r) for n in range(KEPT)]
                values[-1] = values[-1] * step
                Layer(moved, start + k, False).write(h, r, values[-1])
                Layer(flux, start + k, False).write(h, r, finish(*values))


def update(target, here, inward, outward, rows):
    for r in range(0, rows, ROWS):
        for h in HALVES:
            target.write(h, r, jnp.clip(here.read(h, r) - outward.read(h, r) + inward.read(h, r), 0.0, 1.0))


def finish_kernel(peak, *refs, parts):
    kept, (state, outer, out, above, moved, step_out, send, flux) = refs[:parts], refs[parts:]
    rows = moved.shape[2]
    largest = jnp.max(peak[...])
    step = CFL_NUMBER / (jnp.full((8, LANES), largest, jnp.float32) + 1e-6)
    step_out[...] = step
    start = 0
    for ref in kept:
        finish_faces(ref, step[:1, :], flux, moved, start)
        start += ref.shape[0] // KEPT

    @pl.loop(0, state.shape[0])
    def _(k):
        update(Layer(out, k), Layer(state, k), Layer(flux, k + 1, False), Layer(flux, k + 2, False), rows)
        Layer(out, k).wrap()

    update(Layer(above, 0, False), Layer(outer, 0, False), Layer(flux, 0, False), Layer(flux, 1, False), rows)
    copy_layer(Layer(out, out.shape[0] - 1), Layer(send, 0, False), rows)


def first_fluxes(layers, wall, moved, slopes, flux, faces):
    def work(i, h, r, donor):
        speed = Layer(moved, i - 1, False).read(h, r)
        Layer(flux, i - 1, False).write(h, r, face_flux(*donor(speed > 0.0), speed))

    face_work(layers, wall, slopes, faces, flux.shape[2], work)


def own_layers(*refs):
    found = [Layer(ref, k) for ref in refs for k in range(ref.shape[0])]
    return {OUTER + k: layer for k, layer in enumerate(found)}


def middle_kernel(edge, middle, last, moved, wall, flux_out, *slopes):
    rows = moved.shape[2]

    def work(i, h, r, donor):
        speed = Layer(moved, i - 1, False).read(h, r)
        Layer(flux_out, 0, False).write(h, r, face_flux(*donor(speed > 0.0), speed))

    face_work(own_layers(edge, middle, last), wall, slopes, (OUTER + 1,), rows, work)


def inside_kernel(edge, middle, last, inner, beyond, moved, wall, flux_low, out, send, field, *more):
    *slopes, flux = more
    rows = moved.shape[2]
    layers = own_layers(edge, middle, last)
    count = len(layers)
    layers.update(padded_halo(inner, field, [(0, OUTER + count)]))
    layers[OUTER + count + 1] = Layer(beyond, 0, False)
    first_fluxes(layers, wall, moved, slopes, flux, range(OUTER + 2, OUTER + count))
    fluxes = [Layer(flux_low, 0, False)] + [Layer(flux, i - 1, False) for i in range(OUTER + 2, OUTER + count)]
    for k, i in enumerate(range(OUTER + 2, OUTER + count)):
        target = Layer(out, k)
        update(target, layers[i], fluxes[k], fluxes[k + 1], rows)
        target.wrap()
    copy_layer(Layer(out, count - 3), Layer(send, 0, False), rows)


def outside_kernel(edge, middle, last, outer, moved, wall, flux_above, above, out, field, *more):
    *slopes, flux = more
    rows = moved.shape[2]
    layers = own_layers(edge, middle, last)
    layers.update(padded_halo(outer, field, [(k, OUTER - 1 - k) for k in range(OUTER)]))
    first_fluxes(layers, wall, moved, slopes, flux, range(OUTER - 2, OUTER + 1))
    fluxes = [Layer(flux, k, False) for k in range(OUTER)] + [Layer(flux_above, 0, False)]
    for k, target in enumerate((Layer(above, 0, False), Layer(out, 0), Layer(out, 1))):
        update(target, layers[OUTER - 1 + k], fluxes[k], fluxes[k + 1], rows)
        if k > 0:
            target.wrap()


def second_sweep(before, here, after, wall, speed, out, scratch):
    n_s, n_a, n_b, flux = scratch
    rows = out.ref.shape[2] - 2 * PAD
    for r in range(0, rows, ROWS):
        _, n_x, n_y, n_z = normals(before, here, after, wall, r)
        for h in HALVES:
            n_s.write(h, r, n_y[h])
            n_a.write(h, r, soft(n_x[h]))
            n_b.write(h, r, soft(n_z[h]))
    for s in (n_s, n_a, n_b):
        s.wrap()
    for r in range(0, rows, ROWS):
        for h in HALVES:
            moved = speed(h, r)
            ahead = moved > 0.0
            donor = [jnp.where(ahead, s.read(h, r), s.read(h, r + 1)) for s in (here, n_s, n_a, n_b)]
            flux.write(h, r, face_flux(*donor, moved))
    flux.wrap()
    for r in range(0, rows, ROWS):
        for h in HALVES:
            out.write(h, r, jnp.clip(here.read(h, r) - flux.read(h, r) + flux.read(h, r - 1), 0.0, 1.0))
    out.wrap()


def third_sweep(before, here, after, wall, speed, write, rows):
    for r in range(0, rows, ROWS):
        centre, n_x, n_y, n_z = normals(before, here, after, wall, r)
        fields = [centre, n_z, [soft(v) for v in n_x], [soft(v) for v in n_y]]
        above = [from_above(f) for f in fields]
        lane = lane_of(centre[0])
        through = []
        for h in HALVES:
            moved = speed(h, r)
            ahead = moved > 0.0
            through.append(face_flux(*[jnp.where(ahead, f[h], a[h]) for f, a in zip(fields, above)], moved))
        through[1] = jnp.where(lane == LANES - 1, 0.0, through[1])
        below = from_below(through)
        for h in HALVES:
            value = jnp.clip(centre[h] - through[h] + below[h], 0.0, 1.0)
            write(h, r, value)


def gather_layers(refs, places):
    found = {}
    for ref, (start, padded) in zip(refs, places):
        for k in range(ref.shape[0]):
            found[start + k] = Layer(ref, k, padded)
    return found


def second_kernel(odd_ref, step, speed_ref, wall, *refs, places, work, send_last):
    fields, rest = refs[: len(places)], refs[len(places) :]
    out, rest = rest[0], rest[1:]
    send, rest = (rest[0], rest[1:]) if send_last is not None else (None, rest)
    scratch = [Layer(ref, 0) for ref in rest]
    layers = gather_layers(fields, places)
    odd = odd_ref[0] == 1
    count, rows, _ = speed_ref.shape
    for k, p in enumerate(work):
        index = own_index(odd, p, count)
        second_sweep(
            layers[p - 1],
            layers[p],
            layers[p + 1],
            wall.at[p],
            lambda h, r: natural(speed_ref, index, h, r) * step[:1, :],
            Layer(out, k),
            scratch,
        )
    if send is not None:
        copy_layer(Layer(out, work.index(send_last)), Layer(send, 0, False), rows)


def third_kernel(odd_ref, step, speed_ref, wall, *refs, places, work):
    fields, (out,) = refs[: len(places)], refs[len(places) :]
    layers = gather_layers(fields, places)
    odd = odd_ref[0] == 1
    count, rows, _ = speed_ref.shape
    for k, p in enumerate(work):
        index = own_index(odd, p, count)
        third_sweep(
            layers[p - 1],
            layers[p],
            layers[p + 1],
            wall.at[p],
            lambda h, r: natural(speed_ref, index, h, r) * step[:1, :],
            Layer(out, k).write,
            rows,
        )
        Layer(out, k).wrap()


def last_kernel(odd_ref, step, speed_ref, wall, *refs, places):
    fields, rest = refs[: len(places)], refs[len(places) :]
    done, (out, held_out, sems) = rest[:-3], rest[-3:]
    layers = gather_layers(fields, places)
    odd = odd_ref[0] == 1
    count, rows, _ = speed_ref.shape
    copies = []

    def send(source, layer, h, first_row=0):
        rows_here = pl.ds(first_row, source.shape[0])
        target = out.at[own_index(odd, layer, count), rows_here, h * LANES : (h + 1) * LANES]
        copies.append(pltpu.make_async_copy(source, target, sems.at[len(copies)]))
        copies[-1].start()

    p = OUTER + 1
    for ref in done:
        for k in range(ref.shape[0]):
            for h in HALVES:
                send(ref.at[k, h, pl.ds(PAD, rows), :], p, h)
            p += 1

    piece = rows // 2

    def write(h, r, value):
        held_out[h, pl.ds(r, ROWS), :] = value
        if (r + ROWS) % piece == 0:
            start = r + ROWS - piece
            send(held_out.at[h, pl.ds(start, piece), :], OUTER, h, start)

    index = own_index(odd, OUTER, count)
    third_sweep(
        layers[OUTER - 1],
        layers[OUTER],
        layers[OUTER + 1],
        wall.at[OUTER],
        lambda h, r: natural(speed_ref, index, h, r) * step[:1, :],
        write,
        rows,
    )
    for copy in copies:
        copy.wait()


IN_VMEM = pl.BlockSpec(memory_space=pltpu.VMEM)
IN_SMEM = pl.BlockSpec(memory_space=pltpu.SMEM)


def held(shape):
    return pltpu.VMEM(shape, jnp.float32)


def call(kernel, name, outs, scalars, arrays, scratch=(), faces=0.1, resident=True):
    space = pltpu.VMEM if resident else pltpu.HBM
    arrays = [pltpu.with_memory_space_constraint(a, space) for a in arrays]
    work = int(faces * 1.1e9)
    return pl.pallas_call(
        kernel,
        out_shape=outs,
        in_specs=[IN_SMEM] * len(scalars) + [pl.BlockSpec(memory_space=space)] * len(arrays),
        out_specs=[IN_VMEM] * len(outs),
        scratch_shapes=list(scratch),
        compiler_params=pltpu.CompilerParams(vmem_limit_bytes=VMEM_LIMIT),
        cost_estimate=pl.CostEstimate(flops=work, bytes_accessed=1024, transcendentals=0),
        name=name,
    )(*scalars, *arrays)


def swap(array, outer):
    count = lax.axis_size("gx")
    if outer:
        pairs = [(i, (i + 1) % count if i % 2 else (i - 1) % count) for i in range(count)]
    else:
        pairs = [(i, i ^ 1) for i in range(count)]
    return lax.ppermute(array, "gx", pairs)


def largest_round(array, reach, beside):
    count = lax.axis_size("gx")
    if count & (count - 1) == 0:
        pairs = [(i, i ^ reach) for i in range(count)]
    else:
        pairs = [(i, (i + reach) % count) for i in range(count)]
    received = lax.ppermute(array, "gx", pairs)
    if beside:
        received, *_ = lax.optimization_barrier((received, *beside))
    return jnp.maximum(array, received)


def shards(fraction, first, second, third, wall_class, seed_mask):
    count, rows, width = fraction.shape
    layers = OUTER + count + INNER
    own_end = OUTER + count
    device = lax.axis_index("gx")
    odd = (device % 2).astype(jnp.int32).reshape(1)

    def padded(n):
        return (n, 2, rows + 2 * PAD, LANES)

    def plain(n):
        return (n, 2, rows, LANES)

    natural_shape = (count, rows, width)
    first, second, third, peak, state, classes = call(
        begin_kernel,
        "begin",
        [held(natural_shape)] * 3
        + [held((8, LANES)), held(padded(count)), pltpu.VMEM(wall_class.shape, jnp.int32)],
        [odd],
        [fraction, seed_mask, wall_class, first, second, third],
        [
            pltpu.VMEM(natural_shape, jnp.float32),
            pltpu.VMEM(natural_shape, jnp.int32),
            pltpu.SemaphoreType.DMA((6,)),
        ],
        resident=False,
    )
    send_outer, send_inner = call(
        first_send_kernel, "first_send", [held(plain(OUTER + 2)), held(plain(INNER + 1))], [odd], [first, state]
    )
    inner = swap(send_inner, False)
    (wall,) = call(
        wall_kernel, "wall", [held((layers, rows, LANES))], [], [classes], [pltpu.VMEM((LANES, rows), jnp.float32)]
    )
    slopes = [pltpu.VMEM(padded(layers), jnp.float32)] + [pltpu.VMEM(plain(layers), jnp.float32)] * 3

    def prepare_call(faces, **given):
        return call(
            functools.partial(prepare_kernel, kinds=tuple(given), faces=faces, count=count),
            "prepare",
            [held(plain(KEPT * len(faces)))],
            [odd],
            list(given.values()),
            slopes,
            faces=0.02,
        )[0]

    prepare_inside = functools.partial(prepare_call, wall=wall, first=first, own=state, inner=inner)
    outer = swap(send_outer, True)
    size = lax.axis_size("gx")
    reaches = [1 << k for k in range(1, size.bit_length()) if 1 << k < size]
    peak = largest_round(peak, 1, [])
    kept = [prepare_inside(tuple(range(OUTER + 2, own_end)))]
    kept.insert(0, prepare_inside((OUTER + 1,)))
    kept.insert(0, prepare_call((OUTER - 2, OUTER - 1, OUTER), wall=wall, first=first, own=state, outer=outer))
    beside = [[kept[2]], [kept[1]], [kept[0]]]
    for n, reach in enumerate(reaches[::-1]):
        left = len(reaches) - n
        peak = largest_round(peak, reach, beside[-left] if left <= len(beside) else [])
    own, above, moved, step, send_inner = call(
        functools.partial(finish_kernel, parts=len(kept)),
        "finish",
        [held(padded(count)), held(plain(1)), held(plain(count + 2)), held((8, LANES)), held(plain(1))],
        [],
        [peak, *kept, state, outer],
        [pltpu.VMEM(plain(count + 2), jnp.float32)],
        faces=1,
    )
    swept, places = [above, own], [(OUTER - 1, False), (OUTER, True)]
    line = [pltpu.VMEM(padded(1), jnp.float32)] * 4
    def second_call(work, fields, places, send):
        return call(
            functools.partial(second_kernel, places=places, work=work, send_last=work[0] if send else None),
            "second",
            [held(padded(len(work)))] + ([held(plain(1))] if send else []),
            [odd],
            [step, second, wall, *fields],
            line,
            faces=0.1 if own_end - 1 in work else len(work),
        )

    def last_second(part, place, send_inner):
        inner = swap(send_inner, False)
        last, send_inner = second_call((own_end - 1,), [part, inner], [place, (own_end, False)], True)
        return last, swap(send_inner, False)

    for turn in range(STEPS):
        final = turn == STEPS - 1
        if turn > 0:
            flux = pltpu.VMEM(plain(count + 2), jnp.float32)
            (flux_low,) = call(middle_kernel, "middle", [held(plain(1))], [], [*own, moved, wall], slopes[1:])
            inside, send_inner = call(
                inside_kernel,
                "inside",
                [held(padded(count - 2)), held(plain(1))],
                [],
                [*own, inner, beyond, moved, wall, flux_low],
                [*slopes, flux],
                faces=0.1,
            )
            inner = swap(send_inner, False)
            last, send_inner = second_call((own_end - 1,), [inside, inner], [(OUTER + 2, True), (own_end, False)], True)
            outer, last = lax.optimization_barrier((outer, last))
            above, outside = call(
                outside_kernel,
                "outside",
                [held(plain(1)), held(padded(2))],
                [],
                [*own, outer, moved, wall, flux_low],
                [*slopes, flux],
                faces=3,
            )
            swept = [above, outside, inside]
            places = [(OUTER - 1, False), (OUTER, True), (OUTER + 2, True)]
        edge, send_outer = second_call((OUTER,), swept[:2], places[:2], True)
        send_outer, send_inner = lax.optimization_barrier((send_outer, send_inner))
        if turn == 0:
            last, inner = last_second(swept[-1], places[-1], send_inner)
        else:
            inner = swap(send_inner, False)
        after = lax.optimization_barrier((edge, *swept[1:]))[1:]
        (middle,) = second_call(tuple(range(OUTER + 1, own_end - 1)), after, places[1:], False)
        outer = swap(send_outer, True)

        fields = [edge, middle, last, inner]
        starts = [(OUTER, True), (OUTER + 1, True), (own_end - 1, True), (own_end, False)]
        inside_work = tuple(range(OUTER + 1, own_end))
        edge_fields, edge_starts = [outer, edge, middle], [(OUTER - 1, False), (OUTER, True), (OUTER + 1, True)]
        def third_call(work, fields, places):
            return call(
                functools.partial(third_kernel, places=places, work=work),
                "third",
                [held(padded(len(work)))],
                [odd],
                [step, third, wall, *fields],
                faces=len(work),
            )[0]

        middle_new = third_call(inside_work[:-1], fields[:-1], starts[:-1])
        if final:
            last_new = third_call(inside_work[-1:], fields[1:], starts[1:])
            return last_call(odd, step, third, wall, edge_fields, edge_starts, [middle_new, last_new], natural_shape)
        edge_new = third_call((OUTER,), edge_fields, edge_starts)
        send_outer, send_beyond = call(
            pack_kernel, "pack", [held(plain(OUTER)), held(plain(1))], [], [edge_new, middle_new]
        )
        outer = swap(send_outer, True)
        beyond = swap(send_beyond, False)
        beyond, *after = lax.optimization_barrier((beyond, *fields[1:]))
        last_new = third_call(inside_work[-1:], after, starts[1:])
        own = [edge_new, middle_new, last_new]
        (send_inner,) = call(strip_kernel, "strip", [held(plain(1))], [], [last_new])
        inner = swap(send_inner, False)


def last_call(odd, step, speed, wall, fields, places, done, shape):
    arrays = [pltpu.with_memory_space_constraint(a, pltpu.VMEM) for a in (step, speed, wall, *fields, *done)]
    return pl.pallas_call(
        functools.partial(last_kernel, places=places),
        out_shape=jax.ShapeDtypeStruct(shape, jnp.float32),
        in_specs=[IN_SMEM] + [IN_VMEM] * len(arrays),
        out_specs=pl.BlockSpec(memory_space=pltpu.HBM),
        scratch_shapes=[pltpu.VMEM((2, *shape[1:2], LANES), jnp.float32), pltpu.SemaphoreType.DMA((2 * shape[0] + 2,))],
        compiler_params=pltpu.CompilerParams(vmem_limit_bytes=VMEM_LIMIT),
        cost_estimate=pl.CostEstimate(flops=int(1.1e9), bytes_accessed=1024, transcendentals=0),
        name="last",
    )(odd, *arrays)


def pack_kernel(edge, middle, send_outer, send_beyond):
    rows = send_outer.shape[2]
    copy_layer(Layer(edge, 0), Layer(send_outer, 0, False), rows)
    for k in range(OUTER - 1):
        copy_layer(Layer(middle, k), Layer(send_outer, 1 + k, False), rows)
    copy_layer(Layer(middle, middle.shape[0] - 1), Layer(send_beyond, 0, False), rows)


def strip_kernel(last, send):
    copy_layer(Layer(last, 0), Layer(send, 0, False), send.shape[2])


def solution(mesh):
    split = P(("ens", "gx"), None, None)
    return jax.shard_map(
        shards, mesh=mesh, in_specs=(split, split, split, split, P(), split), out_specs=split, check_vma=False
    )
```
